32 devices in a mesh: rows: 4 (over y, x), cols: 8 (over z, core).
Axes of the slice: x: 2, y: 2, z: 4, core: 2. Of those that a mesh axis runs over, the one named last changes fastest.
Arguments:
- tokens: bfloat16 [8, 1536, 1536], P('cols', 'rows'), may hold values from -6 to 6
- segment_ids: int32 [8, 1536], P('cols'), may hold values from 0 to 3, never falling along the last dimension, each value on 1 to 768 neighbouring positions
- expert_ids: int32 [8, 1536, 8], P('cols', 'rows'), may hold values from 0 to 31, all different within a row; in each aligned block of 384 rows (0 to 383, 384 to 767, ..., all dimensions but the last counted through in order) at most 120 rows name the same one
- w_query: bfloat16 [1536, 1536], P('cols', 'rows'), may hold values from -0.625 to 0.625
- key_matrix: bfloat16 [1536, 512], P('cols', 'rows'), may hold values from -0.625 to 0.625
- value_matrix: bfloat16 [1536, 512], P('cols', 'rows'), may hold values from -0.15625 to 0.15625
- w_out: bfloat16 [1536, 1536], P(('rows', 'cols')), may hold values from -1.75 to 1.75
- norm_attn: bfloat16 [1536], P(('rows', 'cols')), may hold values from 0.5 to 1.5
- norm_moe: bfloat16 [1536], P(('rows', 'cols')), may hold values from 0.5 to 1.5
- w_router: bfloat16 [1536, 32], P(('rows', 'cols')), may hold values from -0.078125 to 0.078125
- w_gate: bfloat16 [32, 1536, 512], P('cols', 'rows'), may hold values from -0.15625 to 0.15625
- w_up: bfloat16 [32, 1536, 512], P('cols', 'rows'), may hold values from -0.15625 to 0.15625
- w_down: bfloat16 [32, 512, 1536], P('cols', None, 'rows'), may hold values from -2 to 2
- cotangent: bfloat16 [8, 1536, 1536], P('cols', 'rows'), may hold values from -6 to 6
Outputs:
- block_out: float32 [8, 1536, 1536], P('cols', 'rows')
- grad_tokens: float32 [8, 1536, 1536], P('cols', 'rows')
- grad_w_query: float32 [1536, 1536], P('cols', 'rows')
- grad_w_key: float32 [1536, 512], P('cols', 'rows')
- grad_w_value: float32 [1536, 512], P('cols', 'rows')
- grad_w_out: float32 [1536, 1536], P(('rows', 'cols'))
- grad_norm_attn: float32 [1536], P(('rows', 'cols'))
- grad_norm_moe: float32 [1536], P(('rows', 'cols'))
- grad_w_router: float32 [1536, 32], P(('rows', 'cols'))
- grad_w_gate: float32 [32, 1536, 512], P('cols', 'rows')
- grad_w_up: float32 [32, 1536, 512], P('cols', 'rows')
- grad_w_down: float32 [32, 512, 1536], P('cols', None, 'rows')
The draws below stay inside these ranges and needn't reach their ends.
Inputs may be any that keep to these rules, and one draw needn't show every extreme that they name: `segment_ids`: within a sequence the numbers never fall; each document has at most 768 tokens. `expert_ids`: each token names 8 different experts; among the rows of one device (aligned blocks of 384 tokens) no expert is named more than 120 times, a bound that some block reaches.
All inputs are finite; a program needn't handle non-finite values.
Results may differ from the reference program's by a relative error of at most 0.02.
Values may be sent and summed in bfloat16 or wider, within the bound.
No kernel may reach another device: no remote copies, remote signals or barrier semaphores. Data moves between devices by JAX's collectives and lax.ppermute only.
A program may use at most 320 MiB of HBM per device.

```python
import math
import jax
import jax.numpy as jnp
import numpy as np
from jax import lax

MODEL_DIM = 1536
NQ = 24
KEY_VALUE_HEADS = 8
HEAD_SIZE = 64
FFE = 512
TOPK = 8
EXPERTS = 32
DOCS = 4
TOK_DEV = 384
LEN = 1536
SEQS = 8
CAP = 120


def shard_levels(rng, dims, pieces, least, largest):
    def one(axis_at, parts):
        heights = jax.random.uniform(jax.random.fold_in(jax.random.fold_in(rng, 6), axis_at), (parts,), jnp.float32, least / len(pieces), largest / len(pieces))
        return jnp.repeat(jnp.exp(heights), dims[axis_at] // parts).reshape((-1,) + (1,) * (len(dims) - axis_at - 1))

    level = one(*pieces[0])
    for cut in pieces[1:]:
        level = level * one(*cut)
    return level


def profile(number_of, total, bound, slope):
    weights = [(1 << 20) // math.isqrt(standing ** slope) + 1 for standing in range(2, number_of + 1)]
    spare, holding = total - bound - (number_of - 1), [1] * (number_of - 1)
    while spare > 0:
        movable = [i for i in range(number_of - 1) if holding[i] < bound]
        whole, left = sum([weights[i] for i in movable]), spare
        for i in movable:
            extra = min(bound - holding[i], max(1, left * weights[i] // whole), spare)
            holding[i] = holding[i] + extra
            spare = spare - extra
    return np.array([bound] + holding)


def ragged(own_key, number_of, total, bound, lean):
    if number_of == 2:
        one = jax.random.randint(own_key, (), max(1, total - bound), min(bound, total - 1) + 1)
        return jnp.stack([one, total - one])
    tallies = jnp.asarray(profile(number_of, total, bound, lean), jnp.int32)
    twos = (number_of - 1) // 2
    giver, taker = tallies[1:1 + 2 * twos:2], tallies[2:2 + 2 * twos:2]
    room = jnp.minimum(giver - 1, bound - taker)
    passed = jax.random.randint(jax.random.fold_in(own_key, 1), (twos,), 0, 1 << 20) % (room + 1)
    tallies = tallies.at[1:1 + 2 * twos:2].set(giver - passed).at[2:2 + 2 * twos:2].set(taker + passed)
    return tallies[jax.random.permutation(jax.random.fold_in(own_key, 2), number_of)]


def shared_out(rng, own, number, rows, number_of, top, reach, skew):
    sequence = jax.random.permutation(rng, number_of)
    crowded, usual = load_shares(number_of, rows * top, reach, skew, True), load_shares(number_of, rows * top, reach, skew, False)
    places = jnp.arange(number_of)

    def named(tallies, turn):
        used = int((tallies > 0).sum())
        fixed = max(1, used // 4)
        shifted = fixed + (places - fixed + turn * (used - fixed)) % max(1, number_of - fixed)
        return jnp.zeros((number_of,), jnp.int32).at[sequence[jnp.where(places < fixed, places, shifted)]].set(jnp.asarray(tallies, jnp.int32))

    tallies = jnp.where(number % 4 == 0, named(crowded, number // 4), named(usual, number - number // 4 - 1))
    mixed = jax.random.permutation(jax.random.fold_in(own, 3), number_of)
    donor, sink = mixed[0:number_of // 2 * 2:2], mixed[1:number_of // 2 * 2:2]
    slack = jnp.minimum(tallies[donor] - 1, reach - tallies[sink]) // 2
    slack = jnp.where((donor == sequence[0]) | (sink == sequence[0]) | (tallies[sink] == 0), 0, jnp.maximum(slack, 0))
    shifted = jax.random.randint(jax.random.fold_in(own, 4), (number_of // 2,), 0, 1 << 20) % (slack + 1)
    tallies = tallies.at[donor].add(-shifted).at[sink].add(shifted)
    labels = jnp.searchsorted(jnp.cumsum(tallies), jnp.arange(rows * top), side="right").astype(jnp.int32)
    table = labels.reshape(top, rows).T
    table = table[jax.random.permutation(jax.random.fold_in(own, 1), rows)]
    turn = jax.random.randint(jax.random.fold_in(own, 2), (rows, 1), 0, top)
    return jnp.take_along_axis(table, (jnp.arange(top)[None, :] + turn) % top, axis=1)


def load_shares(number_of, total, limit, slope, full):
    weights = [(1 << 20) // math.isqrt(standing ** slope) + 1 for standing in range(1, number_of + 1)]
    largest = limit if full else min(limit, max(-(-total // number_of), total * weights[0] // sum(weights)))
    least = 1 if total - largest >= number_of - 1 else 0
    given, spare = [largest] + [least] * (number_of - 1), total - largest - least * (number_of - 1)
    while spare > 0:
        movable = [i for i in range(1, number_of) if given[i] < largest] or [i for i in range(1, number_of) if given[i] < limit]
        whole, remaining = sum([weights[i] for i in movable]), spare
        for i in movable:
            addition = min(limit - given[i], max(1, remaining * weights[i] // whole), spare)
            given[i] = given[i] + addition
            spare = spare - addition
    return np.array(given)


def gaussian(stream_key, extent, width, most, pieces=(), kind=jnp.bfloat16):
    entries = jax.random.normal(stream_key, extent, jnp.float32) * width
    if len(pieces) > 0:
        entries = shard_levels(stream_key, extent, pieces, -0.22, 0.18) * entries
    return jnp.clip(entries, min=-most, max=most).astype(kind)


def setup_inputs(seed: int = 0) -> dict:
    arg_keys = jax.random.split(jax.random.key(seed), 15)
    tokens = gaussian(arg_keys[0], (SEQS, LEN, MODEL_DIM), 1.0, 6.0, ((0, 8), (1, 4)))
    segment_ids = jax.vmap(lambda own: jnp.searchsorted(jnp.cumsum(ragged(own, DOCS, LEN, LEN // 2, 1)), jnp.arange(LEN), side="right"))(jax.random.split(arg_keys[1], SEQS)).reshape((SEQS, LEN)).astype(jnp.int32)
    expert_ids_keys = jax.random.split(jax.random.fold_in(arg_keys[2], 1), SEQS * LEN // TOK_DEV)
    expert_ids_turns = jax.random.permutation(jax.random.fold_in(arg_keys[2], 3), SEQS * LEN // TOK_DEV)
    expert_ids = jax.vmap(lambda own, number: shared_out(jax.random.fold_in(arg_keys[2], 2), own, number, TOK_DEV, EXPERTS, TOPK, CAP, 1))(expert_ids_keys, expert_ids_turns).reshape((SEQS, LEN, TOPK))
    w_query = gaussian(arg_keys[3], (MODEL_DIM, NQ * HEAD_SIZE), (MODEL_DIM // 16) ** -0.5, 0.625, ((0, 8), (1, 4)))
    key_matrix = gaussian(arg_keys[4], (MODEL_DIM, KEY_VALUE_HEADS * HEAD_SIZE), (MODEL_DIM // 16) ** -0.5, 0.625, ((0, 8), (1, 4)))
    value_matrix = gaussian(arg_keys[5], (MODEL_DIM, KEY_VALUE_HEADS * HEAD_SIZE), MODEL_DIM ** -0.5, 0.15625, ((0, 8), (1, 4)))
    w_out = gaussian(arg_keys[6], (NQ * HEAD_SIZE, MODEL_DIM), (NQ * HEAD_SIZE // 128) ** -0.5, 1.75, ((0, 32),))
    norm_attn = jnp.clip(1.0 + 0.1 * jax.random.normal(arg_keys[7], (MODEL_DIM,), jnp.float32), 0.5, 1.5).astype(jnp.bfloat16)
    norm_moe = jnp.clip(1.0 + 0.1 * jax.random.normal(arg_keys[8], (MODEL_DIM,), jnp.float32), 0.5, 1.5).astype(jnp.bfloat16)
    w_router = gaussian(arg_keys[9], (MODEL_DIM, EXPERTS), (4 * MODEL_DIM) ** -0.5, 0.078125, ((0, 32),))
    w_gate = gaussian(arg_keys[10], (EXPERTS, MODEL_DIM, FFE), MODEL_DIM ** -0.5, 0.15625, ((0, 8), (1, 4)))
    w_up = gaussian(arg_keys[11], (EXPERTS, MODEL_DIM, FFE), MODEL_DIM ** -0.5, 0.15625, ((0, 8), (1, 4)))
    w_down = gaussian(arg_keys[12], (EXPERTS, FFE, MODEL_DIM), (max(FFE // 64, 1)) ** -0.5, 2.0, ((0, 8), (2, 4)))
    cotangent = gaussian(arg_keys[13], (SEQS, LEN, MODEL_DIM), 1.0, 6.0, ((0, 8), (1, 4)))
    return dict(tokens=tokens, segment_ids=segment_ids, expert_ids=expert_ids, w_query=w_query, key_matrix=key_matrix, value_matrix=value_matrix, w_out=w_out, norm_attn=norm_attn, norm_moe=norm_moe, w_router=w_router, w_gate=w_gate, w_up=w_up, w_down=w_down, cotangent=cotangent)


res_scale = 0.22
att_scale = 0.015625
norm_eps = 1e-06
rope_base = 10000.0
masked_score = -1e+30
highest = lax.Precision.HIGHEST

@jax.custom_vjp
def low(v):
    return lax.optimization_barrier(v.astype(jnp.bfloat16)).astype(jnp.float32)

@jax.custom_vjp
def low_back(v):
    return v

def low_keep(v):
    return (low(v), None)

def low_pass(kept, grad):
    return (grad,)

def back_keep(v):
    return (v, None)

def back_low(kept, grad):
    return (low(grad),)
low.defvjp(low_keep, low_pass)
low_back.defvjp(back_keep, back_low)

def rms_scale(hidden_rows):
    return lax.rsqrt(lax.optimization_barrier(jnp.mean(hidden_rows * hidden_rows, axis=-1, keepdims=True)) + norm_eps)

def doc_positions(segments):
    seq_len = segments.shape[0]
    position_ids = jnp.arange(seq_len, dtype=jnp.int32)
    before = jnp.concatenate([jnp.full((1,), -1, jnp.int32), segments[:-1]])
    doc_starts = lax.cummax(jnp.where(segments != before, position_ids, 0), axis=0)
    return (position_ids - doc_starts).astype(jnp.float32)

def rope_tables(positions, head_dim):
    half_dim = head_dim // 2
    frequency = rope_base ** (-(2.0 * jnp.arange(half_dim, dtype=jnp.float32)) / head_dim)
    angles = positions[:, None] * frequency[None, :]
    return (jnp.cos(angles), jnp.sin(angles))

def rotate(hidden_rows, cosine, sine_part):
    half_dim = hidden_rows.shape[-1] // 2
    lower_portion = hidden_rows[..., :half_dim]
    upper_half = hidden_rows[..., half_dim:]
    cos_rows = cosine[:, None, :]
    sin_rows = sine_part[:, None, :]
    return jnp.concatenate([lower_portion * cos_rows - upper_half * sin_rows, upper_half * cos_rows + lower_portion * sin_rows], axis=-1)

def visible_mask(segments, row_start, block_rows):
    seq_len = segments.shape[0]
    query_pos = row_start + jnp.arange(block_rows, dtype=jnp.int32)
    key_pos = jnp.arange(seq_len, dtype=jnp.int32)
    query_seg = lax.dynamic_slice_in_dim(segments, row_start, block_rows, 0)
    return (query_seg[:, None] == segments[None, :]) & (key_pos[None, :] <= query_pos[:, None])

def slot_tables(expert_rows, experts, capacity):
    tok_count, top_count = expert_rows.shape
    flat_ids = expert_rows.reshape(-1).astype(jnp.int32)
    one_hot = (flat_ids[:, None] == jnp.arange(experts, dtype=jnp.int32)[None, :]).astype(jnp.int32)
    running = jnp.cumsum(one_hot, axis=0).astype(jnp.int32)
    slot_ranks = lax.optimization_barrier(jnp.sum((running - one_hot) * one_hot, axis=1)).astype(jnp.int32)
    slot_index = (flat_ids * capacity + slot_ranks).astype(jnp.int32)
    pair_table = jnp.full((experts * capacity,), tok_count * top_count, jnp.int32)
    pair_table = pair_table.at[slot_index].set(jnp.arange(tok_count * top_count, dtype=jnp.int32))
    return (pair_table.reshape(experts, capacity), slot_index)

def sequence_layer(params, seq_tokens, segments, expert_rows):
    w_query, key_matrix, value_matrix, w_out, gain_attn, gain_moe, w_router, w_gate, w_up, w_down = params
    seq_len, model_width = seq_tokens.shape
    head_q = w_query.shape[1] // HEAD_SIZE
    head_kv = key_matrix.shape[1] // HEAD_SIZE
    group_size = head_q // head_kv
    normed = low(seq_tokens * rms_scale(seq_tokens) * gain_attn)
    query_lin = low_back(jnp.dot(normed, w_query, precision=highest))
    key_lin = low_back(jnp.dot(normed, key_matrix, precision=highest))
    value_rows = low(low_back(jnp.dot(normed, value_matrix, precision=highest))).reshape(seq_len, head_kv, HEAD_SIZE)
    cosine, sine_part = rope_tables(doc_positions(segments), HEAD_SIZE)
    queries = low(rotate(query_lin.reshape(seq_len, head_q, HEAD_SIZE), cosine, sine_part)).reshape(seq_len, head_kv, group_size, HEAD_SIZE)
    key_rows = low(rotate(key_lin.reshape(seq_len, head_kv, HEAD_SIZE), cosine, sine_part))
    block_rows = min(512, seq_len)
    starts = jnp.arange(seq_len // block_rows, dtype=jnp.int32) * block_rows

    def attend(row_start):
        query_block = lax.dynamic_slice_in_dim(queries, row_start, block_rows, 0)
        scores = jnp.einsum('qkgd,tkd->kgqt', query_block, key_rows, precision=highest) * att_scale
        scores = low_back(scores)
        allowed = visible_mask(segments, row_start, block_rows)
        scores = jnp.where(allowed[None, None], scores, masked_score)
        top_score = lax.optimization_barrier(jnp.max(scores, axis=-1, keepdims=True))
        weights = jnp.exp(scores - top_score)
        probabilities = low(weights / lax.optimization_barrier(jnp.sum(weights, axis=-1, keepdims=True)))
        return jnp.einsum('kgqt,tkd->qkgd', probabilities, value_rows, precision=highest)
    attended = lax.map(jax.checkpoint(attend), starts)
    attended = low(low_back(attended.reshape(seq_len, head_q * HEAD_SIZE)))
    branch = low_back(jnp.dot(attended, w_out, precision=highest))
    mixed_rows = seq_tokens + res_scale * branch
    normed_moe = low(mixed_rows * rms_scale(mixed_rows) * gain_moe)
    logits = jnp.dot(normed_moe, w_router, precision=highest)
    gate_weights = jax.nn.softmax(jnp.take_along_axis(logits, expert_rows, axis=1), axis=-1)
    blocks = seq_len // TOK_DEV
    block_ids = expert_rows.reshape(blocks, TOK_DEV, TOPK)
    pair_tables, slot_index = jax.vmap(lambda ids_block: slot_tables(ids_block, EXPERTS, CAP))(block_ids)
    token_tables = pair_tables // TOPK
    padded = jnp.concatenate([normed_moe.reshape(blocks, TOK_DEV, model_width), jnp.zeros((blocks, 1, model_width), jnp.float32)], axis=1)
    inputs = jax.vmap(lambda block_rows_in, token_table: block_rows_in[token_table])(padded, token_tables)
    inputs = low_back(jnp.transpose(inputs, (1, 0, 2, 3)).reshape(EXPERTS, blocks * CAP, model_width))
    gate_hidden = low_back(jnp.einsum('erd,edf->erf', inputs, w_gate, precision=highest))
    up_hidden = low_back(jnp.einsum('erd,edf->erf', inputs, w_up, precision=highest))
    active = low(jax.nn.silu(gate_hidden) * up_hidden)
    returned = low(low_back(jnp.einsum('erf,efd->erd', active, w_down, precision=highest)))
    returned = jnp.transpose(returned.reshape(EXPERTS, blocks, CAP, model_width), (1, 0, 2, 3)).reshape(blocks, EXPERTS * CAP, model_width)
    picked = jax.vmap(lambda block_out_rows, slot_rows: block_out_rows[slot_rows])(returned, slot_index)
    picked = picked.reshape(seq_len, TOPK, model_width)
    moe_out = jnp.einsum('tk,tkd->td', gate_weights, picked, precision=highest)
    return mixed_rows + res_scale * moe_out

def forward_pass(seq_all, params, segment_ids, expert_ids):

    def step(carried, scan_item):
        seq_tokens, segments, expert_rows = scan_item
        return (carried, jax.checkpoint(sequence_layer)(params, seq_tokens, segments, expert_rows))
    _, outputs = lax.scan(step, jnp.zeros((), jnp.float32), (seq_all, segment_ids, expert_ids))
    return outputs

def reference(tokens, segment_ids, expert_ids, w_query, key_matrix, value_matrix, w_out, norm_attn, norm_moe, w_router, w_gate, w_up, w_down, cotangent):
    params = tuple((weight_arg.astype(jnp.float32) for weight_arg in (w_query, key_matrix, value_matrix, w_out, norm_attn, norm_moe, w_router, w_gate, w_up, w_down)))
    outputs, pullback = jax.vjp(lambda seq_all, *weights: forward_pass(seq_all, weights, segment_ids, expert_ids), tokens.astype(jnp.float32), *params)
    gradients = pullback(cotangent.astype(jnp.float32))
    return (outputs, gradients[0], gradients[1], gradients[2], gradients[3], gradients[4], gradients[5], gradients[6], gradients[7], gradients[8], gradients[9], gradients[10])
```

```python
from functools import partial

import jax
import jax.numpy as jnp
from jax import lax
from jax.experimental import pallas as pl
from jax.experimental.pallas import tpu as pltpu
from jax.sharding import PartitionSpec as P

HEAD_SIZE = 64
LANES = 128
LONGEST_DOC = 768

res_scale = 0.22
att_scale = 0.015625
norm_eps = 1e-06
rope_base = 10000.0
masked_score = -1e30
log2_e = 1.4426950408889634
highest = lax.Precision.HIGHEST
bf16 = jnp.bfloat16
f32 = jnp.float32


def rms_scale(hidden_rows):
    return lax.rsqrt(jnp.mean(hidden_rows * hidden_rows, axis=-1, keepdims=True) + norm_eps)


def dot_nt(left, right):
    return lax.dot_general(left, right, (((1,), (1,)), ((), ())), preferred_element_type=f32)


def dot_tn(left, right):
    return lax.dot_general(left, right, (((0,), (0,)), ((), ())), preferred_element_type=f32)


def dot_nn(left, right):
    return jnp.dot(left, right, preferred_element_type=f32)


def rows_swap(array, distance):
    return lax.ppermute(array, "rows", [(i, i ^ distance) for i in range(4)])


def halves(array):
    axis = 0 if array.shape[0] % 2 == 0 else 1
    cut = array.shape[axis] // 2
    return (
        axis,
        lax.slice_in_dim(array, 0, cut, axis=axis),
        lax.slice_in_dim(array, cut, 2 * cut, axis=axis),
    )


def gather_near(array):
    return rows_swap(array, 1), rows_swap(array, 2)


def gather_far(array, from_x, from_y):
    axis, first_y, _ = halves(from_y)
    _, _, second_x = halves(from_x)
    far = jnp.concatenate([rows_swap(first_y, 1), rows_swap(second_x, 2)], axis=axis)
    return [array, from_x, from_y, far]


def rows_exchange(pieces):
    return [pieces[0]] + [rows_swap(pieces[j], j) for j in (1, 2, 3)]


def reduce_far(pieces):
    _, first, second = halves(pieces[3])
    return rows_swap(first, 1), rows_swap(second, 2)


def reduce_add(pieces, from_x, from_y):
    axis, first_x, second_x = halves(pieces[1])
    _, first_y, second_y = halves(pieces[2])
    return (
        jnp.concatenate([first_x, add_low(second_x, from_y)], axis=axis),
        jnp.concatenate([add_low(first_y, from_x), second_y], axis=axis),
    )


def reduce_near(to_x, to_y):
    return rows_swap(to_x, 1), rows_swap(to_y, 2)


def reduce_first(pieces):
    far = rows_swap(pieces[3][0], 1), rows_swap(pieces[3][1], 2)
    near = rows_swap(pieces[1][0], 1), rows_swap(pieces[2][1], 2)
    return far, near


def reduce_second(pieces, far):
    return add_low(pieces[1][1], far[1]), add_low(pieces[2][0], far[0])


def reduce_total(pieces, near, late):
    return [
        add_wide([pieces[0][0], near[0], late[1]]),
        add_wide([pieces[0][1], late[0], near[1]]),
    ]


def add_wide(arrays):
    return sum(array.astype(f32) for array in arrays)


def add_low_all(array):
    return jnp.sum(array.astype(f32), axis=0).astype(bf16)


def add_low(left, right):
    return (left.astype(f32) + right.astype(f32)).astype(bf16)


def chip_shift(array, distance):
    count = lax.axis_size("cols")
    return lax.ppermute(
        array, "cols", [(i, (i + 2 * distance) % count) for i in range(count)]
    )


def core_swap(array):
    count = lax.axis_size("cols")
    return lax.ppermute(array, "cols", [(i, i ^ 1) for i in range(count)])


def chips_exchange(array):
    count = lax.axis_size("cols")
    alike = [list(range(core, count, 2)) for core in range(2)]
    return lax.all_to_all(array, "cols", 0, 0, axis_index_groups=alike, tiled=True)


def chips_spread(array):
    chips = lax.axis_size("cols") // 2
    return chips_exchange(jnp.broadcast_to(array, (chips,) + array.shape))


def cores_in_order(mine, other, core, axis):
    return jnp.stack(
        [jnp.where(core == 0, mine, other), jnp.where(core == 0, other, mine)], axis=axis
    )


def call_params(mebibytes):
    return pltpu.CompilerParams(vmem_limit_bytes=mebibytes * 1024 * 1024)


def cost(micros):
    return pl.CostEstimate(flops=int(micros * 1.15e9), bytes_accessed=0, transcendentals=0)


def turn(rows, cosine, sine):
    lane = lax.broadcasted_iota(jnp.int32, rows.shape, 1)
    partner = jnp.where(
        (lane & (HEAD_SIZE - 1)) < HEAD_SIZE // 2,
        pltpu.roll(rows, LANES - HEAD_SIZE // 2, 1),
        pltpu.roll(rows, HEAD_SIZE // 2, 1),
    )
    return rows * cosine + partner * sine


def project_kernel(meta, *refs):
    parts, found, swapped, gain, cosine, sine = refs[:4], refs[4], refs[5], *refs[6:9]
    q_out, k_out, v_out, n_out, w_out = refs[9:]
    step = pl.program_id(0)
    chips, rows, _ = found.shape

    @pl.when(step == 0)
    def _():
        first_core = meta[2] == 0
        for chip in range(chips):
            mine, other = found[chip], swapped[chip]
            at = 2 * rows * chip
            w_out[at : at + rows, :] = jnp.where(first_core, mine, other)
            w_out[at + rows : at + 2 * rows, :] = jnp.where(first_core, other, mine)

    for index, part in enumerate(parts):

        @pl.when(step == index)
        def _(part=part):
            rows = part[...].astype(f32)
            n_out[0] = (rows * rms_scale(rows) * gain[...]).astype(bf16)

    linear = dot_nn(n_out[0], w_out[...])
    q_cols, k_cols = q_out.shape[1], k_out.shape[1]
    cos_rows, sin_rows = cosine[...], sine[...]
    turned = jnp.concatenate(
        [
            turn(linear[:, at : at + LANES], cos_rows, sin_rows)
            for at in range(0, q_cols + k_cols, LANES)
        ],
        axis=1,
    ).astype(bf16)
    q_out[...] = turned[:, :q_cols]
    k_out[...] = turned[:, q_cols:]
    v_out[...] = linear[:, q_cols + k_cols :].astype(bf16)


def project(meta, parts, found, swapped, gain, cosine, sine, q_cols, k_cols):
    tok, width = parts[0].shape
    length = 4 * tok
    whole = pl.BlockSpec(memory_space=pltpu.VMEM)

    def natural(step, meta):
        return (step ^ meta[0], 0)

    return pl.pallas_call(
        project_kernel,
        grid_spec=pltpu.PrefetchScalarGridSpec(
            num_scalar_prefetch=1,
            grid=(4,),
            in_specs=[whole] * 7
            + [pl.BlockSpec((tok, LANES), natural), pl.BlockSpec((tok, LANES), natural)],
            out_specs=[
                pl.BlockSpec((tok, q_cols), natural),
                pl.BlockSpec((tok, k_cols), natural),
                pl.BlockSpec((tok, k_cols), natural),
                pl.BlockSpec((1, tok, width), lambda step, meta: (step, 0, 0)),
                pl.BlockSpec((width, q_cols + 2 * k_cols), lambda step, meta: (0, 0)),
            ],
        ),
        out_shape=[
            jax.ShapeDtypeStruct((length, q_cols), bf16),
            jax.ShapeDtypeStruct((length, k_cols), bf16),
            jax.ShapeDtypeStruct((length, k_cols), bf16),
            jax.ShapeDtypeStruct((4, tok, width), bf16),
            jax.ShapeDtypeStruct((width, q_cols + 2 * k_cols), bf16),
        ],
        compiler_params=call_params(32),
        cost_estimate=cost(1),
        name="project",
    )(meta, *parts, found, swapped, gain, cosine, sine)


def attend_kernel(meta, queries, keys, values, starts, out, lse, *, bands):
    block = pl.program_id(0)
    rows = queries.shape[0]
    first = meta[3 + block]
    heads = queries.shape[1] // HEAD_SIZE
    group = queries.shape[1] // keys.shape[1]
    for band in range(1, bands + 1):

        @pl.when(block - first + 1 == band)
        def _(band=band):
            width = band * rows
            base = pl.multiple_of(first * rows, rows)
            key_band = keys[pl.ds(base, width), :]
            value_band = values[pl.ds(base, width), :]
            query_pos = block * rows + lax.broadcasted_iota(jnp.int32, (rows, width), 0)
            key_pos = base + lax.broadcasted_iota(jnp.int32, (rows, width), 1)
            allowed = (key_pos >= starts[...]) & (key_pos <= query_pos)
            results = []
            for head in range(heads):
                at = head // group * HEAD_SIZE
                scores = dot_nt(
                    queries[:, head * HEAD_SIZE : (head + 1) * HEAD_SIZE],
                    key_band[:, at : at + HEAD_SIZE],
                )
                scores = jnp.where(allowed, scores, masked_score)
                top = jnp.max(scores, axis=1, keepdims=True)
                weights = jnp.exp2((scores - top) * (att_scale * log2_e))
                total = jnp.sum(weights, axis=1, keepdims=True)
                result = dot_nn(weights.astype(bf16), value_band[:, at : at + HEAD_SIZE])
                results.append(result * (1.0 / total))
                lse[:, head : head + 1] = top * (att_scale * log2_e) + jnp.log2(total)
            out[0] = jnp.concatenate(results, axis=1).astype(bf16)


def attend(meta, queries, keys, values, starts, tok):
    length, q_cols = queries.shape
    k_cols = keys.shape[1]
    blocks = length // tok
    whole = pl.BlockSpec(memory_space=pltpu.VMEM)
    return pl.pallas_call(
        partial(attend_kernel, bands=min(blocks, LONGEST_DOC // tok + 1)),
        grid_spec=pltpu.PrefetchScalarGridSpec(
            num_scalar_prefetch=1,
            grid=(blocks,),
            in_specs=[
                pl.BlockSpec((tok, q_cols), lambda i, meta: (i, 0)),
                whole,
                whole,
                pl.BlockSpec((tok, 1), lambda i, meta: (i, 0)),
            ],
            out_specs=[
                pl.BlockSpec((1, tok, q_cols), lambda i, meta: (i, 0, 0)),
                pl.BlockSpec((tok, 8), lambda i, meta: (i, 0)),
            ],
        ),
        out_shape=[
            jax.ShapeDtypeStruct((blocks, tok, q_cols), bf16),
            jax.ShapeDtypeStruct((length, 8), f32),
        ],
        compiler_params=call_params(32),
        cost_estimate=cost(1),
        name="attend",
    )(meta, queries, keys, values, starts)


def attend_back_kernel(
    meta, queries, grads, lse, starts, keys, values, cosine, sine, out, key_sum, value_sum, *, bands
):
    block = pl.program_id(0)
    rows = queries.shape[0]
    first = meta[3 + block]
    q_cols, k_cols = queries.shape[1], keys.shape[1]
    heads = q_cols // HEAD_SIZE
    group = q_cols // k_cols

    @pl.when(block == 0)
    def _():
        key_sum[...] = jnp.zeros_like(key_sum)
        value_sum[...] = jnp.zeros_like(value_sum)

    for band in range(1, bands + 1):

        @pl.when(block - first + 1 == band)
        def _(band=band):
            width = band * rows
            base = pl.multiple_of(first * rows, rows)
            key_band = keys[pl.ds(base, width), :]
            value_band = values[pl.ds(base, width), :]
            key_pos = base + lax.broadcasted_iota(jnp.int32, (width, rows), 0)
            query_pos = block * rows + lax.broadcasted_iota(jnp.int32, (width, rows), 1)
            allowed = (key_pos >= starts[...]) & (key_pos <= query_pos)
            query_grads, key_parts, value_parts = [], [], []
            for kv_head in range(k_cols // HEAD_SIZE):
                at = kv_head * HEAD_SIZE
                key_rows = key_band[:, at : at + HEAD_SIZE]
                value_rows = value_band[:, at : at + HEAD_SIZE]
                key_part = jnp.zeros((width, HEAD_SIZE), f32)
                value_part = jnp.zeros((width, HEAD_SIZE), f32)
                for head in range(kv_head * group, (kv_head + 1) * group):
                    query_rows = queries[:, head * HEAD_SIZE : (head + 1) * HEAD_SIZE]
                    grad_rows = grads[0, :, head * HEAD_SIZE : (head + 1) * HEAD_SIZE]
                    scores = dot_nt(key_rows, query_rows)
                    probs = jnp.where(
                        allowed,
                        jnp.exp2(scores * (att_scale * log2_e) - lse[head : head + 1, :]),
                        0.0,
                    )
                    grad_probs = dot_nt(value_rows, grad_rows)
                    delta = jnp.sum(probs * grad_probs, axis=0, keepdims=True)
                    grad_scores = (probs * (grad_probs - delta)).astype(bf16)
                    value_part += dot_nn(probs.astype(bf16), grad_rows)
                    key_part += dot_nn(grad_scores, query_rows)
                    query_grads.append(dot_tn(grad_scores, key_rows))
                key_parts.append(key_part)
                value_parts.append(value_part)
            key_sum[pl.ds(base, width), :] += jnp.concatenate(key_parts, axis=1)
            value_sum[pl.ds(base, width), :] += jnp.concatenate(value_parts, axis=1)
            here = pl.ds(pl.multiple_of(block * rows, rows), rows)
            query_grad = jnp.concatenate(query_grads, axis=1) * att_scale
            turned = [
                turn(query_grad[:, c : c + LANES], cosine[here, :], -sine[here, :])
                for c in range(0, q_cols, LANES)
            ]
            out[block ^ meta[0], :, :q_cols] = jnp.concatenate(turned, axis=1).astype(bf16)

    @pl.when(block == pl.num_programs(0) - 1)
    def _():
        for part in range(4):
            here = pl.ds(pl.multiple_of((meta[0] ^ part) * rows, rows), rows)
            key_grad = key_sum[here, :] * att_scale
            turned = [
                turn(key_grad[:, c : c + LANES], cosine[here, :], -sine[here, :])
                for c in range(0, k_cols, LANES)
            ]
            out[part, :, q_cols : q_cols + k_cols] = jnp.concatenate(turned, axis=1).astype(bf16)
            out[part, :, q_cols + k_cols :] = value_sum[here, :].astype(bf16)


def attend_back(meta, queries, grads, lse, starts, keys, values, cosine, sine, tok):
    length, q_cols = queries.shape
    k_cols = keys.shape[1]
    blocks = length // tok
    whole = pl.BlockSpec(memory_space=pltpu.VMEM)
    return pl.pallas_call(
        partial(attend_back_kernel, bands=min(blocks, LONGEST_DOC // tok + 1)),
        grid_spec=pltpu.PrefetchScalarGridSpec(
            num_scalar_prefetch=1,
            grid=(blocks,),
            in_specs=[
                pl.BlockSpec((tok, q_cols), lambda i, meta: (i, 0)),
                pl.BlockSpec((1, tok, q_cols), lambda i, meta: (i, 0, 0)),
                pl.BlockSpec((8, tok), lambda i, meta: (0, i)),
                pl.BlockSpec((1, tok), lambda i, meta: (0, i)),
                whole,
                whole,
                whole,
                whole,
            ],
            out_specs=pl.BlockSpec(
                (blocks, tok, q_cols + 2 * k_cols), lambda i, meta: (0, 0, 0)
            ),
            scratch_shapes=[
                pltpu.VMEM((length, k_cols), f32),
                pltpu.VMEM((length, k_cols), f32),
            ],
        ),
        out_shape=jax.ShapeDtypeStruct((blocks, tok, q_cols + 2 * k_cols), bf16),
        compiler_params=call_params(40),
        cost_estimate=cost(29),
        name="attend_back",
    )(meta, queries, grads, lse, starts, keys, values, cosine, sine)


def low_pair(values):
    high = values.astype(bf16)
    return high, (values - high.astype(f32)).astype(bf16)


def mix_kernel(
    meta, heads, out_parts, tokens, member, gain, router, mixed_out, rows_out, gates_out, *, experts
):
    width = tokens.shape[1]
    branch = sum(dot_nn(heads[meta[0] ^ part], out_parts[part]) for part in range(4))
    mixed = tokens[...].astype(f32) + res_scale * branch
    mixed_out[...] = mixed
    normed = (mixed * rms_scale(mixed) * gain[...]).astype(bf16)
    logits = dot_nn(normed, router[...])
    named = member[...] > 0
    logits = jnp.where(named, logits, masked_score)
    lifted = jnp.exp(logits - jnp.max(logits, axis=1, keepdims=True))
    lifted = jnp.where(named, lifted, 0.0)
    gates = lifted * (1.0 / jnp.sum(lifted, axis=1, keepdims=True))
    gates_out[...] = gates
    high, low = low_pair(gates)
    low = pltpu.roll(low.astype(f32), experts, 1)
    rows_out[:, :width] = normed
    rows_out[:, width:] = (high.astype(f32) + low).astype(bf16)


def mix(meta, heads, out_parts, tokens, member, gain, router, experts):
    tok, width = tokens.shape
    whole = pl.BlockSpec(memory_space=pltpu.VMEM)
    return pl.pallas_call(
        partial(mix_kernel, experts=experts),
        in_specs=[pl.BlockSpec(memory_space=pltpu.SMEM)] + [whole] * 6,
        out_specs=[whole] * 3,
        out_shape=[
            jax.ShapeDtypeStruct((tok, width), f32),
            jax.ShapeDtypeStruct((tok, width + LANES), bf16),
            jax.ShapeDtypeStruct((tok, LANES), f32),
        ],
        compiler_params=call_params(40),
        cost_estimate=cost(6),
        name="mix",
    )(meta, heads, out_parts, tokens, member, gain, router)


def unmix_kernel(
    meta, came, last, mixed_in, cotangent, gates, gain, router, out_parts, heads,
    mixed_grad, heads_out, mine_out, other_out, *, experts
):
    width = cotangent.shape[1]
    summed = came[...].astype(f32) + last[...].astype(f32)
    beside = summed[:, width:]
    lane = lax.broadcasted_iota(jnp.int32, beside.shape, 1)
    weighted = jnp.where(lane < experts, beside + pltpu.roll(beside, LANES - experts, 1), 0.0)
    logit_grads = weighted - gates[...] * jnp.sum(weighted, axis=1, keepdims=True)
    high, low = low_pair(logit_grads)
    normed_grad = summed[:, :width] + dot_nt(high, router[...]) + dot_nt(low, router[...])
    mixed = mixed_in[...]
    scale = rms_scale(mixed)
    unit = mixed * scale
    normed = (unit * gain[...]).astype(bf16)
    one_lane = lax.broadcasted_iota(jnp.int32, (unit.shape[0], LANES), 1) == experts
    one_lane = one_lane.astype(f32).astype(bf16)
    gain_high, gain_low = low_pair(normed_grad * unit)
    shares = dot_tn(normed, high) + dot_tn(normed, low)
    shares = (shares + dot_tn(gain_high, one_lane) + dot_tn(gain_low, one_lane)).astype(bf16)
    unit_grad = normed_grad * gain[...]
    grad = cotangent[...].astype(f32) + scale * (
        unit_grad - unit * jnp.mean(unit_grad * unit, axis=-1, keepdims=True)
    )
    mixed_grad[...] = grad
    branch = (res_scale * grad).astype(bf16)
    for part in range(4):
        heads_out[meta[0] ^ part] = dot_nt(branch, out_parts[part]).astype(bf16)
    first_core = meta[2] == 0
    _, chips, sixth, _ = mine_out.shape
    tok = branch.shape[0]
    for part in range(4):
        wide = dot_tn(heads[part], branch).astype(bf16)
        wide = jnp.concatenate([wide, shares[part * tok : (part + 1) * tok]], axis=1)
        for chip in range(chips):
            at = 2 * chip * sixth
            even, odd = wide[at : at + sixth], wide[at + sixth : at + 2 * sixth]
            mine_out[part, chip] = jnp.where(first_core, even, odd)
            other_out[part, chip] = jnp.where(first_core, odd, even)


def unmix(meta, came, last, mixed, cotangent, gates, gain, router, out_parts, heads, experts, chips):
    tok, width = mixed.shape
    wide = (4, chips, tok // (2 * chips), width + LANES)
    whole = pl.BlockSpec(memory_space=pltpu.VMEM)
    return pl.pallas_call(
        partial(unmix_kernel, experts=experts),
        in_specs=[pl.BlockSpec(memory_space=pltpu.SMEM)] + [whole] * 9,
        out_specs=[whole] * 4,
        out_shape=[
            jax.ShapeDtypeStruct((tok, width), f32),
            jax.ShapeDtypeStruct((4, tok, out_parts.shape[1]), bf16),
            jax.ShapeDtypeStruct(wide, bf16),
            jax.ShapeDtypeStruct(wide, bf16),
        ],
        compiler_params=call_params(32),
        cost_estimate=cost(12),
        name="unmix",
    )(meta, came, last, mixed, cotangent, gates, gain, router, out_parts, heads)


def hidden_weights(parts, cut, ffe):
    tiles = 2 * ffe // LANES
    return jnp.concatenate(
        [
            jnp.concatenate([ref[0, t * cut : (t + 1) * cut, :] for t in range(tiles)], axis=1)
            for ref in parts
        ],
        axis=0,
    )


def down_weights(parts, cut, ffe):
    first = 2 * ffe // LANES * cut
    return jnp.concatenate(
        [
            ref[0, first + t * ffe : first + (t + 1) * ffe, :]
            for ref in parts
            for t in range(cut // LANES)
        ],
        axis=1,
    )


def experts_kernel(meta, *refs, experts, slots, local, final, earlier):
    blocks = 4
    x_refs, g_refs, refs = refs[:blocks], refs[blocks : 2 * blocks], refs[2 * blocks :]
    early, refs = refs[:earlier], refs[earlier:]
    parts, refs = refs[:4], refs[4:]
    returned_out, refs = refs[: blocks * final], refs[blocks * final :]
    x_out, g_out, active_out, grads_out, out_kept, dx_kept, t_kept, refs = *refs[:7], refs[7:]
    x_rows, g_rows, gate_kept, rows_sent, x_here, g_here, arrived, refs = *refs[:7], refs[7:]
    own = pl.program_id(0)
    own_count = x_rows.shape[0]
    tok = x_refs[0].shape[0]
    width = x_rows.shape[2]
    cut = width // 4
    ffe = active_out.shape[2]
    row, first_expert = meta[0], meta[1]
    loads = [
        (
            pltpu.make_async_copy(x_refs[block], x_here.at[block % 2], arrived.at[0, block % 2]),
            pltpu.make_async_copy(g_refs[block], g_here.at[block % 2], arrived.at[1, block % 2]),
        )
        for block in range(blocks)
    ]
    if final:
        ranks_kept, returned, sent, refs = *refs[:3], refs[3:]
    fetches = [
        [
            pltpu.make_async_copy(
                early[which].at[:, pl.ds(block * slots, slots), :],
                refs[which].at[block % 2],
                refs[3].at[which, block % 2],
            )
            for which in range(earlier)
        ]
        for block in range(blocks)
    ]
    row_copies = [
        pltpu.make_async_copy(x_rows, x_out, rows_sent.at[0]),
        pltpu.make_async_copy(g_rows, g_out, rows_sent.at[1]),
    ]

    def columns(part, start=0):
        return pl.ds(pl.multiple_of(start + (row ^ part) * cut, LANES), cut)

    @pl.when(own == 0)
    def _():
        for load in loads[0]:
            load.start()
        slot = lax.broadcasted_iota(jnp.int32, (slots, tok), 0).astype(f32)
        lower = (
            lax.broadcasted_iota(jnp.int32, (tok, tok), 0)
            > lax.broadcasted_iota(jnp.int32, (tok, tok), 1)
        ).astype(f32).astype(bf16)
        source = lax.broadcasted_iota(jnp.int32, (LANES, LANES), 1)
        target = lax.broadcasted_iota(jnp.int32, (LANES, LANES), 0)
        choose = (source == target + first_expert).astype(f32).astype(bf16)
        for block in range(blocks):
            for load in loads[block + 1] if block + 1 < blocks else ():
                load.start()
            for load in loads[block]:
                load.wait()
            x_block, g_block = x_here.at[block % 2], g_here.at[block % 2]
            member = g_block[:, width:]
            rank = jnp.where(member > 0, dot_nn(lower, member), -1.0).astype(bf16)
            if final:
                ranks_kept[block] = dot_nt(rank, choose)
            rank_rows = dot_nt(choose, rank)
            pick = jnp.concatenate(
                [
                    (rank_rows[index : index + 1, :] == slot).astype(f32).astype(bf16)
                    for index in range(local, local + own_count)
                ],
                axis=0,
            )
            beside = dot_nn(pick, x_block[:, width:])
            lane = lax.broadcasted_iota(jnp.int32, beside.shape, 1)
            named = lax.broadcasted_iota(jnp.int32, beside.shape, 0) // slots
            named = named + first_expert + local
            gates = jnp.sum(
                jnp.where((lane == named) | (lane == named + experts), beside, 0.0),
                axis=1,
                keepdims=True,
            )
            here = slice(block * slots, (block + 1) * slots)
            x_part = dot_nn(pick, x_block[:, :width]).astype(bf16)
            g_part = dot_nn(pick, g_block[:, :width]).astype(bf16)
            for index in range(own_count):
                rows = slice(index * slots, (index + 1) * slots)
                gate_kept[index, here, :] = gates[rows]
                for part in range(4):
                    there = slice(part * cut, (part + 1) * cut)
                    x_rows[index, here, columns(part)] = x_part[rows, there]
                    g_rows[index, here, columns(part)] = g_part[rows, there]
        for copy in row_copies:
            copy.start()

    @pl.when(own == own_count - 1)
    def _():
        for fetch in fetches[0] + fetches[1]:
            fetch.start()

    hidden_w = hidden_weights(parts, cut, ffe)
    down_w = down_weights(parts, cut, ffe)
    hidden = dot_nn(x_rows[own], hidden_w)
    hidden_gate, hidden_up = hidden[:, :ffe], hidden[:, ffe:]
    gates = gate_kept[own]
    grad_active = dot_nt(g_rows[own], down_w) * (res_scale * gates)
    sigmoid = jax.nn.sigmoid(hidden_gate)
    silu = hidden_gate * sigmoid
    active = silu * hidden_up
    gated = (active * gates).astype(bf16)
    grad_gate = grad_active * hidden_up * (sigmoid * (1.0 + hidden_gate * (1.0 - sigmoid)))
    grads = jnp.concatenate(
        [grad_gate.astype(bf16), (grad_active * silu).astype(bf16)], axis=1
    )
    weighted = jnp.sum(active * grad_active, axis=1, keepdims=True)
    active_out[0] = gated
    grads_out[0] = grads
    kept = own if final else 0
    out_kept[kept] = dot_nn(gated, down_w).astype(bf16)
    dx_kept[kept] = dot_nt(grads, hidden_w).astype(bf16)
    weighted_high = weighted.astype(bf16).astype(f32)
    lane = lax.broadcasted_iota(jnp.int32, (blocks * slots, LANES), 1)
    named = first_expert + local + own
    t_kept[kept] = jnp.where(
        lane == named,
        weighted_high,
        jnp.where(lane == named + experts, weighted - weighted_high, 0.0),
    ).astype(bf16)

    @pl.when(own == own_count - 1)
    def _():
        if final:
            slot = lax.broadcasted_iota(jnp.int32, (tok, slots), 1).astype(f32)
            gives = [
                pltpu.make_async_copy(
                    returned.at[block % 2], returned_out[block], sent.at[block]
                )
                for block in range(blocks)
            ]
            for block in range(blocks):
                here = slice(block * slots, (block + 1) * slots)
                put = jnp.concatenate(
                    [
                        (ranks_kept[block, :, index : index + 1] == slot).astype(f32).astype(bf16)
                        for index in range(local + own_count)
                    ],
                    axis=1,
                )

                def rows_of(which, here=here, block=block):
                    kept_rows = (out_kept, dx_kept, t_kept)[which]
                    found = [refs[which][block % 2, index] for index in range(local)]
                    found += [kept_rows[index, here, :] for index in range(own_count)]
                    return jnp.concatenate(found, axis=0)

                for fetch in fetches[block]:
                    fetch.wait()
                if block >= 2:
                    gives[block - 2].wait()
                out = dot_nn(put, rows_of(0)).astype(bf16)
                dx = dot_nn(put, rows_of(1)).astype(bf16)
                for part in range(4):
                    there = slice(part * cut, (part + 1) * cut)
                    returned[block % 2, :, columns(part)] = out[:, there]
                    returned[block % 2, :, columns(part, width)] = dx[:, there]
                returned[block % 2, :, 2 * width :] = dot_nn(put, rows_of(2)).astype(bf16)
                gives[block].start()
                for fetch in fetches[block + 2] if block + 2 < blocks else ():
                    fetch.start()
            for give in gives[-2:]:
                give.wait()
        for copy in row_copies:
            copy.wait()


def run_experts(meta, x_blocks, g_blocks, early, parts, ffe, experts, slots, local, final):
    blocks = len(x_blocks)
    tok, padded = x_blocks[0].shape
    width = padded - LANES
    own, packed, _ = parts[0].shape
    rows = blocks * slots
    anywhere = pl.BlockSpec(memory_space=pl.ANY)
    back = 2 * width + LANES
    kept_shapes = [(own, rows, width), (own, rows, width), (own, rows, LANES)]
    row_shapes = [(own, rows, width), (own, rows, width), (own, rows, ffe), (own, rows, 2 * ffe)]

    def one(*shape):
        return pl.BlockSpec((1,) + shape, lambda e, meta: (e, 0, 0))

    out_specs = [anywhere] * 2 + [one(rows, ffe), one(rows, 2 * ffe)]
    out_shapes = [jax.ShapeDtypeStruct(shape, bf16) for shape in row_shapes]
    scratch = []
    if final:
        out_specs = [anywhere] * blocks + out_specs
        out_shapes = [jax.ShapeDtypeStruct((tok, back), bf16)] * blocks + out_shapes
        scratch += [pltpu.VMEM(shape, bf16) for shape in kept_shapes]
    else:
        out_specs += [one(*shape[1:]) for shape in kept_shapes]
        out_shapes += [jax.ShapeDtypeStruct(shape, bf16) for shape in kept_shapes]
    scratch += [
        pltpu.VMEM((own, rows, width), bf16),
        pltpu.VMEM((own, rows, width), bf16),
        pltpu.VMEM((own, rows, 1), f32),
        pltpu.SemaphoreType.DMA((2,)),
        pltpu.VMEM((2, tok, padded), bf16),
        pltpu.VMEM((2, tok, padded), bf16),
        pltpu.SemaphoreType.DMA((2, 2)),
    ]
    if final:
        scratch += [
            pltpu.VMEM((blocks, tok, LANES), f32),
            pltpu.VMEM((2, tok, back), bf16),
            pltpu.SemaphoreType.DMA((blocks,)),
        ]
    if early:
        scratch += [
            pltpu.VMEM((2, array.shape[0], slots, array.shape[2]), bf16) for array in early
        ] + [pltpu.SemaphoreType.DMA((3, 2))]
    return pl.pallas_call(
        partial(
            experts_kernel,
            experts=experts,
            slots=slots,
            local=local,
            final=final,
            earlier=len(early),
        ),
        grid_spec=pltpu.PrefetchScalarGridSpec(
            num_scalar_prefetch=1,
            grid=(own,),
            in_specs=[anywhere] * (2 * blocks + len(early)) + [one(packed, LANES)] * 4,
            out_specs=out_specs,
            scratch_shapes=scratch,
        ),
        out_shape=out_shapes,
        compiler_params=call_params(60),
        cost_estimate=cost(26),
        name="experts",
    )(meta, *x_blocks, *g_blocks, *early, *parts)


def weight_grad_kernel(*refs, chunks, own_count):
    x_refs, grad_refs, active_refs, g_refs = (
        refs[chunks * index : chunks * (index + 1)] for index in range(4)
    )
    refs = refs[4 * chunks :]
    outs, (made, sent) = refs[: 4 * own_count], refs[4 * own_count :]
    x_rows = jnp.concatenate([ref[0] for ref in x_refs], axis=0)
    grads = jnp.concatenate([ref[0] for ref in grad_refs], axis=0)
    active = jnp.concatenate([ref[0] for ref in active_refs], axis=0)
    g_rows = jnp.concatenate([ref[0] for ref in g_refs], axis=0)
    cut = x_rows.shape[1] // 4
    ffe = grads.shape[1] // 2
    first = 2 * ffe // LANES * cut
    own = pl.program_id(0)
    for part in range(4):
        hidden = dot_tn(x_rows[:, part * cut : (part + 1) * cut], grads).astype(bf16)
        for t in range(2 * ffe // LANES):
            made[own, part, t * cut : (t + 1) * cut, :] = hidden[:, t * LANES : (t + 1) * LANES]
    down = (dot_tn(active, g_rows) * res_scale).astype(bf16)
    for part in range(4):
        for t in range(cut // LANES):
            at = part * cut + t * LANES
            here = slice(first + t * ffe, first + (t + 1) * ffe)
            made[own, part, here, :] = down[:, at : at + LANES]
    copies = [
        [
            pltpu.make_async_copy(
                made.at[expert, part], outs[part * own_count + expert].at[0], sent.at[expert, part]
            )
            for part in range(4)
        ]
        for expert in range(own_count)
    ]
    for expert in range(own_count):

        @pl.when(own == expert)
        def _(expert=expert):
            for copy in copies[expert]:
                copy.start()

    @pl.when(own == own_count - 1)
    def _():
        for group in copies:
            for copy in group:
                copy.wait()


def weight_grads(x_chunks, grad_chunks, active_chunks, g_chunks):
    own, rows, width = x_chunks[0].shape
    ffe = active_chunks[0].shape[2]
    chunks = len(x_chunks)
    packed = 3 * ffe * (width // 4) // LANES

    def one(*shape):
        return pl.BlockSpec((1,) + shape, lambda e: (e, 0, 0))

    outs = pl.pallas_call(
        partial(weight_grad_kernel, chunks=chunks, own_count=own),
        grid=(own,),
        in_specs=[one(rows, width)] * chunks
        + [one(rows, 2 * ffe)] * chunks
        + [one(rows, ffe)] * chunks
        + [one(rows, width)] * chunks,
        out_specs=[pl.BlockSpec(memory_space=pl.ANY)] * (4 * own),
        out_shape=[jax.ShapeDtypeStruct((1, packed, LANES), bf16)] * (4 * own),
        scratch_shapes=[
            pltpu.VMEM((own, 4, packed, LANES), bf16),
            pltpu.SemaphoreType.DMA((own, 4)),
        ],
        compiler_params=call_params(60),
        cost_estimate=cost(13),
        name="weight_grads",
    )(*x_chunks, *grad_chunks, *active_chunks, *g_chunks)
    return [list(outs[part * own : (part + 1) * own]) for part in range(4)]


def two_halves(arrays):
    return arrays if len(arrays) == 2 else list(halves(arrays[0])[1:])


def join_halves(arrays, own):
    return arrays if own == 2 else [jnp.concatenate(arrays, axis=1)]


def pack_weights(gate, up, down):
    return jnp.concatenate(
        [
            lax.slice_in_dim(array, at, at + LANES, axis=2)
            for array in (gate, up, down)
            for at in range(0, array.shape[2], LANES)
        ],
        axis=1,
    )


def unpack_weights(packed, cut, ffe):
    tiles = ffe // LANES

    def beside(first, rows, count):
        return jnp.concatenate(
            [packed[:, first + t * rows : first + (t + 1) * rows, :] for t in range(count)], axis=2
        )

    return (
        beside(0, cut, tiles),
        beside(tiles * cut, cut, tiles),
        beside(2 * tiles * cut, ffe, cut // LANES),
    )


def after(array, *earlier):
    return lax.optimization_barrier((array, earlier))[0]


def per_device(
    tokens,
    segment_ids,
    expert_ids,
    w_query,
    key_matrix,
    value_matrix,
    w_out,
    norm_attn,
    norm_moe,
    w_router,
    w_gate,
    w_up,
    w_down,
    cotangent,
):
    row = lax.axis_index("rows")
    column = lax.axis_index("cols")
    columns = lax.axis_size("cols")
    chips = columns // 2
    chip, core = column // 2, column % 2
    own_tokens = tokens[0]
    tok, width = own_tokens.shape
    own_experts = w_gate.shape[0]
    experts = own_experts * columns
    top_count = expert_ids.shape[2]
    capacity = 5 * tok * top_count // (4 * experts)
    slots = -(-capacity // LANES) * LANES
    q_cols, k_cols = w_query.shape[1], key_matrix.shape[1]

    token_near = gather_near(own_tokens)
    project_rows = jnp.concatenate([w_query, key_matrix, value_matrix], axis=1)
    project_found = chips_spread(project_rows)
    project_swapped = core_swap(project_found)
    sixth = w_out.shape[0]
    out_half = chips_spread(after(w_out, project_found)).reshape(chips * sixth, width)
    small = jnp.concatenate(
        [
            w_router,
            norm_attn[:, None],
            norm_moe[:, None],
            jnp.zeros((w_router.shape[0], LANES - experts - 2), bf16),
        ],
        axis=1,
    )
    small_full = lax.all_to_all(
        jnp.tile(after(small, out_half), (4 * columns, 1)), ("rows", "cols"), 0, 0, tiled=True
    )
    gain_attn = small_full[:, experts].astype(f32)[None, :]
    gain_moe = small_full[:, experts + 1].astype(f32)[None, :]
    router_full = jnp.where(jnp.arange(LANES) < experts, small_full, 0)
    token_parts = gather_far(own_tokens, *token_near)
    qkv_cols = q_cols + 2 * k_cols
    out_near = gather_near(after(out_half, token_near))

    expert_rows = expert_ids[0]
    lane_range = jnp.arange(LANES, dtype=jnp.int32)
    member = jnp.any(expert_rows[:, :, None] == lane_range[None, None, :], axis=1).astype(bf16)
    cot_rows = jnp.concatenate([cotangent[0], member], axis=1)
    cot_same = [cot_rows, chip_shift(after(cot_rows, out_half), 1)]

    groups = 2 if own_experts % 2 == 0 else 1
    group_size = own_experts // groups
    packed = []
    for group in range(groups):
        here = slice(group * group_size, (group + 1) * group_size)
        packed.append(pack_weights(after(w_gate[here], own_tokens), w_up[here], w_down[here]))
    weight_near = [gather_near(after(packed[0], token_parts[3], project_swapped, out_near))]

    segments = segment_ids[0]
    length = segments.shape[0]
    starts = jnp.sum((segments[None, :] < segments[:, None]).astype(jnp.int32), axis=1)
    positions = (jnp.arange(length, dtype=jnp.int32) - starts).astype(f32)
    half = HEAD_SIZE // 2
    frequency = rope_base ** (-(2.0 * jnp.arange(half, dtype=f32)) / HEAD_SIZE)
    angles = positions[:, None] * frequency[None, :]
    cos_half, sin_half = jnp.cos(angles), jnp.sin(angles)
    cosine = jnp.concatenate([cos_half] * 4, axis=1)
    sine = jnp.concatenate([-sin_half, sin_half] * 2, axis=1)
    first_blocks = starts[::tok] // tok
    place = jnp.stack([row, chip, core])
    meta = jnp.concatenate([place.astype(jnp.int32), first_blocks.astype(jnp.int32)])

    queries, key_rows, value_rows, normed, project_w = project(
        meta, token_parts, project_found, project_swapped, gain_attn, cosine, sine, q_cols, k_cols
    )
    cot_same[1] = after(cot_same[1], queries)
    attended, lse = attend(after(meta, cot_same[1]), queries, key_rows, value_rows, starts[:, None], tok)
    cot_other = [core_swap(rows) for rows in cot_same]
    for d in range(2, chips):
        cot_same.append(chip_shift(cot_same[-1], 1))
    attended, out_near = after((attended, out_near), weight_near[0], cot_same[3], cot_other)
    own_heads = lax.all_to_all(attended, "rows", 0, 0, tiled=True)
    out_mine = jnp.stack(gather_far(out_half, *out_near)).reshape(4, chips, sixth, width)
    out_parts = cores_in_order(out_mine, core_swap(out_mine), core, 2).reshape(4, tok, width)
    weight_near[0] = after(weight_near[0], own_heads)
    weight_parts = [gather_far(packed[0], *weight_near[0])]
    mixed_rows, moe_rows, gates = mix(
        meta,
        own_heads,
        out_parts,
        own_tokens,
        member,
        gain_moe,
        router_full,
        experts,
    )
    for group in range(1, groups):
        weight_near.append(gather_near(after(packed[group], weight_parts[0][3], moe_rows)))
    moe_same = [moe_rows, chip_shift(moe_rows, 1)]
    moe_other = [core_swap(rows) for rows in moe_same]
    moe_same.append(chip_shift(moe_same[1], 1))
    cot_other += [core_swap(rows) for rows in cot_same[2:]]

    moe_meta = jnp.stack([row, column * own_experts]).astype(jnp.int32)
    ffe = w_down.shape[1]
    kept = [[] for _ in range(groups)]
    pieces = [None] * chips
    grads = []

    def piece(d, start, stop):
        return add_low(pieces[d][0][:, start:stop], pieces[d][1][:, start:stop])

    both = 2 * width + LANES
    pairs = [(d, d + 1) for d in range(0, chips, 2)]
    early = [[] for _ in pairs]
    held = ()
    far, near, late, sums = [], [], [], []

    def make_grads(group, first_rows):
        chunks = kept[group]
        parts = weight_grads(
            [first_rows] + [k[0] for k in chunks[1:]],
            [k[3] for k in chunks],
            [k[2] for k in chunks],
            [k[1] for k in chunks],
        )
        grads.append([two_halves(part) for part in parts])
        for store, sent in zip((far, near), reduce_first(grads[-1])):
            store.append(sent)

    for group in range(groups):
        final = group == groups - 1
        for index, pair in enumerate(pairs):
            result = list(
                run_experts(
                    after(moe_meta, held),
                    [rows for d in pair for rows in (moe_same[d], moe_other[d])],
                    [rows for d in pair for rows in (cot_same[d], cot_other[d])],
                    early[index],
                    weight_parts[group],
                    ffe,
                    experts,
                    slots,
                    group * group_size,
                    final,
                )
            )
            held = result[0]
            if len(moe_other) == 2:
                moe_same[2] = after(moe_same[2], held)
                for d in range(3, chips):
                    moe_same.append(chip_shift(moe_same[-1], 1))
                moe_other += [core_swap(rows) for rows in moe_same[2:]]
                for later in range(1, groups):
                    weight_near[later] = after(weight_near[later], held)
                    weight_parts.append(gather_far(packed[later], *weight_near[later]))
            if not final:
                kept[group].append(result[:4])
                early[index] = result[4:]
                continue
            if index > 0:
                result = after(result, near, dx_hop)
            kept[group].append(result[4:8])
            for place, d in enumerate(pair):
                pieces[d] = (result[2 * place], core_swap(result[2 * place + 1]))
            if index == 0:
                dx_ring = piece(1, width, both)
                if groups > 1:
                    sums.append(reduce_second(grads[0], after(far[0], result[0])))
                    late.append([rows_swap(*sent) for sent in zip(sums[0], (1, 2))])
                held = (dx_ring, sums)
                dx_hop = chip_shift(dx_ring, 1)
                continue
            for d in pair:
                came = dx_hop if d == 2 else chip_shift(dx_ring, 1)
                if d == chips - 1:
                    came = after(came, grads[-1], late)
                    outs = [piece(at, 0, width) for at in range(chips - 1)]
                dx_ring = add_low(came, piece(d, width, both))
                if d == chips - 2:
                    make_grads(group, after(kept[group][0][0], dx_ring))
        if not final:
            make_grads(group, kept[group][0][0])
            held = grads[-1]
    outs.append(piece(chips - 1, 0, width))
    last_piece = piece(0, width, both)
    dx_came = after(chip_shift(dx_ring, 1), outs, last_piece)
    out_hop = chip_shift(after(outs[1], dx_came), 1)

    grad_mixed, grad_heads, wide_mine, wide_other = unmix(
        after(meta, far[-1]),
        dx_came,
        last_piece,
        mixed_rows,
        cotangent[0],
        gates,
        gain_moe,
        router_full,
        out_parts,
        own_heads,
        experts,
        chips,
    )
    grad_attended = lax.all_to_all(after(grad_heads, near[-1]), "rows", 0, 0, tiled=True)

    out_ring = add_low(after(out_hop, grad_attended), outs[2])
    wide_chip = add_low(wide_mine, core_swap(wide_other))
    wide_row = add_low_all(lax.all_to_all(wide_chip, "rows", 0, 0, tiled=True))
    wide_sum = jnp.sum(chips_exchange(wide_row).astype(f32), axis=0)
    grad_out_w = wide_sum[:, :width]
    grad_router_w = wide_sum[:, width : width + experts]
    grad_gain_moe_w = wide_sum[:, width + experts]

    sums.append(after(reduce_second(grads[-1], far[-1]), grad_attended))
    late.append([rows_swap(*sent) for sent in zip(sums[-1], (1, 2))])
    grad_lin = attend_back(
        after(meta, wide_chip, sums),
        queries,
        grad_attended,
        lse.T,
        starts[None, :],
        key_rows,
        value_rows,
        cosine,
        sine,
        tok,
    )
    grad_lin = after(grad_lin, late)
    normed_parts = [None] * 4
    for j in (3, 1, 2, 0):
        normed_parts[j] = dot_nt(grad_lin[j], project_w).astype(bf16)
    normed_sums = reduce_add(normed_parts, *after(reduce_far(normed_parts), wide_row))
    grad_normed = add_wide([normed_parts[0], *reduce_near(*normed_sums)])
    grad_project = dot_tn(normed.reshape(length, width), grad_lin.reshape(length, qkv_cols))
    project_pairs = grad_project.astype(bf16).reshape(chips, 2, width // columns, qkv_cols)
    project_chip = add_low(
        lax.dynamic_index_in_dim(project_pairs, core, 1, keepdims=False),
        core_swap(lax.dynamic_index_in_dim(project_pairs, 1 - core, 1, keepdims=False)),
    )
    project_sum = jnp.sum(chips_exchange(project_chip).astype(f32), axis=0)

    for d in range(3, chips):
        out_ring = add_low(after(chip_shift(out_ring, 1), grad_lin), outs[d])
    moe_out = add_wide([after(chip_shift(out_ring, 1), *normed_sums), outs[0]])
    block_out = mixed_rows + res_scale * moe_out

    totals = []
    for parts, soon, last in zip(grads, near, late):
        total = reduce_total([after(parts[0], *normed_sums)], soon, last)
        for array in join_halves(total, group_size):
            totals.append(unpack_weights(array, width // 4, ffe))
    grad_gate_w, grad_up_w, grad_down_w = (
        jnp.concatenate(arrays, axis=0) for arrays in zip(*totals)
    )

    own_w = jnp.concatenate([w_query, key_matrix, value_matrix], axis=1).astype(f32)
    own_gain = lax.dynamic_slice_in_dim(gain_attn[0], column * own_w.shape[0], own_w.shape[0], 0)
    gain_rows = (jnp.sum(project_sum * own_w, axis=1) / own_gain).reshape(4, -1)
    gain_sum = jnp.sum(lax.all_to_all(gain_rows, "rows", 0, 0, tiled=True), axis=0)
    grad_gain_attn = lax.ppermute(
        gain_sum,
        ("rows", "cols"),
        [(r * columns + c, 4 * c + r) for r in range(4) for c in range(columns)],
    )

    own_float = own_tokens.astype(f32)
    scale_attn = rms_scale(own_float)
    unit_attn = own_float * scale_attn
    grad_unit = grad_normed * gain_attn
    grad_tokens = grad_mixed + scale_attn * (
        grad_unit - unit_attn * jnp.mean(grad_unit * unit_attn, axis=-1, keepdims=True)
    )
    return (
        block_out[None],
        grad_tokens[None],
        project_sum[:, :q_cols],
        project_sum[:, q_cols : q_cols + k_cols],
        project_sum[:, q_cols + k_cols :],
        grad_out_w,
        grad_gain_attn,
        grad_gain_moe_w,
        grad_router_w,
        grad_gate_w,
        grad_up_w,
        grad_down_w,
    )


def solution(mesh):
    placed = (
        P("cols", "rows", None),
        P("cols", None),
        P("cols", "rows", None),
        P("cols", "rows"),
        P("cols", "rows"),
        P("cols", "rows"),
        P(("rows", "cols"), None),
        P(("rows", "cols")),
        P(("rows", "cols")),
        P(("rows", "cols"), None),
        P("cols", "rows", None),
        P("cols", "rows", None),
        P("cols", None, "rows"),
        P("cols", "rows", None),
    )
    return jax.shard_map(
        per_device,
        mesh=mesh,
        in_specs=placed,
        out_specs=(
            P("cols", "rows", None),
            P("cols", "rows", None),
            P("cols", "rows"),
            P("cols", "rows"),
            P("cols", "rows"),
            P(("rows", "cols"), None),
            P(("rows", "cols")),
            P(("rows", "cols")),
            P(("rows", "cols"), None),
            P("cols", "rows", None),
            P("cols", "rows", None),
            P("cols", None, "rows"),
        ),
        check_vma=False,
    )
```

```python
from functools import partial

import jax
import jax.numpy as jnp
from jax import lax
from jax.experimental import pallas as pl
from jax.experimental.pallas import tpu as pltpu
from jax.sharding import PartitionSpec as P

HEAD_SIZE = 64
LANES = 128
LONGEST_DOC = 768

res_scale = 0.22
att_scale = 0.015625
norm_eps = 1e-06
rope_base = 10000.0
masked_score = -1e30
log2_e = 1.4426950408889634
highest = lax.Precision.HIGHEST
bf16 = jnp.bfloat16
f32 = jnp.float32


def rms_scale(hidden_rows):
    return lax.rsqrt(jnp.mean(hidden_rows * hidden_rows, axis=-1, keepdims=True) + norm_eps)


def dot_nt(left, right):
    return lax.dot_general(left, right, (((1,), (1,)), ((), ())), preferred_element_type=f32)


def dot_tn(left, right):
    return lax.dot_general(left, right, (((0,), (0,)), ((), ())), preferred_element_type=f32)


def dot_nn(left, right):
    return jnp.dot(left, right, preferred_element_type=f32)


def rows_swap(array, distance):
    return lax.ppermute(array, "rows", [(i, i ^ distance) for i in range(4)])


def halves(array):
    axis = 0 if array.shape[0] % 2 == 0 else 1
    cut = array.shape[axis] // 2
    return (
        axis,
        lax.slice_in_dim(array, 0, cut, axis=axis),
        lax.slice_in_dim(array, cut, 2 * cut, axis=axis),
    )


def gather_near(array):
    return rows_swap(array, 1), rows_swap(array, 2)


def gather_far(array, from_x, from_y):
    axis, first_y, _ = halves(from_y)
    _, _, second_x = halves(from_x)
    far = jnp.concatenate([rows_swap(first_y, 1), rows_swap(second_x, 2)], axis=axis)
    return [array, from_x, from_y, far]


def rows_exchange(pieces):
    return [pieces[0]] + [rows_swap(pieces[j], j) for j in (1, 2, 3)]


def reduce_far(pieces):
    _, first, second = halves(pieces[3])
    return rows_swap(first, 1), rows_swap(second, 2)


def reduce_add(pieces, from_x, from_y):
    axis, first_x, second_x = halves(pieces[1])
    _, first_y, second_y = halves(pieces[2])
    return (
        jnp.concatenate([first_x, add_low(second_x, from_y)], axis=axis),
        jnp.concatenate([add_low(first_y, from_x), second_y], axis=axis),
    )


def reduce_near(to_x, to_y):
    return rows_swap(to_x, 1), rows_swap(to_y, 2)


def reduce_first(pieces):
    return rows_swap(pieces[3][0], 1), rows_swap(pieces[3][1], 2)


def reduce_second(pieces, far):
    return (
        jnp.concatenate([pieces[1][0], add_low(pieces[1][1], far[1])], axis=0),
        jnp.concatenate([add_low(pieces[2][0], far[0]), pieces[2][1]], axis=0),
    )


def reduce_total(pieces, late):
    return add_wide([jnp.concatenate(pieces[0], axis=0), *late])


def add_wide(arrays):
    return sum(array.astype(f32) for array in arrays)


def add_low_all(array):
    return jnp.sum(array.astype(f32), axis=0).astype(bf16)


def add_low(left, right):
    return (left.astype(f32) + right.astype(f32)).astype(bf16)


def chip_shift(array, distance):
    count = lax.axis_size("cols")
    return lax.ppermute(
        array, "cols", [(i, (i + 2 * distance) % count) for i in range(count)]
    )


def core_swap(array):
    count = lax.axis_size("cols")
    return lax.ppermute(array, "cols", [(i, i ^ 1) for i in range(count)])


def chips_gather(array):
    chips = lax.axis_size("cols") // 2
    return [array] + [chip_shift(array, d) for d in range(1, chips)]


def chips_in_order(array, chip):
    chips = array.shape[0]
    twice = jnp.concatenate([array[::-1]] * 2, axis=0)
    return lax.dynamic_slice_in_dim(twice, chips - 1 - chip, chips, 0)


def cores_sum(array):
    count = lax.axis_size("cols")
    pairs = [[i, i + 1] for i in range(0, count, 2)]
    came = lax.all_to_all(array, "cols", 0, 0, axis_index_groups=pairs, tiled=True)
    return add_low(came[0], came[1])


def chips_exchange(array):
    count = lax.axis_size("cols")
    alike = [list(range(core, count, 2)) for core in range(2)]
    return lax.all_to_all(array, "cols", 0, 0, axis_index_groups=alike, tiled=True)


def cores_in_order(mine, other, core, axis):
    return jnp.stack(
        [jnp.where(core == 0, mine, other), jnp.where(core == 0, other, mine)], axis=axis
    )


def call_params(mebibytes):
    return pltpu.CompilerParams(vmem_limit_bytes=mebibytes * 1024 * 1024)


def cost(micros):
    return pl.CostEstimate(flops=int(micros * 1.15e9), bytes_accessed=0, transcendentals=0)


def turn(rows, cosine, sine):
    lane = lax.broadcasted_iota(jnp.int32, rows.shape, 1)
    partner = jnp.where(
        (lane & (HEAD_SIZE - 1)) < HEAD_SIZE // 2,
        pltpu.roll(rows, LANES - HEAD_SIZE // 2, 1),
        pltpu.roll(rows, HEAD_SIZE // 2, 1),
    )
    return rows * cosine + partner * sine


def project_kernel(meta, *refs):
    parts, found, swapped, gain, cosine, sine = refs[:4], refs[4], refs[5], *refs[6:9]
    q_out, k_out, v_out, n_out, w_out = refs[9:]
    step = pl.program_id(0)
    chips, rows, _ = found.shape
    chip = meta[1]

    @pl.when(step == 0)
    def _():
        first_core = meta[2] == 0
        for d in range(chips):
            mine, other = found[d], swapped[d]
            here = pl.multiple_of(lax.rem(chip + chips - d, chips) * (2 * rows), 2 * rows)
            w_out[pl.ds(here, 2 * rows), :] = jnp.concatenate(
                [jnp.where(first_core, mine, other), jnp.where(first_core, other, mine)], axis=0
            )

    for index, part in enumerate(parts):

        @pl.when(step == index)
        def _(part=part):
            rows = part[...].astype(f32)
            n_out[0] = (rows * rms_scale(rows) * gain[...]).astype(bf16)

    linear = dot_nn(n_out[0], w_out[...])
    q_cols, k_cols = q_out.shape[1], k_out.shape[1]
    cos_rows, sin_rows = cosine[...], sine[...]
    turned = jnp.concatenate(
        [
            turn(linear[:, at : at + LANES], cos_rows, sin_rows)
            for at in range(0, q_cols + k_cols, LANES)
        ],
        axis=1,
    ).astype(bf16)
    q_out[...] = turned[:, :q_cols]
    k_out[...] = turned[:, q_cols:]
    v_out[...] = linear[:, q_cols + k_cols :].astype(bf16)


def project(meta, parts, found, swapped, gain, cosine, sine, q_cols, k_cols):
    tok, width = parts[0].shape
    length = 4 * tok
    whole = pl.BlockSpec(memory_space=pltpu.VMEM)

    def natural(step, meta):
        return (step ^ meta[0], 0)

    return pl.pallas_call(
        project_kernel,
        grid_spec=pltpu.PrefetchScalarGridSpec(
            num_scalar_prefetch=1,
            grid=(4,),
            in_specs=[whole] * 7
            + [pl.BlockSpec((tok, LANES), natural), pl.BlockSpec((tok, LANES), natural)],
            out_specs=[
                pl.BlockSpec((tok, q_cols), natural),
                pl.BlockSpec((tok, k_cols), natural),
                pl.BlockSpec((tok, k_cols), natural),
                pl.BlockSpec((1, tok, width), lambda step, meta: (step, 0, 0)),
                pl.BlockSpec((width, q_cols + 2 * k_cols), lambda step, meta: (0, 0)),
            ],
        ),
        out_shape=[
            jax.ShapeDtypeStruct((length, q_cols), bf16),
            jax.ShapeDtypeStruct((length, k_cols), bf16),
            jax.ShapeDtypeStruct((length, k_cols), bf16),
            jax.ShapeDtypeStruct((4, tok, width), bf16),
            jax.ShapeDtypeStruct((width, q_cols + 2 * k_cols), bf16),
        ],
        compiler_params=call_params(32),
        cost_estimate=cost(10),
        name="project",
    )(meta, *parts, found, swapped, gain, cosine, sine)


def attend_kernel(meta, queries, keys, values, starts, out, lse, *, bands):
    block = pl.program_id(0)
    rows = queries.shape[0]
    first = meta[3 + block]
    heads = queries.shape[1] // HEAD_SIZE
    group = queries.shape[1] // keys.shape[1]
    for band in range(1, bands + 1):

        @pl.when(block - first + 1 == band)
        def _(band=band):
            width = band * rows
            base = pl.multiple_of(first * rows, rows)
            key_band = keys[pl.ds(base, width), :]
            value_band = values[pl.ds(base, width), :]
            query_pos = block * rows + lax.broadcasted_iota(jnp.int32, (rows, width), 0)
            key_pos = base + lax.broadcasted_iota(jnp.int32, (rows, width), 1)
            allowed = (key_pos >= starts[...]) & (key_pos <= query_pos)
            results = []
            for head in range(heads):
                at = head // group * HEAD_SIZE
                scores = dot_nt(
                    queries[:, head * HEAD_SIZE : (head + 1) * HEAD_SIZE],
                    key_band[:, at : at + HEAD_SIZE],
                )
                scores = jnp.where(allowed, scores, masked_score)
                top = jnp.max(scores, axis=1, keepdims=True)
                weights = jnp.exp2((scores - top) * (att_scale * log2_e))
                total = jnp.sum(weights, axis=1, keepdims=True)
                result = dot_nn(weights.astype(bf16), value_band[:, at : at + HEAD_SIZE])
                results.append(result * (1.0 / total))
                lse[:, head : head + 1] = top * (att_scale * log2_e) + jnp.log2(total)
            out[0] = jnp.concatenate(results, axis=1).astype(bf16)


def attend(meta, queries, keys, values, starts, tok):
    length, q_cols = queries.shape
    k_cols = keys.shape[1]
    blocks = length // tok
    whole = pl.BlockSpec(memory_space=pltpu.VMEM)
    return pl.pallas_call(
        partial(attend_kernel, bands=min(blocks, LONGEST_DOC // tok + 1)),
        grid_spec=pltpu.PrefetchScalarGridSpec(
            num_scalar_prefetch=1,
            grid=(blocks,),
            in_specs=[
                pl.BlockSpec((tok, q_cols), lambda i, meta: (i, 0)),
                whole,
                whole,
                pl.BlockSpec((tok, 1), lambda i, meta: (i, 0)),
            ],
            out_specs=[
                pl.BlockSpec((1, tok, q_cols), lambda i, meta: (i, 0, 0)),
                pl.BlockSpec((tok, 8), lambda i, meta: (i, 0)),
            ],
        ),
        out_shape=[
            jax.ShapeDtypeStruct((blocks, tok, q_cols), bf16),
            jax.ShapeDtypeStruct((length, 8), f32),
        ],
        compiler_params=call_params(32),
        cost_estimate=cost(16),
        name="attend",
    )(meta, queries, keys, values, starts)


def attend_back_kernel(
    meta, queries, grads, lse, starts, keys, values, cosine, sine, out, key_sum, value_sum, *, bands
):
    block = pl.program_id(0)
    rows = queries.shape[0]
    first = meta[3 + block]
    q_cols, k_cols = queries.shape[1], keys.shape[1]
    heads = q_cols // HEAD_SIZE
    group = q_cols // k_cols

    @pl.when(block == 0)
    def _():
        key_sum[...] = jnp.zeros_like(key_sum)
        value_sum[...] = jnp.zeros_like(value_sum)

    for band in range(1, bands + 1):

        @pl.when(block - first + 1 == band)
        def _(band=band):
            width = band * rows
            base = pl.multiple_of(first * rows, rows)
            key_band = keys[pl.ds(base, width), :]
            value_band = values[pl.ds(base, width), :]
            key_pos = base + lax.broadcasted_iota(jnp.int32, (width, rows), 0)
            query_pos = block * rows + lax.broadcasted_iota(jnp.int32, (width, rows), 1)
            allowed = (key_pos >= starts[...]) & (key_pos <= query_pos)
            query_grads, key_parts, value_parts = [], [], []
            for kv_head in range(k_cols // HEAD_SIZE):
                at = kv_head * HEAD_SIZE
                key_rows = key_band[:, at : at + HEAD_SIZE]
                value_rows = value_band[:, at : at + HEAD_SIZE]
                key_part = jnp.zeros((width, HEAD_SIZE), f32)
                value_part = jnp.zeros((width, HEAD_SIZE), f32)
                for head in range(kv_head * group, (kv_head + 1) * group):
                    query_rows = queries[:, head * HEAD_SIZE : (head + 1) * HEAD_SIZE]
                    grad_rows = grads[0, :, head * HEAD_SIZE : (head + 1) * HEAD_SIZE]
                    scores = dot_nt(key_rows, query_rows)
                    probs = jnp.where(
                        allowed,
                        jnp.exp2(scores * (att_scale * log2_e) - lse[head : head + 1, :]),
                        0.0,
                    )
                    grad_probs = dot_nt(value_rows, grad_rows)
                    delta = jnp.sum(probs * grad_probs, axis=0, keepdims=True)
                    grad_scores = (probs * (grad_probs - delta)).astype(bf16)
                    value_part += dot_nn(probs.astype(bf16), grad_rows)
                    key_part += dot_nn(grad_scores, query_rows)
                    query_grads.append(dot_tn(grad_scores, key_rows))
                key_parts.append(key_part)
                value_parts.append(value_part)
            key_sum[pl.ds(base, width), :] += jnp.concatenate(key_parts, axis=1)
            value_sum[pl.ds(base, width), :] += jnp.concatenate(value_parts, axis=1)
            here = pl.ds(pl.multiple_of(block * rows, rows), rows)
            query_grad = jnp.concatenate(query_grads, axis=1) * att_scale
            turned = [
                turn(query_grad[:, c : c + LANES], cosine[here, :], -sine[here, :])
                for c in range(0, q_cols, LANES)
            ]
            out[block ^ meta[0], :, :q_cols] = jnp.concatenate(turned, axis=1).astype(bf16)

    @pl.when(block == pl.num_programs(0) - 1)
    def _():
        for part in range(4):
            here = pl.ds(pl.multiple_of((meta[0] ^ part) * rows, rows), rows)
            key_grad = key_sum[here, :] * att_scale
            turned = [
                turn(key_grad[:, c : c + LANES], cosine[here, :], -sine[here, :])
                for c in range(0, k_cols, LANES)
            ]
            out[part, :, q_cols : q_cols + k_cols] = jnp.concatenate(turned, axis=1).astype(bf16)
            out[part, :, q_cols + k_cols :] = value_sum[here, :].astype(bf16)


def attend_back(meta, queries, grads, lse, starts, keys, values, cosine, sine, tok):
    length, q_cols = queries.shape
    k_cols = keys.shape[1]
    blocks = length // tok
    whole = pl.BlockSpec(memory_space=pltpu.VMEM)
    return pl.pallas_call(
        partial(attend_back_kernel, bands=min(blocks, LONGEST_DOC // tok + 1)),
        grid_spec=pltpu.PrefetchScalarGridSpec(
            num_scalar_prefetch=1,
            grid=(blocks,),
            in_specs=[
                pl.BlockSpec((tok, q_cols), lambda i, meta: (i, 0)),
                pl.BlockSpec((1, tok, q_cols), lambda i, meta: (i, 0, 0)),
                pl.BlockSpec((8, tok), lambda i, meta: (0, i)),
                pl.BlockSpec((1, tok), lambda i, meta: (0, i)),
                whole,
                whole,
                whole,
                whole,
            ],
            out_specs=pl.BlockSpec(
                (blocks, tok, q_cols + 2 * k_cols), lambda i, meta: (0, 0, 0)
            ),
            scratch_shapes=[
                pltpu.VMEM((length, k_cols), f32),
                pltpu.VMEM((length, k_cols), f32),
            ],
        ),
        out_shape=jax.ShapeDtypeStruct((blocks, tok, q_cols + 2 * k_cols), bf16),
        compiler_params=call_params(40),
        cost_estimate=cost(29),
        name="attend_back",
    )(meta, queries, grads, lse, starts, keys, values, cosine, sine)


def low_pair(values):
    high = values.astype(bf16)
    return high, (values - high.astype(f32)).astype(bf16)


def mix_kernel(
    meta, heads, out_parts, tokens, member, gain, router, mixed_out, rows_out, gates_out, *, experts
):
    width = tokens.shape[1]
    branch = sum(dot_nn(heads[meta[0] ^ part], out_parts[part]) for part in range(4))
    mixed = tokens[...].astype(f32) + res_scale * branch
    mixed_out[...] = mixed
    normed = (mixed * rms_scale(mixed) * gain[...]).astype(bf16)
    logits = dot_nn(normed, router[...])
    named = member[...] > 0
    logits = jnp.where(named, logits, masked_score)
    lifted = jnp.exp(logits - jnp.max(logits, axis=1, keepdims=True))
    lifted = jnp.where(named, lifted, 0.0)
    gates = lifted * (1.0 / jnp.sum(lifted, axis=1, keepdims=True))
    gates_out[...] = gates
    high, low = low_pair(gates)
    low = pltpu.roll(low.astype(f32), experts, 1)
    rows_out[:, :width] = normed
    rows_out[:, width:] = (high.astype(f32) + low).astype(bf16)


def mix(meta, heads, out_parts, tokens, member, gain, router, experts):
    tok, width = tokens.shape
    whole = pl.BlockSpec(memory_space=pltpu.VMEM)
    return pl.pallas_call(
        partial(mix_kernel, experts=experts),
        in_specs=[pl.BlockSpec(memory_space=pltpu.SMEM)] + [whole] * 6,
        out_specs=[whole] * 3,
        out_shape=[
            jax.ShapeDtypeStruct((tok, width), f32),
            jax.ShapeDtypeStruct((tok, width + LANES), bf16),
            jax.ShapeDtypeStruct((tok, LANES), f32),
        ],
        compiler_params=call_params(40),
        cost_estimate=cost(6),
        name="mix",
    )(meta, heads, out_parts, tokens, member, gain, router)


def unmix_kernel(
    meta, came, last, mixed_in, cotangent, gates, gain, router, out_parts, heads,
    mixed_grad, heads_out, mine_out, other_out, *, experts
):
    width = cotangent.shape[1]
    summed = came[...].astype(f32) + last[...].astype(f32)
    beside = summed[:, width:]
    lane = lax.broadcasted_iota(jnp.int32, beside.shape, 1)
    weighted = jnp.where(lane < experts, beside + pltpu.roll(beside, LANES - experts, 1), 0.0)
    logit_grads = weighted - gates[...] * jnp.sum(weighted, axis=1, keepdims=True)
    high, low = low_pair(logit_grads)
    normed_grad = summed[:, :width] + dot_nt(high, router[...]) + dot_nt(low, router[...])
    mixed = mixed_in[...]
    scale = rms_scale(mixed)
    unit = mixed * scale
    normed = (unit * gain[...]).astype(bf16)
    one_lane = lax.broadcasted_iota(jnp.int32, (unit.shape[0], LANES), 1) == experts
    one_lane = one_lane.astype(f32).astype(bf16)
    gain_high, gain_low = low_pair(normed_grad * unit)
    shares = dot_tn(normed, high) + dot_tn(normed, low)
    shares = (shares + dot_tn(gain_high, one_lane) + dot_tn(gain_low, one_lane)).astype(bf16)
    unit_grad = normed_grad * gain[...]
    grad = cotangent[...].astype(f32) + scale * (
        unit_grad - unit * jnp.mean(unit_grad * unit, axis=-1, keepdims=True)
    )
    mixed_grad[...] = grad
    branch = (res_scale * grad).astype(bf16)
    for part in range(4):
        heads_out[meta[0] ^ part] = dot_nt(branch, out_parts[part]).astype(bf16)
    first_core = meta[2] == 0
    _, chips, sixth, _ = mine_out.shape
    tok = branch.shape[0]
    for part in range(4):
        wide = dot_tn(heads[part], branch).astype(bf16)
        wide = jnp.concatenate([wide, shares[part * tok : (part + 1) * tok]], axis=1)
        for chip in range(chips):
            at = 2 * chip * sixth
            even, odd = wide[at : at + sixth], wide[at + sixth : at + 2 * sixth]
            mine_out[part, chip] = jnp.where(first_core, even, odd)
            other_out[part, chip] = jnp.where(first_core, odd, even)


def unmix(meta, came, last, mixed, cotangent, gates, gain, router, out_parts, heads, experts, chips):
    tok, width = mixed.shape
    wide = (4, chips, tok // (2 * chips), width + LANES)
    whole = pl.BlockSpec(memory_space=pltpu.VMEM)
    return pl.pallas_call(
        partial(unmix_kernel, experts=experts),
        in_specs=[pl.BlockSpec(memory_space=pltpu.SMEM)] + [whole] * 9,
        out_specs=[whole] * 4,
        out_shape=[
            jax.ShapeDtypeStruct((tok, width), f32),
            jax.ShapeDtypeStruct((4, tok, out_parts.shape[1]), bf16),
            jax.ShapeDtypeStruct(wide, bf16),
            jax.ShapeDtypeStruct(wide, bf16),
        ],
        compiler_params=call_params(32),
        cost_estimate=cost(12),
        name="unmix",
    )(meta, came, last, mixed, cotangent, gates, gain, router, out_parts, heads)


def hidden_weights(parts, cut, ffe):
    tiles = 2 * ffe // LANES
    return jnp.concatenate(
        [
            jnp.concatenate([ref[0, t * cut : (t + 1) * cut, :] for t in range(tiles)], axis=1)
            for ref in parts
        ],
        axis=0,
    )


def down_weights(parts, cut, ffe):
    first = 2 * ffe // LANES * cut
    return jnp.concatenate(
        [
            ref[0, first + t * ffe : first + (t + 1) * ffe, :]
            for ref in parts
            for t in range(cut // LANES)
        ],
        axis=1,
    )


def experts_kernel(meta, *refs, experts, slots, local, final, earlier):
    blocks = 4
    x_refs, g_refs, refs = refs[:blocks], refs[blocks : 2 * blocks], refs[2 * blocks :]
    early, refs = refs[:earlier], refs[earlier:]
    parts, refs = refs[:4], refs[4:]
    returned_out, refs = refs[: blocks * final], refs[blocks * final :]
    x_out, g_out, active_out, grads_out, out_kept, dx_kept, t_kept, refs = *refs[:7], refs[7:]
    x_rows, g_rows, gate_kept, rows_sent, x_here, g_here, arrived, refs = *refs[:7], refs[7:]
    own = pl.program_id(0)
    own_count = x_rows.shape[0]
    tok = x_refs[0].shape[0]
    width = x_rows.shape[2]
    cut = width // 4
    ffe = active_out.shape[2]
    row, first_expert = meta[0], meta[1]
    loads = [
        (
            pltpu.make_async_copy(x_refs[block], x_here.at[block % 2], arrived.at[0, block % 2]),
            pltpu.make_async_copy(g_refs[block], g_here.at[block % 2], arrived.at[1, block % 2]),
        )
        for block in range(blocks)
    ]
    if final:
        ranks_kept, returned, sent, refs = *refs[:3], refs[3:]
    fetches = [
        [
            pltpu.make_async_copy(
                early[which].at[:, pl.ds(block * slots, slots), :],
                refs[which].at[block % 2],
                refs[3].at[which, block % 2],
            )
            for which in range(earlier)
        ]
        for block in range(blocks)
    ]
    row_copies = [
        pltpu.make_async_copy(x_rows, x_out, rows_sent.at[0]),
        pltpu.make_async_copy(g_rows, g_out, rows_sent.at[1]),
    ]

    def columns(part, start=0):
        return pl.ds(pl.multiple_of(start + (row ^ part) * cut, LANES), cut)

    @pl.when(own == 0)
    def _():
        for load in loads[0]:
            load.start()
        slot = lax.broadcasted_iota(jnp.int32, (slots, tok), 0).astype(f32)
        lower = (
            lax.broadcasted_iota(jnp.int32, (tok, tok), 0)
            > lax.broadcasted_iota(jnp.int32, (tok, tok), 1)
        ).astype(f32).astype(bf16)
        source = lax.broadcasted_iota(jnp.int32, (LANES, LANES), 1)
        target = lax.broadcasted_iota(jnp.int32, (LANES, LANES), 0)
        choose = (source == target + first_expert).astype(f32).astype(bf16)
        for block in range(blocks):
            for load in loads[block + 1] if block + 1 < blocks else ():
                load.start()
            for load in loads[block]:
                load.wait()
            x_block, g_block = x_here.at[block % 2], g_here.at[block % 2]
            member = g_block[:, width:]
            rank = jnp.where(member > 0, dot_nn(lower, member), -1.0).astype(bf16)
            if final:
                ranks_kept[block] = dot_nt(rank, choose)
            rank_rows = dot_nt(choose, rank)
            pick = jnp.concatenate(
                [
                    (rank_rows[index : index + 1, :] == slot).astype(f32).astype(bf16)
                    for index in range(local, local + own_count)
                ],
                axis=0,
            )
            beside = dot_nn(pick, x_block[:, width:])
            lane = lax.broadcasted_iota(jnp.int32, beside.shape, 1)
            named = lax.broadcasted_iota(jnp.int32, beside.shape, 0) // slots
            named = named + first_expert + local
            gates = jnp.sum(
                jnp.where((lane == named) | (lane == named + experts), beside, 0.0),
                axis=1,
                keepdims=True,
            )
            here = slice(block * slots, (block + 1) * slots)
            x_part = dot_nn(pick, x_block[:, :width]).astype(bf16)
            g_part = dot_nn(pick, g_block[:, :width]).astype(bf16)
            for index in range(own_count):
                rows = slice(index * slots, (index + 1) * slots)
                gate_kept[index, here, :] = gates[rows]
                for part in range(4):
                    there = slice(part * cut, (part + 1) * cut)
                    x_rows[index, here, columns(part)] = x_part[rows, there]
                    g_rows[index, here, columns(part)] = g_part[rows, there]
        for copy in row_copies:
            copy.start()

    @pl.when(own == own_count - 1)
    def _():
        for fetch in fetches[0] + fetches[1]:
            fetch.start()

    hidden_w = hidden_weights(parts, cut, ffe)
    down_w = down_weights(parts, cut, ffe)
    hidden = dot_nn(x_rows[own], hidden_w)
    hidden_gate, hidden_up = hidden[:, :ffe], hidden[:, ffe:]
    gates = gate_kept[own]
    grad_active = dot_nt(g_rows[own], down_w) * (res_scale * gates)
    sigmoid = jax.nn.sigmoid(hidden_gate)
    silu = hidden_gate * sigmoid
    active = silu * hidden_up
    gated = (active * gates).astype(bf16)
    grad_gate = grad_active * hidden_up * (sigmoid * (1.0 + hidden_gate * (1.0 - sigmoid)))
    grads = jnp.concatenate(
        [grad_gate.astype(bf16), (grad_active * silu).astype(bf16)], axis=1
    )
    weighted = jnp.sum(active * grad_active, axis=1, keepdims=True)
    active_out[0] = gated
    grads_out[0] = grads
    kept = own if final else 0
    out_kept[kept] = dot_nn(gated, down_w).astype(bf16)
    dx_kept[kept] = dot_nt(grads, hidden_w).astype(bf16)
    weighted_high = weighted.astype(bf16).astype(f32)
    lane = lax.broadcasted_iota(jnp.int32, (blocks * slots, LANES), 1)
    named = first_expert + local + own
    t_kept[kept] = jnp.where(
        lane == named,
        weighted_high,
        jnp.where(lane == named + experts, weighted - weighted_high, 0.0),
    ).astype(bf16)

    @pl.when(own == own_count - 1)
    def _():
        if final:
            slot = lax.broadcasted_iota(jnp.int32, (tok, slots), 1).astype(f32)
            gives = [
                pltpu.make_async_copy(
                    returned.at[block % 2], returned_out[block], sent.at[block]
                )
                for block in range(blocks)
            ]
            for block in range(blocks):
                here = slice(block * slots, (block + 1) * slots)
                put = jnp.concatenate(
                    [
                        (ranks_kept[block, :, index : index + 1] == slot).astype(f32).astype(bf16)
                        for index in range(local + own_count)
                    ],
                    axis=1,
                )

                def rows_of(which, here=here, block=block):
                    kept_rows = (out_kept, dx_kept, t_kept)[which]
                    found = [refs[which][block % 2, index] for index in range(local)]
                    found += [kept_rows[index, here, :] for index in range(own_count)]
                    return jnp.concatenate(found, axis=0)

                for fetch in fetches[block]:
                    fetch.wait()
                if block >= 2:
                    gives[block - 2].wait()
                out = dot_nn(put, rows_of(0)).astype(bf16)
                dx = dot_nn(put, rows_of(1)).astype(bf16)
                for part in range(4):
                    there = slice(part * cut, (part + 1) * cut)
                    returned[block % 2, :, columns(part)] = out[:, there]
                    returned[block % 2, :, columns(part, width)] = dx[:, there]
                returned[block % 2, :, 2 * width :] = dot_nn(put, rows_of(2)).astype(bf16)
                gives[block].start()
                for fetch in fetches[block + 2] if block + 2 < blocks else ():
                    fetch.start()
            for give in gives[-2:]:
                give.wait()
        for copy in row_copies:
            copy.wait()


def run_experts(meta, x_blocks, g_blocks, early, parts, ffe, experts, slots, local, final):
    blocks = len(x_blocks)
    tok, padded = x_blocks[0].shape
    width = padded - LANES
    own, packed, _ = parts[0].shape
    rows = blocks * slots
    anywhere = pl.BlockSpec(memory_space=pl.ANY)
    back = 2 * width + LANES
    kept_shapes = [(own, rows, width), (own, rows, width), (own, rows, LANES)]
    row_shapes = [(own, rows, width), (own, rows, width), (own, rows, ffe), (own, rows, 2 * ffe)]

    def one(*shape):
        return pl.BlockSpec((1,) + shape, lambda e, meta: (e, 0, 0))

    out_specs = [anywhere] * 2 + [one(rows, ffe), one(rows, 2 * ffe)]
    out_shapes = [jax.ShapeDtypeStruct(shape, bf16) for shape in row_shapes]
    scratch = []
    if final:
        out_specs = [anywhere] * blocks + out_specs
        out_shapes = [jax.ShapeDtypeStruct((tok, back), bf16)] * blocks + out_shapes
        scratch += [pltpu.VMEM(shape, bf16) for shape in kept_shapes]
    else:
        out_specs += [one(*shape[1:]) for shape in kept_shapes]
        out_shapes += [jax.ShapeDtypeStruct(shape, bf16) for shape in kept_shapes]
    scratch += [
        pltpu.VMEM((own, rows, width), bf16),
        pltpu.VMEM((own, rows, width), bf16),
        pltpu.VMEM((own, rows, 1), f32),
        pltpu.SemaphoreType.DMA((2,)),
        pltpu.VMEM((2, tok, padded), bf16),
        pltpu.VMEM((2, tok, padded), bf16),
        pltpu.SemaphoreType.DMA((2, 2)),
    ]
    if final:
        scratch += [
            pltpu.VMEM((blocks, tok, LANES), f32),
            pltpu.VMEM((2, tok, back), bf16),
            pltpu.SemaphoreType.DMA((blocks,)),
        ]
    if early:
        scratch += [
            pltpu.VMEM((2, array.shape[0], slots, array.shape[2]), bf16) for array in early
        ] + [pltpu.SemaphoreType.DMA((3, 2))]
    return pl.pallas_call(
        partial(
            experts_kernel,
            experts=experts,
            slots=slots,
            local=local,
            final=final,
            earlier=len(early),
        ),
        grid_spec=pltpu.PrefetchScalarGridSpec(
            num_scalar_prefetch=1,
            grid=(own,),
            in_specs=[anywhere] * (2 * blocks + len(early)) + [one(packed, LANES)] * 4,
            out_specs=out_specs,
            scratch_shapes=scratch,
        ),
        out_shape=out_shapes,
        compiler_params=call_params(60),
        cost_estimate=cost(26),
        name="experts",
    )(meta, *x_blocks, *g_blocks, *early, *parts)


def weight_grad_kernel(*refs, chunks, own_count):
    x_refs, grad_refs, active_refs, g_refs = (
        refs[chunks * index : chunks * (index + 1)] for index in range(4)
    )
    refs = refs[4 * chunks :]
    outs, (made, sent) = refs[: 4 * own_count], refs[4 * own_count :]
    x_rows = jnp.concatenate([ref[0] for ref in x_refs], axis=0)
    grads = jnp.concatenate([ref[0] for ref in grad_refs], axis=0)
    active = jnp.concatenate([ref[0] for ref in active_refs], axis=0)
    g_rows = jnp.concatenate([ref[0] for ref in g_refs], axis=0)
    cut = x_rows.shape[1] // 4
    ffe = grads.shape[1] // 2
    first = 2 * ffe // LANES * cut
    own = pl.program_id(0)
    for part in range(4):
        hidden = dot_tn(x_rows[:, part * cut : (part + 1) * cut], grads).astype(bf16)
        for t in range(2 * ffe // LANES):
            made[own, part, t * cut : (t + 1) * cut, :] = hidden[:, t * LANES : (t + 1) * LANES]
    down = (dot_tn(active, g_rows) * res_scale).astype(bf16)
    for part in range(4):
        for t in range(cut // LANES):
            at = part * cut + t * LANES
            here = slice(first + t * ffe, first + (t + 1) * ffe)
            made[own, part, here, :] = down[:, at : at + LANES]
    copies = [
        [
            pltpu.make_async_copy(
                made.at[expert, part], outs[part * own_count + expert].at[0], sent.at[expert, part]
            )
            for part in range(4)
        ]
        for expert in range(own_count)
    ]
    for expert in range(own_count):

        @pl.when(own == expert)
        def _(expert=expert):
            for copy in copies[expert]:
                copy.start()

    @pl.when(own == own_count - 1)
    def _():
        for group in copies:
            for copy in group:
                copy.wait()


def weight_grads(x_chunks, grad_chunks, active_chunks, g_chunks):
    own, rows, width = x_chunks[0].shape
    ffe = active_chunks[0].shape[2]
    chunks = len(x_chunks)
    packed = 3 * ffe * (width // 4) // LANES

    def one(*shape):
        return pl.BlockSpec((1,) + shape, lambda e: (e, 0, 0))

    outs = pl.pallas_call(
        partial(weight_grad_kernel, chunks=chunks, own_count=own),
        grid=(own,),
        in_specs=[one(rows, width)] * chunks
        + [one(rows, 2 * ffe)] * chunks
        + [one(rows, ffe)] * chunks
        + [one(rows, width)] * chunks,
        out_specs=[pl.BlockSpec(memory_space=pl.ANY)] * (4 * own),
        out_shape=[jax.ShapeDtypeStruct((1, packed, LANES), bf16)] * (4 * own),
        scratch_shapes=[
            pltpu.VMEM((own, 4, packed, LANES), bf16),
            pltpu.SemaphoreType.DMA((own, 4)),
        ],
        compiler_params=call_params(60),
        cost_estimate=cost(13),
        name="weight_grads",
    )(*x_chunks, *grad_chunks, *active_chunks, *g_chunks)
    return [list(outs[part * own : (part + 1) * own]) for part in range(4)]


def two_halves(arrays):
    return arrays if len(arrays) == 2 else list(halves(arrays[0])[1:])


def join_halves(array, own):
    return array.reshape(own, 2 * array.shape[1] // own, array.shape[2])


def pack_weights(gate, up, down):
    return jnp.concatenate(
        [
            lax.slice_in_dim(array, at, at + LANES, axis=2)
            for array in (gate, up, down)
            for at in range(0, array.shape[2], LANES)
        ],
        axis=1,
    )


def unpack_weights(packed, cut, ffe):
    tiles = ffe // LANES

    def beside(first, rows, count):
        return jnp.concatenate(
            [packed[:, first + t * rows : first + (t + 1) * rows, :] for t in range(count)], axis=2
        )

    return (
        beside(0, cut, tiles),
        beside(tiles * cut, cut, tiles),
        beside(2 * tiles * cut, ffe, cut // LANES),
    )


def after(array, *earlier):
    return lax.optimization_barrier((array, earlier))[0]


def per_device(
    tokens,
    segment_ids,
    expert_ids,
    w_query,
    key_matrix,
    value_matrix,
    w_out,
    norm_attn,
    norm_moe,
    w_router,
    w_gate,
    w_up,
    w_down,
    cotangent,
):
    row = lax.axis_index("rows")
    column = lax.axis_index("cols")
    columns = lax.axis_size("cols")
    chips = columns // 2
    chip, core = column // 2, column % 2
    own_tokens = tokens[0]
    tok, width = own_tokens.shape
    own_experts = w_gate.shape[0]
    experts = own_experts * columns
    top_count = expert_ids.shape[2]
    capacity = 5 * tok * top_count // (4 * experts)
    slots = -(-capacity // LANES) * LANES
    q_cols, k_cols = w_query.shape[1], key_matrix.shape[1]

    token_near = gather_near(own_tokens)
    qkv_cols = q_cols + 2 * k_cols
    sixth = w_out.shape[0]
    found = chips_gather(
        jnp.concatenate(
            [w_query, key_matrix, value_matrix, w_out.reshape(4 * sixth, width // 4)], axis=1
        )
    )
    small = jnp.concatenate(
        [
            w_router,
            norm_attn[:, None],
            norm_moe[:, None],
            jnp.zeros((w_router.shape[0], LANES - experts - 2), bf16),
        ],
        axis=1,
    )
    small_full = lax.all_to_all(
        jnp.tile(small, (4 * columns, 1)), ("rows", "cols"), 0, 0, tiled=True
    )
    gain_attn = small_full[:, experts].astype(f32)[None, :]
    gain_moe = small_full[:, experts + 1].astype(f32)[None, :]
    router_full = jnp.where(jnp.arange(LANES) < experts, small_full, 0)
    token_parts = gather_far(own_tokens, *token_near)
    found = after(found, token_near)
    project_found = jnp.stack([rows[:, :qkv_cols] for rows in found])
    project_swapped = core_swap(project_found)

    out_half = jnp.stack([rows[:, qkv_cols:].reshape(sixth, width) for rows in found])
    out_half = chips_in_order(out_half, chip).reshape(chips * sixth, width)
    out_near = gather_near(after(out_half, token_parts[3]))

    expert_rows = expert_ids[0]
    lane_range = jnp.arange(LANES, dtype=jnp.int32)
    member = jnp.any(expert_rows[:, :, None] == lane_range[None, None, :], axis=1).astype(bf16)
    cot_rows = jnp.concatenate([cotangent[0], member], axis=1)
    cot_same = [cot_rows, chip_shift(after(cot_rows, found[1:], token_parts[3]), 1)]

    groups = 2 if own_experts % 2 == 0 else 1
    group_size = own_experts // groups
    packed = []
    for group in range(groups):
        here = slice(group * group_size, (group + 1) * group_size)
        packed.append(pack_weights(after(w_gate[here], own_tokens), w_up[here], w_down[here]))
    weight_near = [gather_near(after(packed[0], token_parts[3], project_swapped, out_half))]

    segments = segment_ids[0]
    length = segments.shape[0]
    starts = jnp.sum((segments[None, :] < segments[:, None]).astype(jnp.int32), axis=1)
    positions = (jnp.arange(length, dtype=jnp.int32) - starts).astype(f32)
    half = HEAD_SIZE // 2
    frequency = rope_base ** (-(2.0 * jnp.arange(half, dtype=f32)) / HEAD_SIZE)
    angles = positions[:, None] * frequency[None, :]
    cos_half, sin_half = jnp.cos(angles), jnp.sin(angles)
    cosine = jnp.concatenate([cos_half] * 4, axis=1)
    sine = jnp.concatenate([-sin_half, sin_half] * 2, axis=1)
    first_blocks = starts[::tok] // tok
    place = jnp.stack([row, chip, core])
    meta = jnp.concatenate([place.astype(jnp.int32), first_blocks.astype(jnp.int32)])

    queries, key_rows, value_rows, normed, project_w = project(
        meta, token_parts, project_found, project_swapped, gain_attn, cosine, sine, q_cols, k_cols
    )
    attended, lse = attend(meta, queries, key_rows, value_rows, starts[:, None], tok)
    cot_same[1], out_near = after((cot_same[1], out_near), attended)
    cot_other = [core_swap(rows) for rows in cot_same]
    for d in range(2, chips):
        cot_same.append(chip_shift(cot_same[-1], 1))
    attended, out_near = after((attended, out_near), weight_near[0], cot_same[2], cot_other)
    own_heads = lax.all_to_all(attended, "rows", 0, 0, tiled=True)
    out_mine = jnp.stack(gather_far(out_half, *out_near)).reshape(4, chips, sixth, width)
    out_parts = cores_in_order(out_mine, core_swap(out_mine), core, 2).reshape(4, tok, width)
    weight_near[0] = after(weight_near[0], own_heads)
    weight_parts = [gather_far(packed[0], *weight_near[0])]
    mixed_rows, moe_rows, gates = mix(
        meta,
        own_heads,
        out_parts,
        own_tokens,
        member,
        gain_moe,
        router_full,
        experts,
    )
    for group in range(1, groups):
        weight_near.append(gather_near(after(packed[group], weight_parts[0][3], moe_rows)))
    moe_same = [moe_rows, chip_shift(after(moe_rows, cot_same[3]), 1)]
    moe_other = [core_swap(rows) for rows in moe_same]
    moe_same.append(chip_shift(moe_same[1], 1))
    cot_other += [core_swap(rows) for rows in cot_same[2:]]

    moe_meta = jnp.stack([row, column * own_experts]).astype(jnp.int32)
    ffe = w_down.shape[1]
    kept = [[] for _ in range(groups)]
    pieces = [None] * chips
    grads = []

    def piece(d, start, stop):
        return add_low(pieces[d][0][:, start:stop], pieces[d][1][:, start:stop])

    both = 2 * width + LANES
    pairs = [(d, d + 1) for d in range(0, chips, 2)]
    early = [[] for _ in pairs]
    held = ()
    far, late, sums = [], [], []

    def make_grads(group, first_rows):
        chunks = kept[group]
        parts = weight_grads(
            [first_rows] + [k[0] for k in chunks[1:]],
            [k[3] for k in chunks],
            [k[2] for k in chunks],
            [k[1] for k in chunks],
        )
        grads.append([two_halves(part) for part in parts])

    for index, pair in enumerate(pairs):
        for group in range(groups):
            final = group == groups - 1
            if final and index == len(pairs) - 1 and groups > 1:
                make_grads(0, kept[0][0][0])
                far.append(reduce_first(grads[0]))
                held = grads[0]
            result = list(
                run_experts(
                    after(moe_meta, held),
                    [rows for d in pair for rows in (moe_same[d], moe_other[d])],
                    [rows for d in pair for rows in (cot_same[d], cot_other[d])],
                    early[index],
                    weight_parts[group],
                    ffe,
                    experts,
                    slots,
                    group * group_size,
                    final,
                )
            )
            held = result[0]
            if len(moe_other) == 2:
                moe_same[2] = after(moe_same[2], held)
                held = (held, moe_same[2])
                for d in range(3, chips):
                    moe_same.append(chip_shift(moe_same[-1], 1))
                moe_other += [core_swap(rows) for rows in moe_same[2:]]
                for later in range(1, groups):
                    weight_near[later] = after(weight_near[later], held)
                    weight_parts.append(gather_far(packed[later], *weight_near[later]))
            if not final:
                kept[group].append(result[:4])
                early[index] = result[4:]
                continue
            if index == 0:
                result = after(result, moe_same[3])
            if index == len(pairs) - 1:
                result = after(result, dx_hop, far if groups > 1 else ())
            kept[group].append(result[4:8])
            for place, d in enumerate(pair):
                pieces[d] = (result[2 * place], core_swap(result[2 * place + 1]))
            if index == 0:
                dx_ring = piece(1, width, both)
                held = dx_ring
                dx_hop = chip_shift(dx_ring, 1)
                continue
            for d in pair:
                came = dx_hop if d == 2 else chip_shift(dx_ring, 1)
                if d == chips - 1:
                    came = after(came, grads[-1])
                    far.append(reduce_first(after(grads[-1], came)))
                dx_ring = add_low(came, last_pieces[0] if d == chips - 1 else piece(d, width, both))
                if d != chips - 2:
                    continue
                last_pieces = [piece(chips - 1, width, both), piece(0, width, both)]
                if groups > 1:
                    sums.append(reduce_second(grads[0], after(far[0], dx_ring)))
                    late.append([rows_swap(*sent) for sent in zip(sums[0], (1, 2))])
                make_grads(group, after(kept[group][0][0], dx_ring, sums, last_pieces))
    for d in range(chips):
        pieces[d] = after(pieces[d], dx_ring)
    outs = [piece(d, 0, width) for d in range(chips - 1)]
    outs.append(piece(chips - 1, 0, width))
    dx_came = after(chip_shift(dx_ring, 1), outs)
    out_hop = chip_shift(after(outs[1], dx_came), 1)

    grad_mixed, grad_heads, wide_mine, wide_other = unmix(
        after(meta, late[:1]),
        dx_came,
        last_pieces[1],
        mixed_rows,
        cotangent[0],
        gates,
        gain_moe,
        router_full,
        out_parts,
        own_heads,
        experts,
        chips,
    )
    grad_attended = lax.all_to_all(grad_heads, "rows", 0, 0, tiled=True)

    wide_chip = add_low(wide_mine, core_swap(after(wide_other, far[-1])))
    wide_came = lax.all_to_all(wide_chip, "rows", 0, 0, tiled=True)

    grad_lin = attend_back(
        after(meta, wide_chip),
        queries,
        grad_attended,
        lse.T,
        starts[None, :],
        key_rows,
        value_rows,
        cosine,
        sine,
        tok,
    )
    grad_lin = after(grad_lin, late[:1], wide_came)
    normed_parts = [None] * 4
    for j in (3, 1, 2, 0):
        normed_parts[j] = dot_nt(grad_lin[j], project_w).astype(bf16)
    normed_sums = reduce_add(normed_parts, *reduce_far(normed_parts))
    normed_near = reduce_near(*normed_sums)
    sums.append(reduce_second(grads[-1], after(far[-1], *normed_sums)))
    late.append([rows_swap(*sent) for sent in zip(sums[-1], (1, 2))])
    grad_project = dot_tn(
        after(normed, *normed_parts).reshape(length, width), grad_lin.reshape(length, qkv_cols)
    )
    project_pairs = after(grad_project.astype(bf16), *normed_sums)
    project_pairs = project_pairs.reshape(chips, 2, width // columns, qkv_cols)
    project_chip = cores_sum(project_pairs.transpose(1, 0, 2, 3))
    project_came = chips_exchange(project_chip)
    project_sum = jnp.sum(after(project_came, late[-1]).astype(f32), axis=0)
    grad_normed = add_wide([normed_parts[0], *after(normed_near, project_sum)])
    wide_row = add_low_all(after(wide_came, project_came))
    wide_sum = jnp.sum(chips_exchange(wide_row).astype(f32), axis=0)
    grad_out_w = wide_sum[:, :width]
    grad_router_w = wide_sum[:, width : width + experts]
    grad_gain_moe_w = wide_sum[:, width + experts]

    out_ring = add_low(after(out_hop, grad_lin), outs[2])
    for d in range(3, chips):
        out_ring = add_low(after(chip_shift(out_ring, 1), *normed_sums), outs[d])
    moe_out = add_wide([after(chip_shift(out_ring, 1), project_chip), outs[0]])
    block_out = mixed_rows + res_scale * moe_out

    totals = []
    for parts, came in zip(grads, late):
        total = reduce_total([after(parts[0], *normed_sums, project_chip)], came)
        totals.append(unpack_weights(join_halves(total, group_size), width // 4, ffe))
    grad_gate_w, grad_up_w, grad_down_w = (
        jnp.concatenate(arrays, axis=0) for arrays in zip(*totals)
    )

    own_w = jnp.concatenate([w_query, key_matrix, value_matrix], axis=1).astype(f32)
    own_gain = lax.dynamic_slice_in_dim(gain_attn[0], column * own_w.shape[0], own_w.shape[0], 0)
    gain_rows = (jnp.sum(project_sum * own_w, axis=1) / own_gain).reshape(4, -1)
    gain_sum = jnp.sum(lax.all_to_all(gain_rows, "rows", 0, 0, tiled=True), axis=0)
    grad_gain_attn = lax.ppermute(
        gain_sum,
        ("rows", "cols"),
        [(r * columns + c, 4 * c + r) for r in range(4) for c in range(columns)],
    )

    own_float = own_tokens.astype(f32)
    scale_attn = rms_scale(own_float)
    unit_attn = own_float * scale_attn
    grad_unit = grad_normed * gain_attn
    grad_tokens = grad_mixed + scale_attn * (
        grad_unit - unit_attn * jnp.mean(grad_unit * unit_attn, axis=-1, keepdims=True)
    )
    return (
        block_out[None],
        grad_tokens[None],
        project_sum[:, :q_cols],
        project_sum[:, q_cols : q_cols + k_cols],
        project_sum[:, q_cols + k_cols :],
        grad_out_w,
        grad_gain_attn,
        grad_gain_moe_w,
        grad_router_w,
        grad_gate_w,
        grad_up_w,
        grad_down_w,
    )


def solution(mesh):
    placed = (
        P("cols", "rows", None),
        P("cols", None),
        P("cols", "rows", None),
        P("cols", "rows"),
        P("cols", "rows"),
        P("cols", "rows"),
        P(("rows", "cols"), None),
        P(("rows", "cols")),
        P(("rows", "cols")),
        P(("rows", "cols"), None),
        P("cols", "rows", None),
        P("cols", "rows", None),
        P("cols", None, "rows"),
        P("cols", "rows", None),
    )
    return jax.shard_map(
        per_device,
        mesh=mesh,
        in_specs=placed,
        out_specs=(
            P("cols", "rows", None),
            P("cols", "rows", None),
            P("cols", "rows"),
            P("cols", "rows"),
            P("cols", "rows"),
            P(("rows", "cols"), None),
            P(("rows", "cols")),
            P(("rows", "cols")),
            P(("rows", "cols"), None),
            P("cols", "rows", None),
            P("cols", "rows", None),
            P("cols", None, "rows"),
        ),
        check_vma=False,
    )
```

```python
from functools import partial

import jax
import jax.numpy as jnp
from jax import lax
from jax.experimental import pallas as pl
from jax.experimental.pallas import tpu as pltpu
from jax.sharding import PartitionSpec as P

HEAD_SIZE = 64
LANES = 128
LONGEST_DOC = 768

res_scale = 0.22
att_scale = 0.015625
norm_eps = 1e-06
rope_base = 10000.0
masked_score = -1e30
log2_e = 1.4426950408889634
highest = lax.Precision.HIGHEST
bf16 = jnp.bfloat16
f32 = jnp.float32


def rms_scale(hidden_rows):
    return lax.rsqrt(jnp.mean(hidden_rows * hidden_rows, axis=-1, keepdims=True) + norm_eps)


def dot_nt(left, right):
    return lax.dot_general(left, right, (((1,), (1,)), ((), ())), preferred_element_type=f32)


def dot_tn(left, right):
    return lax.dot_general(left, right, (((0,), (0,)), ((), ())), preferred_element_type=f32)


def dot_nn(left, right):
    return jnp.dot(left, right, preferred_element_type=f32)


def rows_swap(array, distance):
    return lax.ppermute(array, "rows", [(i, i ^ distance) for i in range(4)])


def halves(array):
    axis = 0 if array.shape[0] % 2 == 0 else 1
    cut = array.shape[axis] // 2
    return (
        axis,
        lax.slice_in_dim(array, 0, cut, axis=axis),
        lax.slice_in_dim(array, cut, 2 * cut, axis=axis),
    )


def gather_near(array):
    return rows_swap(array, 1), rows_swap(array, 2)


def far_halves(from_x, from_y):
    _, first_y, _ = halves(from_y)
    _, _, second_x = halves(from_x)
    return rows_swap(first_y, 1), rows_swap(second_x, 2)


def join_far(array, from_x, from_y, far):
    return [array, from_x, from_y, jnp.concatenate(far, axis=halves(array)[0])]


def gather_far(array, from_x, from_y):
    return join_far(array, from_x, from_y, far_halves(from_x, from_y))


def rows_exchange(pieces):
    return [pieces[0]] + [rows_swap(pieces[j], j) for j in (1, 2, 3)]


def reduce_far(pieces):
    _, first, second = halves(pieces[3])
    return rows_swap(first, 1), rows_swap(second, 2)


def reduce_add(pieces, from_x, from_y):
    axis, first_x, second_x = halves(pieces[1])
    _, first_y, second_y = halves(pieces[2])
    return (
        jnp.concatenate([first_x, add_low(second_x, from_y)], axis=axis),
        jnp.concatenate([add_low(first_y, from_x), second_y], axis=axis),
    )


def reduce_near(to_x, to_y):
    return rows_swap(to_x, 1), rows_swap(to_y, 2)


def reduce_first(pieces):
    return rows_swap(pieces[3][0], 1), rows_swap(pieces[3][1], 2)


def reduce_second(pieces, far):
    return (
        jnp.concatenate([pieces[1][0], add_low(pieces[1][1], far[1])], axis=0),
        jnp.concatenate([add_low(pieces[2][0], far[0]), pieces[2][1]], axis=0),
    )


def reduce_total(pieces, late):
    return add_wide([jnp.concatenate(pieces[0], axis=0), *late])


def add_wide(arrays):
    return sum(array.astype(f32) for array in arrays)


def add_low_all(array):
    return jnp.sum(array.astype(f32), axis=0).astype(bf16)


def add_low(left, right):
    return (left.astype(f32) + right.astype(f32)).astype(bf16)


def chip_shift(array, distance):
    count = lax.axis_size("cols")
    return lax.ppermute(
        array, "cols", [(i, (i + 2 * distance) % count) for i in range(count)]
    )


def core_swap(array):
    count = lax.axis_size("cols")
    return lax.ppermute(array, "cols", [(i, i ^ 1) for i in range(count)])


def chips_gather(array):
    chips = lax.axis_size("cols") // 2
    return [array] + [chip_shift(array, d) for d in range(1, chips)]


def chips_in_order(array, chip):
    chips = array.shape[0]
    twice = jnp.concatenate([array[::-1]] * 2, axis=0)
    return lax.dynamic_slice_in_dim(twice, chips - 1 - chip, chips, 0)


def cores_sum(array):
    count = lax.axis_size("cols")
    pairs = [[i, i + 1] for i in range(0, count, 2)]
    came = lax.all_to_all(array, "cols", 0, 0, axis_index_groups=pairs, tiled=True)
    return add_low(came[0], came[1])


def chips_exchange(array):
    count = lax.axis_size("cols")
    alike = [list(range(core, count, 2)) for core in range(2)]
    return lax.all_to_all(array, "cols", 0, 0, axis_index_groups=alike, tiled=True)


def cores_in_order(mine, other, core, axis):
    return jnp.stack(
        [jnp.where(core == 0, mine, other), jnp.where(core == 0, other, mine)], axis=axis
    )


def call_params(mebibytes):
    return pltpu.CompilerParams(vmem_limit_bytes=mebibytes * 1024 * 1024)


def cost(micros):
    return pl.CostEstimate(flops=int(micros * 1.15e9), bytes_accessed=0, transcendentals=0)


def turn(rows, cosine, sine):
    lane = lax.broadcasted_iota(jnp.int32, rows.shape, 1)
    partner = jnp.where(
        (lane & (HEAD_SIZE - 1)) < HEAD_SIZE // 2,
        pltpu.roll(rows, LANES - HEAD_SIZE // 2, 1),
        pltpu.roll(rows, HEAD_SIZE // 2, 1),
    )
    return rows * cosine + partner * sine


def project_kernel(meta, *refs):
    parts, found, swapped, gain, cosine, sine = refs[:4], refs[4], refs[5], *refs[6:9]
    q_out, k_out, v_out, n_out, w_out = refs[9:]
    step = pl.program_id(0)
    chips, rows, _ = found.shape
    chip = meta[1]

    @pl.when(step == 0)
    def _():
        first_core = meta[2] == 0
        for d in range(chips):
            mine, other = found[d], swapped[d]
            here = pl.multiple_of(lax.rem(chip + chips - d, chips) * (2 * rows), 2 * rows)
            w_out[pl.ds(here, 2 * rows), :] = jnp.concatenate(
                [jnp.where(first_core, mine, other), jnp.where(first_core, other, mine)], axis=0
            )

    for index, part in enumerate(parts):

        @pl.when(step == index)
        def _(part=part):
            rows = part[...].astype(f32)
            n_out[0] = (rows * rms_scale(rows) * gain[...]).astype(bf16)

    linear = dot_nn(n_out[0], w_out[...])
    q_cols, k_cols = q_out.shape[1], k_out.shape[1]
    cos_rows, sin_rows = cosine[...], sine[...]
    turned = jnp.concatenate(
        [
            turn(linear[:, at : at + LANES], cos_rows, sin_rows)
            for at in range(0, q_cols + k_cols, LANES)
        ],
        axis=1,
    ).astype(bf16)
    q_out[...] = turned[:, :q_cols]
    k_out[...] = turned[:, q_cols:]
    v_out[...] = linear[:, q_cols + k_cols :].astype(bf16)


def project(meta, parts, found, swapped, gain, cosine, sine, q_cols, k_cols):
    tok, width = parts[0].shape
    length = 4 * tok
    whole = pl.BlockSpec(memory_space=pltpu.VMEM)

    def natural(step, meta):
        return (step ^ meta[0], 0)

    return pl.pallas_call(
        project_kernel,
        grid_spec=pltpu.PrefetchScalarGridSpec(
            num_scalar_prefetch=1,
            grid=(4,),
            in_specs=[whole] * 7
            + [pl.BlockSpec((tok, LANES), natural), pl.BlockSpec((tok, LANES), natural)],
            out_specs=[
                pl.BlockSpec((tok, q_cols), natural),
                pl.BlockSpec((tok, k_cols), natural),
                pl.BlockSpec((tok, k_cols), natural),
                pl.BlockSpec((1, tok, width), lambda step, meta: (step, 0, 0)),
                pl.BlockSpec((width, q_cols + 2 * k_cols), lambda step, meta: (0, 0)),
            ],
        ),
        out_shape=[
            jax.ShapeDtypeStruct((length, q_cols), bf16),
            jax.ShapeDtypeStruct((length, k_cols), bf16),
            jax.ShapeDtypeStruct((length, k_cols), bf16),
            jax.ShapeDtypeStruct((4, tok, width), bf16),
            jax.ShapeDtypeStruct((width, q_cols + 2 * k_cols), bf16),
        ],
        compiler_params=call_params(32),
        cost_estimate=cost(10),
        name="project",
    )(meta, *parts, found, swapped, gain, cosine, sine)


def attend_kernel(meta, queries, keys, values, starts, out, lse, *, bands):
    block = pl.program_id(0)
    rows = queries.shape[0]
    first = meta[3 + block]
    heads = queries.shape[1] // HEAD_SIZE
    group = queries.shape[1] // keys.shape[1]
    for band in range(1, bands + 1):

        @pl.when(block - first + 1 == band)
        def _(band=band):
            width = band * rows
            base = pl.multiple_of(first * rows, rows)
            key_band = keys[pl.ds(base, width), :]
            value_band = values[pl.ds(base, width), :]
            query_pos = block * rows + lax.broadcasted_iota(jnp.int32, (rows, width), 0)
            key_pos = base + lax.broadcasted_iota(jnp.int32, (rows, width), 1)
            allowed = (key_pos >= starts[...]) & (key_pos <= query_pos)
            results = []
            for head in range(heads):
                at = head // group * HEAD_SIZE
                scores = dot_nt(
                    queries[:, head * HEAD_SIZE : (head + 1) * HEAD_SIZE],
                    key_band[:, at : at + HEAD_SIZE],
                )
                scores = jnp.where(allowed, scores, masked_score)
                top = jnp.max(scores, axis=1, keepdims=True)
                weights = jnp.exp2((scores - top) * (att_scale * log2_e))
                total = jnp.sum(weights, axis=1, keepdims=True)
                result = dot_nn(weights.astype(bf16), value_band[:, at : at + HEAD_SIZE])
                results.append(result * (1.0 / total))
                lse[:, head : head + 1] = top * (att_scale * log2_e) + jnp.log2(total)
            out[0] = jnp.concatenate(results, axis=1).astype(bf16)


def attend(meta, queries, keys, values, starts, tok):
    length, q_cols = queries.shape
    k_cols = keys.shape[1]
    blocks = length // tok
    whole = pl.BlockSpec(memory_space=pltpu.VMEM)
    return pl.pallas_call(
        partial(attend_kernel, bands=min(blocks, LONGEST_DOC // tok + 1)),
        grid_spec=pltpu.PrefetchScalarGridSpec(
            num_scalar_prefetch=1,
            grid=(blocks,),
            in_specs=[
                pl.BlockSpec((tok, q_cols), lambda i, meta: (i, 0)),
                whole,
                whole,
                pl.BlockSpec((tok, 1), lambda i, meta: (i, 0)),
            ],
            out_specs=[
                pl.BlockSpec((1, tok, q_cols), lambda i, meta: (i, 0, 0)),
                pl.BlockSpec((tok, 8), lambda i, meta: (i, 0)),
            ],
        ),
        out_shape=[
            jax.ShapeDtypeStruct((blocks, tok, q_cols), bf16),
            jax.ShapeDtypeStruct((length, 8), f32),
        ],
        compiler_params=call_params(32),
        cost_estimate=cost(16),
        name="attend",
    )(meta, queries, keys, values, starts)


def attend_back_kernel(
    meta, queries, grads, lse, starts, keys, values, cosine, sine, out, key_sum, value_sum, *, bands
):
    block = pl.program_id(0)
    rows = queries.shape[0]
    first = meta[3 + block]
    q_cols, k_cols = queries.shape[1], keys.shape[1]
    heads = q_cols // HEAD_SIZE
    group = q_cols // k_cols

    @pl.when(block == 0)
    def _():
        key_sum[...] = jnp.zeros_like(key_sum)
        value_sum[...] = jnp.zeros_like(value_sum)

    for band in range(1, bands + 1):

        @pl.when(block - first + 1 == band)
        def _(band=band):
            width = band * rows
            base = pl.multiple_of(first * rows, rows)
            key_band = keys[pl.ds(base, width), :]
            value_band = values[pl.ds(base, width), :]
            key_pos = base + lax.broadcasted_iota(jnp.int32, (width, rows), 0)
            query_pos = block * rows + lax.broadcasted_iota(jnp.int32, (width, rows), 1)
            allowed = (key_pos >= starts[...]) & (key_pos <= query_pos)
            query_grads, key_parts, value_parts = [], [], []
            for kv_head in range(k_cols // HEAD_SIZE):
                at = kv_head * HEAD_SIZE
                key_rows = key_band[:, at : at + HEAD_SIZE]
                value_rows = value_band[:, at : at + HEAD_SIZE]
                key_part = jnp.zeros((width, HEAD_SIZE), f32)
                value_part = jnp.zeros((width, HEAD_SIZE), f32)
                for head in range(kv_head * group, (kv_head + 1) * group):
                    query_rows = queries[:, head * HEAD_SIZE : (head + 1) * HEAD_SIZE]
                    grad_rows = grads[0, :, head * HEAD_SIZE : (head + 1) * HEAD_SIZE]
                    scores = dot_nt(key_rows, query_rows)
                    probs = jnp.where(
                        allowed,
                        jnp.exp2(scores * (att_scale * log2_e) - lse[head : head + 1, :]),
                        0.0,
                    )
                    grad_probs = dot_nt(value_rows, grad_rows)
                    delta = jnp.sum(probs * grad_probs, axis=0, keepdims=True)
                    grad_scores = (probs * (grad_probs - delta)).astype(bf16)
                    value_part += dot_nn(probs.astype(bf16), grad_rows)
                    key_part += dot_nn(grad_scores, query_rows)
                    query_grads.append(dot_tn(grad_scores, key_rows))
                key_parts.append(key_part)
                value_parts.append(value_part)
            key_sum[pl.ds(base, width), :] += jnp.concatenate(key_parts, axis=1)
            value_sum[pl.ds(base, width), :] += jnp.concatenate(value_parts, axis=1)
            here = pl.ds(pl.multiple_of(block * rows, rows), rows)
            query_grad = jnp.concatenate(query_grads, axis=1) * att_scale
            turned = [
                turn(query_grad[:, c : c + LANES], cosine[here, :], -sine[here, :])
                for c in range(0, q_cols, LANES)
            ]
            out[block ^ meta[0], :, :q_cols] = jnp.concatenate(turned, axis=1).astype(bf16)

    @pl.when(block == pl.num_programs(0) - 1)
    def _():
        for part in range(4):
            here = pl.ds(pl.multiple_of((meta[0] ^ part) * rows, rows), rows)
            key_grad = key_sum[here, :] * att_scale
            turned = [
                turn(key_grad[:, c : c + LANES], cosine[here, :], -sine[here, :])
                for c in range(0, k_cols, LANES)
            ]
            out[part, :, q_cols : q_cols + k_cols] = jnp.concatenate(turned, axis=1).astype(bf16)
            out[part, :, q_cols + k_cols :] = value_sum[here, :].astype(bf16)


def attend_back(meta, queries, grads, lse, starts, keys, values, cosine, sine, tok):
    length, q_cols = queries.shape
    k_cols = keys.shape[1]
    blocks = length // tok
    whole = pl.BlockSpec(memory_space=pltpu.VMEM)
    return pl.pallas_call(
        partial(attend_back_kernel, bands=min(blocks, LONGEST_DOC // tok + 1)),
        grid_spec=pltpu.PrefetchScalarGridSpec(
            num_scalar_prefetch=1,
            grid=(blocks,),
            in_specs=[
                pl.BlockSpec((tok, q_cols), lambda i, meta: (i, 0)),
                pl.BlockSpec((1, tok, q_cols), lambda i, meta: (i, 0, 0)),
                pl.BlockSpec((8, tok), lambda i, meta: (0, i)),
                pl.BlockSpec((1, tok), lambda i, meta: (0, i)),
                whole,
                whole,
                whole,
                whole,
            ],
            out_specs=pl.BlockSpec(
                (blocks, tok, q_cols + 2 * k_cols), lambda i, meta: (0, 0, 0)
            ),
            scratch_shapes=[
                pltpu.VMEM((length, k_cols), f32),
                pltpu.VMEM((length, k_cols), f32),
            ],
        ),
        out_shape=jax.ShapeDtypeStruct((blocks, tok, q_cols + 2 * k_cols), bf16),
        compiler_params=call_params(40),
        cost_estimate=cost(29),
        name="attend_back",
    )(meta, queries, grads, lse, starts, keys, values, cosine, sine)


def low_pair(values):
    high = values.astype(bf16)
    return high, (values - high.astype(f32)).astype(bf16)


def mix_kernel(
    meta, heads, out_parts, tokens, member, gain, router, mixed_out, rows_out, gates_out, *, experts
):
    width = tokens.shape[1]
    branch = sum(dot_nn(heads[meta[0] ^ part], out_parts[part]) for part in range(4))
    mixed = tokens[...].astype(f32) + res_scale * branch
    mixed_out[...] = mixed
    normed = (mixed * rms_scale(mixed) * gain[...]).astype(bf16)
    logits = dot_nn(normed, router[...])
    named = member[...] > 0
    logits = jnp.where(named, logits, masked_score)
    lifted = jnp.exp(logits - jnp.max(logits, axis=1, keepdims=True))
    lifted = jnp.where(named, lifted, 0.0)
    gates = lifted * (1.0 / jnp.sum(lifted, axis=1, keepdims=True))
    gates_out[...] = gates
    high, low = low_pair(gates)
    low = pltpu.roll(low.astype(f32), experts, 1)
    rows_out[:, :width] = normed
    rows_out[:, width:] = (high.astype(f32) + low).astype(bf16)


def mix(meta, heads, out_parts, tokens, member, gain, router, experts):
    tok, width = tokens.shape
    whole = pl.BlockSpec(memory_space=pltpu.VMEM)
    return pl.pallas_call(
        partial(mix_kernel, experts=experts),
        in_specs=[pl.BlockSpec(memory_space=pltpu.SMEM)] + [whole] * 6,
        out_specs=[whole] * 3,
        out_shape=[
            jax.ShapeDtypeStruct((tok, width), f32),
            jax.ShapeDtypeStruct((tok, width + LANES), bf16),
            jax.ShapeDtypeStruct((tok, LANES), f32),
        ],
        compiler_params=call_params(40),
        cost_estimate=cost(6),
        name="mix",
    )(meta, heads, out_parts, tokens, member, gain, router)


def unmix_kernel(
    meta, came, last, mixed_in, cotangent, gates, gain, router, out_parts, heads,
    mixed_grad, heads_out, mine_out, other_out, *, experts
):
    width = cotangent.shape[1]
    summed = came[...].astype(f32) + last[...].astype(f32)
    beside = summed[:, width:]
    lane = lax.broadcasted_iota(jnp.int32, beside.shape, 1)
    weighted = jnp.where(lane < experts, beside + pltpu.roll(beside, LANES - experts, 1), 0.0)
    logit_grads = weighted - gates[...] * jnp.sum(weighted, axis=1, keepdims=True)
    high, low = low_pair(logit_grads)
    normed_grad = summed[:, :width] + dot_nt(high, router[...]) + dot_nt(low, router[...])
    mixed = mixed_in[...]
    scale = rms_scale(mixed)
    unit = mixed * scale
    normed = (unit * gain[...]).astype(bf16)
    one_lane = lax.broadcasted_iota(jnp.int32, (unit.shape[0], LANES), 1) == experts
    one_lane = one_lane.astype(f32).astype(bf16)
    gain_high, gain_low = low_pair(normed_grad * unit)
    shares = dot_tn(normed, high) + dot_tn(normed, low)
    shares = (shares + dot_tn(gain_high, one_lane) + dot_tn(gain_low, one_lane)).astype(bf16)
    unit_grad = normed_grad * gain[...]
    grad = cotangent[...].astype(f32) + scale * (
        unit_grad - unit * jnp.mean(unit_grad * unit, axis=-1, keepdims=True)
    )
    mixed_grad[...] = grad
    branch = (res_scale * grad).astype(bf16)
    for part in range(4):
        heads_out[meta[0] ^ part] = dot_nt(branch, out_parts[part]).astype(bf16)
    first_core = meta[2] == 0
    _, chips, sixth, _ = mine_out.shape
    tok = branch.shape[0]
    for part in range(4):
        wide = dot_tn(heads[part], branch).astype(bf16)
        wide = jnp.concatenate([wide, shares[part * tok : (part + 1) * tok]], axis=1)
        for chip in range(chips):
            at = 2 * chip * sixth
            even, odd = wide[at : at + sixth], wide[at + sixth : at + 2 * sixth]
            mine_out[part, chip] = jnp.where(first_core, even, odd)
            other_out[part, chip] = jnp.where(first_core, odd, even)


def unmix(meta, came, last, mixed, cotangent, gates, gain, router, out_parts, heads, experts, chips):
    tok, width = mixed.shape
    wide = (4, chips, tok // (2 * chips), width + LANES)
    whole = pl.BlockSpec(memory_space=pltpu.VMEM)
    return pl.pallas_call(
        partial(unmix_kernel, experts=experts),
        in_specs=[pl.BlockSpec(memory_space=pltpu.SMEM)] + [whole] * 9,
        out_specs=[whole] * 4,
        out_shape=[
            jax.ShapeDtypeStruct((tok, width), f32),
            jax.ShapeDtypeStruct((4, tok, out_parts.shape[1]), bf16),
            jax.ShapeDtypeStruct(wide, bf16),
            jax.ShapeDtypeStruct(wide, bf16),
        ],
        compiler_params=call_params(32),
        cost_estimate=cost(12),
        name="unmix",
    )(meta, came, last, mixed, cotangent, gates, gain, router, out_parts, heads)


def hidden_weights(parts, cut, ffe):
    tiles = 2 * ffe // LANES
    return jnp.concatenate(
        [
            jnp.concatenate([ref[0, t * cut : (t + 1) * cut, :] for t in range(tiles)], axis=1)
            for ref in parts
        ],
        axis=0,
    )


def down_weights(parts, cut, ffe):
    first = 2 * ffe // LANES * cut
    return jnp.concatenate(
        [
            ref[0, first + t * ffe : first + (t + 1) * ffe, :]
            for ref in parts
            for t in range(cut // LANES)
        ],
        axis=1,
    )


def experts_kernel(meta, *refs, experts, slots, local, final, earlier):
    blocks = 4
    x_refs, g_refs, refs = refs[:blocks], refs[blocks : 2 * blocks], refs[2 * blocks :]
    early, refs = refs[:earlier], refs[earlier:]
    parts, refs = refs[:4], refs[4:]
    returned_out, refs = refs[: blocks * final], refs[blocks * final :]
    x_out, g_out, active_out, grads_out, out_kept, dx_kept, t_kept, refs = *refs[:7], refs[7:]
    x_rows, g_rows, gate_kept, rows_sent, x_here, g_here, arrived, refs = *refs[:7], refs[7:]
    own = pl.program_id(0)
    own_count = x_rows.shape[0]
    tok = x_refs[0].shape[0]
    width = x_rows.shape[2]
    cut = width // 4
    ffe = active_out.shape[2]
    row, first_expert = meta[0], meta[1]
    loads = [
        (
            pltpu.make_async_copy(x_refs[block], x_here.at[block % 2], arrived.at[0, block % 2]),
            pltpu.make_async_copy(g_refs[block], g_here.at[block % 2], arrived.at[1, block % 2]),
        )
        for block in range(blocks)
    ]
    if final:
        ranks_kept, returned, sent, refs = *refs[:3], refs[3:]
    fetches = [
        [
            pltpu.make_async_copy(
                early[which].at[:, pl.ds(block * slots, slots), :],
                refs[which].at[block % 2],
                refs[3].at[which, block % 2],
            )
            for which in range(earlier)
        ]
        for block in range(blocks)
    ]
    row_copies = [
        pltpu.make_async_copy(x_rows, x_out, rows_sent.at[0]),
        pltpu.make_async_copy(g_rows, g_out, rows_sent.at[1]),
    ]

    def columns(part, start=0):
        return pl.ds(pl.multiple_of(start + (row ^ part) * cut, LANES), cut)

    @pl.when(own == 0)
    def _():
        for load in loads[0]:
            load.start()
        slot = lax.broadcasted_iota(jnp.int32, (slots, tok), 0).astype(f32)
        lower = (
            lax.broadcasted_iota(jnp.int32, (tok, tok), 0)
            > lax.broadcasted_iota(jnp.int32, (tok, tok), 1)
        ).astype(f32).astype(bf16)
        source = lax.broadcasted_iota(jnp.int32, (LANES, LANES), 1)
        target = lax.broadcasted_iota(jnp.int32, (LANES, LANES), 0)
        choose = (source == target + first_expert).astype(f32).astype(bf16)
        for block in range(blocks):
            for load in loads[block + 1] if block + 1 < blocks else ():
                load.start()
            for load in loads[block]:
                load.wait()
            x_block, g_block = x_here.at[block % 2], g_here.at[block % 2]
            member = g_block[:, width:]
            rank = jnp.where(member > 0, dot_nn(lower, member), -1.0).astype(bf16)
            if final:
                ranks_kept[block] = dot_nt(rank, choose)
            rank_rows = dot_nt(choose, rank)
            pick = jnp.concatenate(
                [
                    (rank_rows[index : index + 1, :] == slot).astype(f32).astype(bf16)
                    for index in range(local, local + own_count)
                ],
                axis=0,
            )
            beside = dot_nn(pick, x_block[:, width:])
            lane = lax.broadcasted_iota(jnp.int32, beside.shape, 1)
            named = lax.broadcasted_iota(jnp.int32, beside.shape, 0) // slots
            named = named + first_expert + local
            gates = jnp.sum(
                jnp.where((lane == named) | (lane == named + experts), beside, 0.0),
                axis=1,
                keepdims=True,
            )
            here = slice(block * slots, (block + 1) * slots)
            x_part = dot_nn(pick, x_block[:, :width]).astype(bf16)
            g_part = dot_nn(pick, g_block[:, :width]).astype(bf16)
            for index in range(own_count):
                rows = slice(index * slots, (index + 1) * slots)
                gate_kept[index, here, :] = gates[rows]
                for part in range(4):
                    there = slice(part * cut, (part + 1) * cut)
                    x_rows[index, here, columns(part)] = x_part[rows, there]
                    g_rows[index, here, columns(part)] = g_part[rows, there]
        for copy in row_copies:
            copy.start()

    @pl.when(own == own_count - 1)
    def _():
        for fetch in fetches[0] + fetches[1]:
            fetch.start()

    hidden_w = hidden_weights(parts, cut, ffe)
    down_w = down_weights(parts, cut, ffe)
    hidden = dot_nn(x_rows[own], hidden_w)
    hidden_gate, hidden_up = hidden[:, :ffe], hidden[:, ffe:]
    gates = gate_kept[own]
    grad_active = dot_nt(g_rows[own], down_w) * (res_scale * gates)
    sigmoid = jax.nn.sigmoid(hidden_gate)
    silu = hidden_gate * sigmoid
    active = silu * hidden_up
    gated = (active * gates).astype(bf16)
    grad_gate = grad_active * hidden_up * (sigmoid * (1.0 + hidden_gate * (1.0 - sigmoid)))
    grads = jnp.concatenate(
        [grad_gate.astype(bf16), (grad_active * silu).astype(bf16)], axis=1
    )
    weighted = jnp.sum(active * grad_active, axis=1, keepdims=True)
    active_out[0] = gated
    grads_out[0] = grads
    kept = own if final else 0
    out_kept[kept] = dot_nn(gated, down_w).astype(bf16)
    dx_kept[kept] = dot_nt(grads, hidden_w).astype(bf16)
    weighted_high = weighted.astype(bf16).astype(f32)
    lane = lax.broadcasted_iota(jnp.int32, (blocks * slots, LANES), 1)
    named = first_expert + local + own
    t_kept[kept] = jnp.where(
        lane == named,
        weighted_high,
        jnp.where(lane == named + experts, weighted - weighted_high, 0.0),
    ).astype(bf16)

    @pl.when(own == own_count - 1)
    def _():
        if final:
            slot = lax.broadcasted_iota(jnp.int32, (tok, slots), 1).astype(f32)
            gives = [
                pltpu.make_async_copy(
                    returned.at[block % 2], returned_out[block], sent.at[block]
                )
                for block in range(blocks)
            ]
            for block in range(blocks):
                here = slice(block * slots, (block + 1) * slots)
                put = jnp.concatenate(
                    [
                        (ranks_kept[block, :, index : index + 1] == slot).astype(f32).astype(bf16)
                        for index in range(local + own_count)
                    ],
                    axis=1,
                )

                def rows_of(which, here=here, block=block):
                    kept_rows = (out_kept, dx_kept, t_kept)[which]
                    found = [refs[which][block % 2, index] for index in range(local)]
                    found += [kept_rows[index, here, :] for index in range(own_count)]
                    return jnp.concatenate(found, axis=0)

                for fetch in fetches[block]:
                    fetch.wait()
                if block >= 2:
                    gives[block - 2].wait()
                out = dot_nn(put, rows_of(0)).astype(bf16)
                dx = dot_nn(put, rows_of(1)).astype(bf16)
                for part in range(4):
                    there = slice(part * cut, (part + 1) * cut)
                    returned[block % 2, :, columns(part)] = out[:, there]
                    returned[block % 2, :, columns(part, width)] = dx[:, there]
                returned[block % 2, :, 2 * width :] = dot_nn(put, rows_of(2)).astype(bf16)
                gives[block].start()
                for fetch in fetches[block + 2] if block + 2 < blocks else ():
                    fetch.start()
            for give in gives[-2:]:
                give.wait()
        for copy in row_copies:
            copy.wait()


def run_experts(meta, x_blocks, g_blocks, early, parts, ffe, experts, slots, local, final):
    blocks = len(x_blocks)
    tok, padded = x_blocks[0].shape
    width = padded - LANES
    own, packed, _ = parts[0].shape
    rows = blocks * slots
    anywhere = pl.BlockSpec(memory_space=pl.ANY)
    back = 2 * width + LANES
    kept_shapes = [(own, rows, width), (own, rows, width), (own, rows, LANES)]
    row_shapes = [(own, rows, width), (own, rows, width), (own, rows, ffe), (own, rows, 2 * ffe)]

    def one(*shape):
        return pl.BlockSpec((1,) + shape, lambda e, meta: (e, 0, 0))

    out_specs = [anywhere] * 2 + [one(rows, ffe), one(rows, 2 * ffe)]
    out_shapes = [jax.ShapeDtypeStruct(shape, bf16) for shape in row_shapes]
    scratch = []
    if final:
        out_specs = [anywhere] * blocks + out_specs
        out_shapes = [jax.ShapeDtypeStruct((tok, back), bf16)] * blocks + out_shapes
        scratch += [pltpu.VMEM(shape, bf16) for shape in kept_shapes]
    else:
        out_specs += [one(*shape[1:]) for shape in kept_shapes]
        out_shapes += [jax.ShapeDtypeStruct(shape, bf16) for shape in kept_shapes]
    scratch += [
        pltpu.VMEM((own, rows, width), bf16),
        pltpu.VMEM((own, rows, width), bf16),
        pltpu.VMEM((own, rows, 1), f32),
        pltpu.SemaphoreType.DMA((2,)),
        pltpu.VMEM((2, tok, padded), bf16),
        pltpu.VMEM((2, tok, padded), bf16),
        pltpu.SemaphoreType.DMA((2, 2)),
    ]
    if final:
        scratch += [
            pltpu.VMEM((blocks, tok, LANES), f32),
            pltpu.VMEM((2, tok, back), bf16),
            pltpu.SemaphoreType.DMA((blocks,)),
        ]
    if early:
        scratch += [
            pltpu.VMEM((2, array.shape[0], slots, array.shape[2]), bf16) for array in early
        ] + [pltpu.SemaphoreType.DMA((3, 2))]
    return pl.pallas_call(
        partial(
            experts_kernel,
            experts=experts,
            slots=slots,
            local=local,
            final=final,
            earlier=len(early),
        ),
        grid_spec=pltpu.PrefetchScalarGridSpec(
            num_scalar_prefetch=1,
            grid=(own,),
            in_specs=[anywhere] * (2 * blocks + len(early)) + [one(packed, LANES)] * 4,
            out_specs=out_specs,
            scratch_shapes=scratch,
        ),
        out_shape=out_shapes,
        compiler_params=call_params(60),
        cost_estimate=cost(26),
        name="experts",
    )(meta, *x_blocks, *g_blocks, *early, *parts)


def weight_grad_kernel(*refs, chunks, own_count):
    x_refs, grad_refs, active_refs, g_refs = (
        refs[chunks * index : chunks * (index + 1)] for index in range(4)
    )
    refs = refs[4 * chunks :]
    outs, (made, sent) = refs[: 4 * own_count], refs[4 * own_count :]
    x_rows = jnp.concatenate([ref[0] for ref in x_refs], axis=0)
    grads = jnp.concatenate([ref[0] for ref in grad_refs], axis=0)
    active = jnp.concatenate([ref[0] for ref in active_refs], axis=0)
    g_rows = jnp.concatenate([ref[0] for ref in g_refs], axis=0)
    cut = x_rows.shape[1] // 4
    ffe = grads.shape[1] // 2
    first = 2 * ffe // LANES * cut
    own = pl.program_id(0)
    for part in range(4):
        hidden = dot_tn(x_rows[:, part * cut : (part + 1) * cut], grads).astype(bf16)
        for t in range(2 * ffe // LANES):
            made[own, part, t * cut : (t + 1) * cut, :] = hidden[:, t * LANES : (t + 1) * LANES]
    down = (dot_tn(active, g_rows) * res_scale).astype(bf16)
    for part in range(4):
        for t in range(cut // LANES):
            at = part * cut + t * LANES
            here = slice(first + t * ffe, first + (t + 1) * ffe)
            made[own, part, here, :] = down[:, at : at + LANES]
    copies = [
        [
            pltpu.make_async_copy(
                made.at[expert, part], outs[part * own_count + expert].at[0], sent.at[expert, part]
            )
            for part in range(4)
        ]
        for expert in range(own_count)
    ]
    for expert in range(own_count):

        @pl.when(own == expert)
        def _(expert=expert):
            for copy in copies[expert]:
                copy.start()

    @pl.when(own == own_count - 1)
    def _():
        for group in copies:
            for copy in group:
                copy.wait()


def weight_grads(x_chunks, grad_chunks, active_chunks, g_chunks):
    own, rows, width = x_chunks[0].shape
    ffe = active_chunks[0].shape[2]
    chunks = len(x_chunks)
    packed = 3 * ffe * (width // 4) // LANES

    def one(*shape):
        return pl.BlockSpec((1,) + shape, lambda e: (e, 0, 0))

    outs = pl.pallas_call(
        partial(weight_grad_kernel, chunks=chunks, own_count=own),
        grid=(own,),
        in_specs=[one(rows, width)] * chunks
        + [one(rows, 2 * ffe)] * chunks
        + [one(rows, ffe)] * chunks
        + [one(rows, width)] * chunks,
        out_specs=[pl.BlockSpec(memory_space=pl.ANY)] * (4 * own),
        out_shape=[jax.ShapeDtypeStruct((1, packed, LANES), bf16)] * (4 * own),
        scratch_shapes=[
            pltpu.VMEM((own, 4, packed, LANES), bf16),
            pltpu.SemaphoreType.DMA((own, 4)),
        ],
        compiler_params=call_params(60),
        cost_estimate=cost(13),
        name="weight_grads",
    )(*x_chunks, *grad_chunks, *active_chunks, *g_chunks)
    return [list(outs[part * own : (part + 1) * own]) for part in range(4)]


def two_halves(arrays):
    return arrays if len(arrays) == 2 else list(halves(arrays[0])[1:])


def join_halves(array, own):
    return array.reshape(own, 2 * array.shape[1] // own, array.shape[2])


def pack_weights(gate, up, down):
    return jnp.concatenate(
        [
            lax.slice_in_dim(array, at, at + LANES, axis=2)
            for array in (gate, up, down)
            for at in range(0, array.shape[2], LANES)
        ],
        axis=1,
    )


def unpack_weights(packed, cut, ffe):
    tiles = ffe // LANES

    def beside(first, rows, count):
        return jnp.concatenate(
            [packed[:, first + t * rows : first + (t + 1) * rows, :] for t in range(count)], axis=2
        )

    return (
        beside(0, cut, tiles),
        beside(tiles * cut, cut, tiles),
        beside(2 * tiles * cut, ffe, cut // LANES),
    )


def after(array, *earlier):
    return lax.optimization_barrier((array, earlier))[0]


def per_device(
    tokens,
    segment_ids,
    expert_ids,
    w_query,
    key_matrix,
    value_matrix,
    w_out,
    norm_attn,
    norm_moe,
    w_router,
    w_gate,
    w_up,
    w_down,
    cotangent,
):
    row = lax.axis_index("rows")
    column = lax.axis_index("cols")
    columns = lax.axis_size("cols")
    chips = columns // 2
    chip, core = column // 2, column % 2
    own_tokens = tokens[0]
    tok, width = own_tokens.shape
    own_experts = w_gate.shape[0]
    experts = own_experts * columns
    top_count = expert_ids.shape[2]
    capacity = 5 * tok * top_count // (4 * experts)
    slots = -(-capacity // LANES) * LANES
    q_cols, k_cols = w_query.shape[1], key_matrix.shape[1]

    token_near = gather_near(own_tokens)
    qkv_cols = q_cols + 2 * k_cols
    sixth = w_out.shape[0]
    found = chips_gather(
        jnp.concatenate(
            [w_query, key_matrix, value_matrix, w_out.reshape(4 * sixth, width // 4)], axis=1
        )
    )
    small = jnp.concatenate(
        [
            w_router,
            norm_attn[:, None],
            norm_moe[:, None],
            jnp.zeros((w_router.shape[0], LANES - experts - 2), bf16),
        ],
        axis=1,
    )
    small_full = lax.all_to_all(
        jnp.tile(small, (4 * columns, 1)), ("rows", "cols"), 0, 0, tiled=True
    )
    gain_attn = small_full[:, experts].astype(f32)[None, :]
    gain_moe = small_full[:, experts + 1].astype(f32)[None, :]
    router_full = jnp.where(jnp.arange(LANES) < experts, small_full, 0)
    token_parts = gather_far(own_tokens, *token_near)
    found = after(found, token_parts[3])
    project_found = jnp.stack([rows[:, :qkv_cols] for rows in found])
    project_swapped = core_swap(project_found)

    out_half = jnp.stack([rows[:, qkv_cols:].reshape(sixth, width) for rows in found])
    out_half = chips_in_order(out_half, chip).reshape(chips * sixth, width)
    out_near = gather_near(after(out_half, token_parts[3]))

    expert_rows = expert_ids[0]
    lane_range = jnp.arange(LANES, dtype=jnp.int32)
    member = jnp.any(expert_rows[:, :, None] == lane_range[None, None, :], axis=1).astype(bf16)
    cot_rows = jnp.concatenate([cotangent[0], member], axis=1)
    cot_same = [cot_rows, chip_shift(after(cot_rows, found[1:], token_parts[3]), 1)]

    groups = 2 if own_experts % 2 == 0 else 1
    group_size = own_experts // groups
    packed = []
    for group in range(groups):
        here = slice(group * group_size, (group + 1) * group_size)
        packed.append(pack_weights(after(w_gate[here], own_tokens), w_up[here], w_down[here]))
    weight_near = [gather_near(after(packed[0], token_parts[3], project_swapped, out_half))]

    segments = segment_ids[0]
    length = segments.shape[0]
    starts = jnp.sum((segments[None, :] < segments[:, None]).astype(jnp.int32), axis=1)
    positions = (jnp.arange(length, dtype=jnp.int32) - starts).astype(f32)
    half = HEAD_SIZE // 2
    frequency = rope_base ** (-(2.0 * jnp.arange(half, dtype=f32)) / HEAD_SIZE)
    angles = positions[:, None] * frequency[None, :]
    cos_half, sin_half = jnp.cos(angles), jnp.sin(angles)
    cosine = jnp.concatenate([cos_half] * 4, axis=1)
    sine = jnp.concatenate([-sin_half, sin_half] * 2, axis=1)
    first_blocks = starts[::tok] // tok
    place = jnp.stack([row, chip, core])
    meta = jnp.concatenate([place.astype(jnp.int32), first_blocks.astype(jnp.int32)])

    queries, key_rows, value_rows, normed, project_w = project(
        meta, token_parts, project_found, project_swapped, gain_attn, cosine, sine, q_cols, k_cols
    )
    attended, lse = attend(meta, queries, key_rows, value_rows, starts[:, None], tok)
    cot_same[1], out_near = after((cot_same[1], out_near), attended)
    for d in range(2, chips):
        cot_same.append(chip_shift(cot_same[-1], 1))
    attended = after(attended, weight_near[0])
    own_heads = lax.all_to_all(attended, "rows", 0, 0, tiled=True)
    out_mine = jnp.stack(gather_far(out_half, *out_near)).reshape(4, chips, sixth, width)
    out_mine = after(out_mine, cot_same[2])
    out_parts = cores_in_order(out_mine, core_swap(out_mine), core, 2).reshape(4, tok, width)
    weight_near[0] = after(weight_near[0], own_heads)
    first_far = far_halves(*weight_near[0])
    mixed_rows, moe_rows, gates = mix(
        meta,
        own_heads,
        out_parts,
        own_tokens,
        member,
        gain_moe,
        router_full,
        experts,
    )
    weight_parts = [join_far(packed[0], *weight_near[0], after(first_far, moe_rows))]
    for group in range(1, groups):
        weight_near.append(gather_near(after(packed[group], weight_parts[0][3])))
    moe_same = [moe_rows, chip_shift(after(moe_rows, cot_same[3], weight_parts[0][3]), 1)]
    moe_other = [core_swap(rows) for rows in moe_same]
    moe_same.append(chip_shift(moe_same[1], 1))
    cot_other = [core_swap(after(rows, moe_rows)) for rows in cot_same]

    moe_meta = jnp.stack([row, column * own_experts]).astype(jnp.int32)
    ffe = w_down.shape[1]
    kept = [[] for _ in range(groups)]
    pieces = [None] * chips
    grads = []

    def piece(d, start, stop):
        return add_low(pieces[d][0][:, start:stop], pieces[d][1][:, start:stop])

    both = 2 * width + LANES
    pairs = [(d, d + 1) for d in range(0, chips, 2)]
    early = [[] for _ in pairs]
    held = ()
    far, late, sums = [], [], []

    def make_grads(group, first_rows):
        chunks = kept[group]
        parts = weight_grads(
            [first_rows] + [k[0] for k in chunks[1:]],
            [k[3] for k in chunks],
            [k[2] for k in chunks],
            [k[1] for k in chunks],
        )
        grads.append([two_halves(part) for part in parts])

    for index, pair in enumerate(pairs):
        for group in range(groups):
            final = group == groups - 1
            if final and index == len(pairs) - 1 and groups > 1:
                make_grads(0, kept[0][0][0])
                far.append(reduce_first(grads[0]))
                held = grads[0]
            result = list(
                run_experts(
                    after(moe_meta, held),
                    [rows for d in pair for rows in (moe_same[d], moe_other[d])],
                    [rows for d in pair for rows in (cot_same[d], cot_other[d])],
                    early[index],
                    weight_parts[group],
                    ffe,
                    experts,
                    slots,
                    group * group_size,
                    final,
                )
            )
            held = result[0]
            if len(moe_other) == 2:
                moe_same[2] = after(moe_same[2], held)
                held = (held, moe_same[2])
                for d in range(3, chips):
                    moe_same.append(chip_shift(moe_same[-1], 1))
                moe_other += [core_swap(rows) for rows in moe_same[2:]]
                for later in range(1, groups):
                    weight_near[later] = after(weight_near[later], held)
                    weight_parts.append(gather_far(packed[later], *weight_near[later]))
            if not final:
                kept[group].append(result[:4])
                early[index] = result[4:]
                continue
            if index == 0:
                result = after(result, moe_same[3])
            if index == len(pairs) - 1:
                result = after(result, dx_hop, far if groups > 1 else ())
            kept[group].append(result[4:8])
            for place, d in enumerate(pair):
                pieces[d] = (result[2 * place], core_swap(result[2 * place + 1]))
            if index == 0:
                dx_ring = piece(1, width, both)
                held = dx_ring
                dx_hop = chip_shift(dx_ring, 1)
                continue
            for d in pair:
                came = dx_hop if d == 2 else chip_shift(dx_ring, 1)
                if d == chips - 1:
                    came = after(came, grads[-1])
                    far.append(reduce_first(after(grads[-1], came)))
                dx_ring = add_low(came, last_pieces[0] if d == chips - 1 else piece(d, width, both))
                if d != chips - 2:
                    continue
                last_pieces = [piece(chips - 1, width, both), piece(0, width, both)]
                if groups > 1:
                    sums.append(reduce_second(grads[0], after(far[0], dx_ring)))
                    late.append([rows_swap(*sent) for sent in zip(sums[0], (1, 2))])
                make_grads(group, after(kept[group][0][0], dx_ring, sums, last_pieces))
    for d in range(chips):
        pieces[d] = after(pieces[d], dx_ring)
    outs = [piece(d, 0, width) for d in range(chips - 1)]
    outs.append(piece(chips - 1, 0, width))
    dx_came = after(chip_shift(dx_ring, 1), outs)
    out_hop = chip_shift(after(outs[1], dx_came), 1)

    grad_mixed, grad_heads, wide_mine, wide_other = unmix(
        after(meta, late[:1]),
        dx_came,
        last_pieces[1],
        mixed_rows,
        cotangent[0],
        gates,
        gain_moe,
        router_full,
        out_parts,
        own_heads,
        experts,
        chips,
    )
    grad_attended = lax.all_to_all(grad_heads, "rows", 0, 0, tiled=True)

    wide_chip = add_low(wide_mine, core_swap(after(wide_other, far[-1])))
    wide_came = lax.all_to_all(wide_chip, "rows", 0, 0, tiled=True)

    grad_lin = attend_back(
        after(meta, wide_chip),
        queries,
        grad_attended,
        lse.T,
        starts[None, :],
        key_rows,
        value_rows,
        cosine,
        sine,
        tok,
    )
    grad_lin = after(grad_lin, late[:1], wide_came)
    normed_parts = [None] * 4
    for j in (3, 1, 2, 0):
        normed_parts[j] = dot_nt(grad_lin[j], project_w).astype(bf16)
    normed_sums = reduce_add(normed_parts, *reduce_far(normed_parts))
    normed_near = reduce_near(*normed_sums)
    sums.append(reduce_second(grads[-1], after(far[-1], *normed_sums)))
    late.append([rows_swap(*sent) for sent in zip(sums[-1], (1, 2))])
    grad_project = dot_tn(
        after(normed, *normed_parts).reshape(length, width), grad_lin.reshape(length, qkv_cols)
    )
    project_pairs = after(grad_project.astype(bf16), *normed_sums)
    project_pairs = project_pairs.reshape(chips, 2, width // columns, qkv_cols)
    project_chip = cores_sum(project_pairs.transpose(1, 0, 2, 3))
    project_came = chips_exchange(project_chip)
    project_sum = jnp.sum(after(project_came, late[-1]).astype(f32), axis=0)
    grad_normed = add_wide([normed_parts[0], *after(normed_near, project_sum)])
    wide_row = add_low_all(after(wide_came, project_came))
    wide_sum = jnp.sum(chips_exchange(wide_row).astype(f32), axis=0)
    grad_out_w = wide_sum[:, :width]
    grad_router_w = wide_sum[:, width : width + experts]
    grad_gain_moe_w = wide_sum[:, width + experts]

    out_ring = add_low(after(out_hop, grad_lin), outs[2])
    for d in range(3, chips):
        out_ring = add_low(after(chip_shift(out_ring, 1), *normed_sums), outs[d])
    moe_out = add_wide([after(chip_shift(out_ring, 1), project_chip), outs[0]])
    block_out = mixed_rows + res_scale * moe_out

    totals = []
    for parts, came in zip(grads, late):
        total = reduce_total([after(parts[0], *normed_sums, project_chip)], came)
        totals.append(unpack_weights(join_halves(total, group_size), width // 4, ffe))
    grad_gate_w, grad_up_w, grad_down_w = (
        jnp.concatenate(arrays, axis=0) for arrays in zip(*totals)
    )

    own_w = jnp.concatenate([w_query, key_matrix, value_matrix], axis=1).astype(f32)
    own_gain = lax.dynamic_slice_in_dim(gain_attn[0], column * own_w.shape[0], own_w.shape[0], 0)
    gain_rows = (jnp.sum(project_sum * own_w, axis=1) / own_gain).reshape(4, -1)
    gain_rows = after(gain_rows, wide_sum)
    gain_sum = jnp.sum(lax.all_to_all(gain_rows, "rows", 0, 0, tiled=True), axis=0)
    grad_gain_attn = lax.ppermute(
        gain_sum,
        ("rows", "cols"),
        [(r * columns + c, 4 * c + r) for r in range(4) for c in range(columns)],
    )

    own_float = own_tokens.astype(f32)
    scale_attn = rms_scale(own_float)
    unit_attn = own_float * scale_attn
    grad_unit = grad_normed * gain_attn
    grad_tokens = grad_mixed + scale_attn * (
        grad_unit - unit_attn * jnp.mean(grad_unit * unit_attn, axis=-1, keepdims=True)
    )
    return (
        block_out[None],
        grad_tokens[None],
        project_sum[:, :q_cols],
        project_sum[:, q_cols : q_cols + k_cols],
        project_sum[:, q_cols + k_cols :],
        grad_out_w,
        grad_gain_attn,
        grad_gain_moe_w,
        grad_router_w,
        grad_gate_w,
        grad_up_w,
        grad_down_w,
    )


def solution(mesh):
    placed = (
        P("cols", "rows", None),
        P("cols", None),
        P("cols", "rows", None),
        P("cols", "rows"),
        P("cols", "rows"),
        P("cols", "rows"),
        P(("rows", "cols"), None),
        P(("rows", "cols")),
        P(("rows", "cols")),
        P(("rows", "cols"), None),
        P("cols", "rows", None),
        P("cols", "rows", None),
        P("cols", None, "rows"),
        P("cols", "rows", None),
    )
    return jax.shard_map(
        per_device,
        mesh=mesh,
        in_specs=placed,
        out_specs=(
            P("cols", "rows", None),
            P("cols", "rows", None),
            P("cols", "rows"),
            P("cols", "rows"),
            P("cols", "rows"),
            P(("rows", "cols"), None),
            P(("rows", "cols")),
            P(("rows", "cols")),
            P(("rows", "cols"), None),
            P("cols", "rows", None),
            P("cols", "rows", None),
            P("cols", None, "rows"),
        ),
        check_vma=False,
    )
```

```python
from functools import partial

import jax
import jax.numpy as jnp
from jax import lax
from jax.experimental import pallas as pl
from jax.experimental.pallas import tpu as pltpu
from jax.sharding import PartitionSpec as P

HEAD_SIZE = 64
LANES = 128
LONGEST_DOC = 768

res_scale = 0.22
att_scale = 0.015625
norm_eps = 1e-06
rope_base = 10000.0
masked_score = -1e30
log2_e = 1.4426950408889634
highest = lax.Precision.HIGHEST
bf16 = jnp.bfloat16
f32 = jnp.float32


def rms_scale(hidden_rows):
    return lax.rsqrt(jnp.mean(hidden_rows * hidden_rows, axis=-1, keepdims=True) + norm_eps)


def dot_nt(left, right):
    return lax.dot_general(left, right, (((1,), (1,)), ((), ())), preferred_element_type=f32)


def dot_tn(left, right):
    return lax.dot_general(left, right, (((0,), (0,)), ((), ())), preferred_element_type=f32)


def dot_nn(left, right):
    return jnp.dot(left, right, preferred_element_type=f32)


def rows_swap(array, distance):
    return lax.ppermute(array, "rows", [(i, i ^ distance) for i in range(4)])


def halves(array):
    axis = 0 if array.shape[0] % 2 == 0 else 1
    cut = array.shape[axis] // 2
    return (
        axis,
        lax.slice_in_dim(array, 0, cut, axis=axis),
        lax.slice_in_dim(array, cut, 2 * cut, axis=axis),
    )


def gather_near(array):
    return rows_swap(array, 1), rows_swap(array, 2)


def far_halves(from_x, from_y):
    _, first_y, _ = halves(from_y)
    _, _, second_x = halves(from_x)
    return rows_swap(first_y, 1), rows_swap(second_x, 2)


def join_far(array, from_x, from_y, far):
    return [array, from_x, from_y, jnp.concatenate(far, axis=halves(array)[0])]


def gather_far(array, from_x, from_y):
    return join_far(array, from_x, from_y, far_halves(from_x, from_y))


def rows_exchange(pieces):
    return [pieces[0]] + [rows_swap(pieces[j], j) for j in (1, 2, 3)]


def reduce_far(pieces):
    _, first, second = halves(pieces[3])
    return rows_swap(first, 1), rows_swap(second, 2)


def reduce_add(pieces, from_x, from_y):
    axis, first_x, second_x = halves(pieces[1])
    _, first_y, second_y = halves(pieces[2])
    return (
        jnp.concatenate([first_x, add_low(second_x, from_y)], axis=axis),
        jnp.concatenate([add_low(first_y, from_x), second_y], axis=axis),
    )


def reduce_near(to_x, to_y):
    return rows_swap(to_x, 1), rows_swap(to_y, 2)


def reduce_first(pieces):
    return rows_swap(pieces[3][0], 1), rows_swap(pieces[3][1], 2)


def reduce_second(pieces, far):
    return (
        jnp.concatenate([pieces[1][0], add_low(pieces[1][1], far[1])], axis=0),
        jnp.concatenate([add_low(pieces[2][0], far[0]), pieces[2][1]], axis=0),
    )


def reduce_total(pieces, late):
    return add_wide([jnp.concatenate(pieces[0], axis=0), *late])


def add_wide(arrays):
    return sum(array.astype(f32) for array in arrays)


def add_low_all(array):
    return jnp.sum(array.astype(f32), axis=0).astype(bf16)


def add_low(left, right):
    return (left.astype(f32) + right.astype(f32)).astype(bf16)


def chip_shift(array, distance):
    count = lax.axis_size("cols")
    return lax.ppermute(
        array, "cols", [(i, (i + 2 * distance) % count) for i in range(count)]
    )


def core_swap(array):
    count = lax.axis_size("cols")
    return lax.ppermute(array, "cols", [(i, i ^ 1) for i in range(count)])


def chips_gather(array):
    chips = lax.axis_size("cols") // 2
    return [array] + [chip_shift(array, d) for d in range(1, chips)]


def chips_in_order(array, chip):
    chips = array.shape[0]
    twice = jnp.concatenate([array[::-1]] * 2, axis=0)
    return lax.dynamic_slice_in_dim(twice, chips - 1 - chip, chips, 0)


def cores_sum(array):
    count = lax.axis_size("cols")
    pairs = [[i, i + 1] for i in range(0, count, 2)]
    came = lax.all_to_all(array, "cols", 0, 0, axis_index_groups=pairs, tiled=True)
    return add_low(came[0], came[1])


def chips_exchange(array):
    count = lax.axis_size("cols")
    alike = [list(range(core, count, 2)) for core in range(2)]
    return lax.all_to_all(array, "cols", 0, 0, axis_index_groups=alike, tiled=True)


def cores_in_order(mine, other, core, axis):
    return jnp.stack(
        [jnp.where(core == 0, mine, other), jnp.where(core == 0, other, mine)], axis=axis
    )


def call_params(mebibytes):
    return pltpu.CompilerParams(vmem_limit_bytes=mebibytes * 1024 * 1024)


def cost(micros):
    return pl.CostEstimate(flops=int(micros * 1.15e9), bytes_accessed=0, transcendentals=0)


def turn(rows, cosine, sine):
    lane = lax.broadcasted_iota(jnp.int32, rows.shape, 1)
    partner = jnp.where(
        (lane & (HEAD_SIZE - 1)) < HEAD_SIZE // 2,
        pltpu.roll(rows, LANES - HEAD_SIZE // 2, 1),
        pltpu.roll(rows, HEAD_SIZE // 2, 1),
    )
    return rows * cosine + partner * sine


def project_kernel(meta, *refs):
    parts, found, swapped, gain, cosine, sine = refs[:4], refs[4], refs[5], *refs[6:9]
    q_out, k_out, v_out, n_out, w_out = refs[9:]
    step = pl.program_id(0)
    chips, rows, _ = found.shape
    chip = meta[1]

    @pl.when(step == 0)
    def _():
        first_core = meta[2] == 0
        for d in range(chips):
            mine, other = found[d], swapped[d]
            here = pl.multiple_of(lax.rem(chip + chips - d, chips) * (2 * rows), 2 * rows)
            w_out[pl.ds(here, 2 * rows), :] = jnp.concatenate(
                [jnp.where(first_core, mine, other), jnp.where(first_core, other, mine)], axis=0
            )

    for index, part in enumerate(parts):

        @pl.when(step == index)
        def _(part=part):
            rows = part[...].astype(f32)
            n_out[0] = (rows * rms_scale(rows) * gain[...]).astype(bf16)

    linear = dot_nn(n_out[0], w_out[...])
    q_cols, k_cols = q_out.shape[1], k_out.shape[1]
    cos_rows, sin_rows = cosine[...], sine[...]
    turned = jnp.concatenate(
        [
            turn(linear[:, at : at + LANES], cos_rows, sin_rows)
            for at in range(0, q_cols + k_cols, LANES)
        ],
        axis=1,
    ).astype(bf16)
    q_out[...] = turned[:, :q_cols]
    k_out[...] = turned[:, q_cols:]
    v_out[...] = linear[:, q_cols + k_cols :].astype(bf16)


def project(meta, parts, found, swapped, gain, cosine, sine, q_cols, k_cols):
    tok, width = parts[0].shape
    length = 4 * tok
    whole = pl.BlockSpec(memory_space=pltpu.VMEM)

    def natural(step, meta):
        return (step ^ meta[0], 0)

    return pl.pallas_call(
        project_kernel,
        grid_spec=pltpu.PrefetchScalarGridSpec(
            num_scalar_prefetch=1,
            grid=(4,),
            in_specs=[whole] * 7
            + [pl.BlockSpec((tok, LANES), natural), pl.BlockSpec((tok, LANES), natural)],
            out_specs=[
                pl.BlockSpec((tok, q_cols), natural),
                pl.BlockSpec((tok, k_cols), natural),
                pl.BlockSpec((tok, k_cols), natural),
                pl.BlockSpec((1, tok, width), lambda step, meta: (step, 0, 0)),
                pl.BlockSpec((width, q_cols + 2 * k_cols), lambda step, meta: (0, 0)),
            ],
        ),
        out_shape=[
            jax.ShapeDtypeStruct((length, q_cols), bf16),
            jax.ShapeDtypeStruct((length, k_cols), bf16),
            jax.ShapeDtypeStruct((length, k_cols), bf16),
            jax.ShapeDtypeStruct((4, tok, width), bf16),
            jax.ShapeDtypeStruct((width, q_cols + 2 * k_cols), bf16),
        ],
        compiler_params=call_params(32),
        cost_estimate=cost(10),
        name="project",
    )(meta, *parts, found, swapped, gain, cosine, sine)


def attend_kernel(meta, queries, keys, values, starts, out, lse, *, bands):
    block = pl.program_id(0)
    rows = queries.shape[0]
    first = meta[3 + block]
    heads = queries.shape[1] // HEAD_SIZE
    group = queries.shape[1] // keys.shape[1]
    for band in range(1, bands + 1):

        @pl.when(block - first + 1 == band)
        def _(band=band):
            width = band * rows
            base = pl.multiple_of(first * rows, rows)
            key_band = keys[pl.ds(base, width), :]
            value_band = values[pl.ds(base, width), :]
            query_pos = block * rows + lax.broadcasted_iota(jnp.int32, (rows, width), 0)
            key_pos = base + lax.broadcasted_iota(jnp.int32, (rows, width), 1)
            allowed = (key_pos >= starts[...]) & (key_pos <= query_pos)
            results = []
            for head in range(heads):
                at = head // group * HEAD_SIZE
                scores = dot_nt(
                    queries[:, head * HEAD_SIZE : (head + 1) * HEAD_SIZE],
                    key_band[:, at : at + HEAD_SIZE],
                )
                scores = jnp.where(allowed, scores, masked_score)
                top = jnp.max(scores, axis=1, keepdims=True)
                weights = jnp.exp2((scores - top) * (att_scale * log2_e))
                total = jnp.sum(weights, axis=1, keepdims=True)
                result = dot_nn(weights.astype(bf16), value_band[:, at : at + HEAD_SIZE])
                results.append(result * (1.0 / total))
                lse[:, head : head + 1] = top * (att_scale * log2_e) + jnp.log2(total)
            out[0] = jnp.concatenate(results, axis=1).astype(bf16)


def attend(meta, queries, keys, values, starts, tok):
    length, q_cols = queries.shape
    k_cols = keys.shape[1]
    blocks = length // tok
    whole = pl.BlockSpec(memory_space=pltpu.VMEM)
    return pl.pallas_call(
        partial(attend_kernel, bands=min(blocks, LONGEST_DOC // tok + 1)),
        grid_spec=pltpu.PrefetchScalarGridSpec(
            num_scalar_prefetch=1,
            grid=(blocks,),
            in_specs=[
                pl.BlockSpec((tok, q_cols), lambda i, meta: (i, 0)),
                whole,
                whole,
                pl.BlockSpec((tok, 1), lambda i, meta: (i, 0)),
            ],
            out_specs=[
                pl.BlockSpec((1, tok, q_cols), lambda i, meta: (i, 0, 0)),
                pl.BlockSpec((tok, 8), lambda i, meta: (i, 0)),
            ],
        ),
        out_shape=[
            jax.ShapeDtypeStruct((blocks, tok, q_cols), bf16),
            jax.ShapeDtypeStruct((length, 8), f32),
        ],
        compiler_params=call_params(32),
        cost_estimate=cost(16),
        name="attend",
    )(meta, queries, keys, values, starts)


def attend_back_kernel(
    meta, queries, grads, lse, starts, keys, values, cosine, sine, out, key_sum, value_sum, *, bands
):
    block = pl.program_id(0)
    rows = queries.shape[0]
    first = meta[3 + block]
    q_cols, k_cols = queries.shape[1], keys.shape[1]
    heads = q_cols // HEAD_SIZE
    group = q_cols // k_cols

    @pl.when(block == 0)
    def _():
        key_sum[...] = jnp.zeros_like(key_sum)
        value_sum[...] = jnp.zeros_like(value_sum)

    for band in range(1, bands + 1):

        @pl.when(block - first + 1 == band)
        def _(band=band):
            width = band * rows
            base = pl.multiple_of(first * rows, rows)
            key_band = keys[pl.ds(base, width), :]
            value_band = values[pl.ds(base, width), :]
            key_pos = base + lax.broadcasted_iota(jnp.int32, (width, rows), 0)
            query_pos = block * rows + lax.broadcasted_iota(jnp.int32, (width, rows), 1)
            allowed = (key_pos >= starts[...]) & (key_pos <= query_pos)
            query_grads, key_parts, value_parts = [], [], []
            for kv_head in range(k_cols // HEAD_SIZE):
                at = kv_head * HEAD_SIZE
                key_rows = key_band[:, at : at + HEAD_SIZE]
                value_rows = value_band[:, at : at + HEAD_SIZE]
                key_part = jnp.zeros((width, HEAD_SIZE), f32)
                value_part = jnp.zeros((width, HEAD_SIZE), f32)
                for head in range(kv_head * group, (kv_head + 1) * group):
                    query_rows = queries[:, head * HEAD_SIZE : (head + 1) * HEAD_SIZE]
                    grad_rows = grads[0, :, head * HEAD_SIZE : (head + 1) * HEAD_SIZE]
                    scores = dot_nt(key_rows, query_rows)
                    probs = jnp.where(
                        allowed,
                        jnp.exp2(scores * (att_scale * log2_e) - lse[head : head + 1, :]),
                        0.0,
                    )
                    grad_probs = dot_nt(value_rows, grad_rows)
                    delta = jnp.sum(probs * grad_probs, axis=0, keepdims=True)
                    grad_scores = (probs * (grad_probs - delta)).astype(bf16)
                    value_part += dot_nn(probs.astype(bf16), grad_rows)
                    key_part += dot_nn(grad_scores, query_rows)
                    query_grads.append(dot_tn(grad_scores, key_rows))
                key_parts.append(key_part)
                value_parts.append(value_part)
            key_sum[pl.ds(base, width), :] += jnp.concatenate(key_parts, axis=1)
            value_sum[pl.ds(base, width), :] += jnp.concatenate(value_parts, axis=1)
            here = pl.ds(pl.multiple_of(block * rows, rows), rows)
            query_grad = jnp.concatenate(query_grads, axis=1) * att_scale
            turned = [
                turn(query_grad[:, c : c + LANES], cosine[here, :], -sine[here, :])
                for c in range(0, q_cols, LANES)
            ]
            out[block ^ meta[0], :, :q_cols] = jnp.concatenate(turned, axis=1).astype(bf16)

    @pl.when(block == pl.num_programs(0) - 1)
    def _():
        for part in range(4):
            here = pl.ds(pl.multiple_of((meta[0] ^ part) * rows, rows), rows)
            key_grad = key_sum[here, :] * att_scale
            turned = [
                turn(key_grad[:, c : c + LANES], cosine[here, :], -sine[here, :])
                for c in range(0, k_cols, LANES)
            ]
            out[part, :, q_cols : q_cols + k_cols] = jnp.concatenate(turned, axis=1).astype(bf16)
            out[part, :, q_cols + k_cols :] = value_sum[here, :].astype(bf16)


def attend_back(meta, queries, grads, lse, starts, keys, values, cosine, sine, tok):
    length, q_cols = queries.shape
    k_cols = keys.shape[1]
    blocks = length // tok
    whole = pl.BlockSpec(memory_space=pltpu.VMEM)
    return pl.pallas_call(
        partial(attend_back_kernel, bands=min(blocks, LONGEST_DOC // tok + 1)),
        grid_spec=pltpu.PrefetchScalarGridSpec(
            num_scalar_prefetch=1,
            grid=(blocks,),
            in_specs=[
                pl.BlockSpec((tok, q_cols), lambda i, meta: (i, 0)),
                pl.BlockSpec((1, tok, q_cols), lambda i, meta: (i, 0, 0)),
                pl.BlockSpec((8, tok), lambda i, meta: (0, i)),
                pl.BlockSpec((1, tok), lambda i, meta: (0, i)),
                whole,
                whole,
                whole,
                whole,
            ],
            out_specs=pl.BlockSpec(
                (blocks, tok, q_cols + 2 * k_cols), lambda i, meta: (0, 0, 0)
            ),
            scratch_shapes=[
                pltpu.VMEM((length, k_cols), f32),
                pltpu.VMEM((length, k_cols), f32),
            ],
        ),
        out_shape=jax.ShapeDtypeStruct((blocks, tok, q_cols + 2 * k_cols), bf16),
        compiler_params=call_params(40),
        cost_estimate=cost(29),
        name="attend_back",
    )(meta, queries, grads, lse, starts, keys, values, cosine, sine)


def low_pair(values):
    high = values.astype(bf16)
    return high, (values - high.astype(f32)).astype(bf16)


def mix_kernel(
    meta, heads, out_parts, tokens, member, gain, router, mixed_out, rows_out, gates_out, *, experts
):
    width = tokens.shape[1]
    branch = sum(dot_nn(heads[meta[0] ^ part], out_parts[part]) for part in range(4))
    mixed = tokens[...].astype(f32) + res_scale * branch
    mixed_out[...] = mixed
    normed = (mixed * rms_scale(mixed) * gain[...]).astype(bf16)
    logits = dot_nn(normed, router[...])
    named = member[...] > 0
    logits = jnp.where(named, logits, masked_score)
    lifted = jnp.exp(logits - jnp.max(logits, axis=1, keepdims=True))
    lifted = jnp.where(named, lifted, 0.0)
    gates = lifted * (1.0 / jnp.sum(lifted, axis=1, keepdims=True))
    gates_out[...] = gates
    high, low = low_pair(gates)
    low = pltpu.roll(low.astype(f32), experts, 1)
    rows_out[:, :width] = normed
    rows_out[:, width:] = (high.astype(f32) + low).astype(bf16)


def mix(meta, heads, out_parts, tokens, member, gain, router, experts):
    tok, width = tokens.shape
    whole = pl.BlockSpec(memory_space=pltpu.VMEM)
    return pl.pallas_call(
        partial(mix_kernel, experts=experts),
        in_specs=[pl.BlockSpec(memory_space=pltpu.SMEM)] + [whole] * 6,
        out_specs=[whole] * 3,
        out_shape=[
            jax.ShapeDtypeStruct((tok, width), f32),
            jax.ShapeDtypeStruct((tok, width + LANES), bf16),
            jax.ShapeDtypeStruct((tok, LANES), f32),
        ],
        compiler_params=call_params(40),
        cost_estimate=cost(6),
        name="mix",
    )(meta, heads, out_parts, tokens, member, gain, router)


def unmix_kernel(
    meta, came, last, mixed_in, cotangent, gates, gain, router, out_parts, heads,
    mixed_grad, heads_out, mine_out, other_out, *, experts
):
    width = cotangent.shape[1]
    summed = came[...].astype(f32) + last[...].astype(f32)
    beside = summed[:, width:]
    lane = lax.broadcasted_iota(jnp.int32, beside.shape, 1)
    weighted = jnp.where(lane < experts, beside + pltpu.roll(beside, LANES - experts, 1), 0.0)
    logit_grads = weighted - gates[...] * jnp.sum(weighted, axis=1, keepdims=True)
    high, low = low_pair(logit_grads)
    normed_grad = summed[:, :width] + dot_nt(high, router[...]) + dot_nt(low, router[...])
    mixed = mixed_in[...]
    scale = rms_scale(mixed)
    unit = mixed * scale
    normed = (unit * gain[...]).astype(bf16)
    one_lane = lax.broadcasted_iota(jnp.int32, (unit.shape[0], LANES), 1) == experts
    one_lane = one_lane.astype(f32).astype(bf16)
    gain_high, gain_low = low_pair(normed_grad * unit)
    shares = dot_tn(normed, high) + dot_tn(normed, low)
    shares = (shares + dot_tn(gain_high, one_lane) + dot_tn(gain_low, one_lane)).astype(bf16)
    unit_grad = normed_grad * gain[...]
    grad = cotangent[...].astype(f32) + scale * (
        unit_grad - unit * jnp.mean(unit_grad * unit, axis=-1, keepdims=True)
    )
    mixed_grad[...] = grad
    branch = (res_scale * grad).astype(bf16)
    for part in range(4):
        heads_out[meta[0] ^ part] = dot_nt(branch, out_parts[part]).astype(bf16)
    first_core = meta[2] == 0
    _, chips, sixth, _ = mine_out.shape
    tok = branch.shape[0]
    for part in range(4):
        wide = dot_tn(heads[part], branch).astype(bf16)
        wide = jnp.concatenate([wide, shares[part * tok : (part + 1) * tok]], axis=1)
        for chip in range(chips):
            at = 2 * chip * sixth
            even, odd = wide[at : at + sixth], wide[at + sixth : at + 2 * sixth]
            mine_out[part, chip] = jnp.where(first_core, even, odd)
            other_out[part, chip] = jnp.where(first_core, odd, even)


def unmix(meta, came, last, mixed, cotangent, gates, gain, router, out_parts, heads, experts, chips):
    tok, width = mixed.shape
    wide = (4, chips, tok // (2 * chips), width + LANES)
    whole = pl.BlockSpec(memory_space=pltpu.VMEM)
    return pl.pallas_call(
        partial(unmix_kernel, experts=experts),
        in_specs=[pl.BlockSpec(memory_space=pltpu.SMEM)] + [whole] * 9,
        out_specs=[whole] * 4,
        out_shape=[
            jax.ShapeDtypeStruct((tok, width), f32),
            jax.ShapeDtypeStruct((4, tok, out_parts.shape[1]), bf16),
            jax.ShapeDtypeStruct(wide, bf16),
            jax.ShapeDtypeStruct(wide, bf16),
        ],
        compiler_params=call_params(32),
        cost_estimate=cost(12),
        name="unmix",
    )(meta, came, last, mixed, cotangent, gates, gain, router, out_parts, heads)


def hidden_weights(parts, cut, ffe):
    tiles = 2 * ffe // LANES
    return jnp.concatenate(
        [
            jnp.concatenate([ref[0, t * cut : (t + 1) * cut, :] for t in range(tiles)], axis=1)
            for ref in parts
        ],
        axis=0,
    )


def down_weights(parts, cut, ffe):
    first = 2 * ffe // LANES * cut
    return jnp.concatenate(
        [
            ref[0, first + t * ffe : first + (t + 1) * ffe, :]
            for ref in parts
            for t in range(cut // LANES)
        ],
        axis=1,
    )


def experts_kernel(meta, *refs, experts, slots, local, final, earlier):
    blocks = 4
    x_refs, g_refs, refs = refs[:blocks], refs[blocks : 2 * blocks], refs[2 * blocks :]
    early, refs = refs[:earlier], refs[earlier:]
    parts, refs = refs[:4], refs[4:]
    returned_out, refs = refs[: blocks * final], refs[blocks * final :]
    x_out, g_out, active_out, grads_out, out_kept, dx_kept, t_kept, refs = *refs[:7], refs[7:]
    x_rows, g_rows, gate_kept, rows_sent, x_here, g_here, arrived, refs = *refs[:7], refs[7:]
    own = pl.program_id(0)
    own_count = x_rows.shape[0]
    tok = x_refs[0].shape[0]
    width = x_rows.shape[2]
    cut = width // 4
    ffe = active_out.shape[2]
    row, first_expert = meta[0], meta[1]
    loads = [
        (
            pltpu.make_async_copy(x_refs[block], x_here.at[block % 2], arrived.at[0, block % 2]),
            pltpu.make_async_copy(g_refs[block], g_here.at[block % 2], arrived.at[1, block % 2]),
        )
        for block in range(blocks)
    ]
    if final:
        ranks_kept, returned, sent, refs = *refs[:3], refs[3:]
    fetches = [
        [
            pltpu.make_async_copy(
                early[which].at[:, pl.ds(block * slots, slots), :],
                refs[which].at[block % 2],
                refs[3].at[which, block % 2],
            )
            for which in range(earlier)
        ]
        for block in range(blocks)
    ]
    row_copies = [
        pltpu.make_async_copy(x_rows, x_out, rows_sent.at[0]),
        pltpu.make_async_copy(g_rows, g_out, rows_sent.at[1]),
    ]

    def columns(part, start=0):
        return pl.ds(pl.multiple_of(start + (row ^ part) * cut, LANES), cut)

    @pl.when(own == 0)
    def _():
        for load in loads[0]:
            load.start()
        slot = lax.broadcasted_iota(jnp.int32, (slots, tok), 0).astype(f32)
        lower = (
            lax.broadcasted_iota(jnp.int32, (tok, tok), 0)
            > lax.broadcasted_iota(jnp.int32, (tok, tok), 1)
        ).astype(f32).astype(bf16)
        source = lax.broadcasted_iota(jnp.int32, (LANES, LANES), 1)
        target = lax.broadcasted_iota(jnp.int32, (LANES, LANES), 0)
        choose = (source == target + first_expert).astype(f32).astype(bf16)
        for block in range(blocks):
            for load in loads[block + 1] if block + 1 < blocks else ():
                load.start()
            for load in loads[block]:
                load.wait()
            x_block, g_block = x_here.at[block % 2], g_here.at[block % 2]
            member = g_block[:, width:]
            rank = jnp.where(member > 0, dot_nn(lower, member), -1.0).astype(bf16)
            if final:
                ranks_kept[block] = dot_nt(rank, choose)
            rank_rows = dot_nt(choose, rank)
            pick = jnp.concatenate(
                [
                    (rank_rows[index : index + 1, :] == slot).astype(f32).astype(bf16)
                    for index in range(local, local + own_count)
                ],
                axis=0,
            )
            beside = dot_nn(pick, x_block[:, width:])
            lane = lax.broadcasted_iota(jnp.int32, beside.shape, 1)
            named = lax.broadcasted_iota(jnp.int32, beside.shape, 0) // slots
            named = named + first_expert + local
            gates = jnp.sum(
                jnp.where((lane == named) | (lane == named + experts), beside, 0.0),
                axis=1,
                keepdims=True,
            )
            here = slice(block * slots, (block + 1) * slots)
            x_part = dot_nn(pick, x_block[:, :width]).astype(bf16)
            g_part = dot_nn(pick, g_block[:, :width]).astype(bf16)
            for index in range(own_count):
                rows = slice(index * slots, (index + 1) * slots)
                gate_kept[index, here, :] = gates[rows]
                for part in range(4):
                    there = slice(part * cut, (part + 1) * cut)
                    x_rows[index, here, columns(part)] = x_part[rows, there]
                    g_rows[index, here, columns(part)] = g_part[rows, there]
        for copy in row_copies:
            copy.start()

    @pl.when(own == own_count - 1)
    def _():
        for fetch in fetches[0] + fetches[1]:
            fetch.start()

    hidden_w = hidden_weights(parts, cut, ffe)
    down_w = down_weights(parts, cut, ffe)
    hidden = dot_nn(x_rows[own], hidden_w)
    hidden_gate, hidden_up = hidden[:, :ffe], hidden[:, ffe:]
    gates = gate_kept[own]
    grad_active = dot_nt(g_rows[own], down_w) * (res_scale * gates)
    sigmoid = jax.nn.sigmoid(hidden_gate)
    silu = hidden_gate * sigmoid
    active = silu * hidden_up
    gated = (active * gates).astype(bf16)
    grad_gate = grad_active * hidden_up * (sigmoid * (1.0 + hidden_gate * (1.0 - sigmoid)))
    grads = jnp.concatenate(
        [grad_gate.astype(bf16), (grad_active * silu).astype(bf16)], axis=1
    )
    weighted = jnp.sum(active * grad_active, axis=1, keepdims=True)
    active_out[0] = gated
    grads_out[0] = grads
    kept = own if final else 0
    out_kept[kept] = dot_nn(gated, down_w).astype(bf16)
    dx_kept[kept] = dot_nt(grads, hidden_w).astype(bf16)
    weighted_high = weighted.astype(bf16).astype(f32)
    lane = lax.broadcasted_iota(jnp.int32, (blocks * slots, LANES), 1)
    named = first_expert + local + own
    t_kept[kept] = jnp.where(
        lane == named,
        weighted_high,
        jnp.where(lane == named + experts, weighted - weighted_high, 0.0),
    ).astype(bf16)

    @pl.when(own == own_count - 1)
    def _():
        if final:
            slot = lax.broadcasted_iota(jnp.int32, (tok, slots), 1).astype(f32)
            gives = [
                pltpu.make_async_copy(
                    returned.at[block % 2], returned_out[block], sent.at[block]
                )
                for block in range(blocks)
            ]
            for block in range(blocks):
                here = slice(block * slots, (block + 1) * slots)
                put = jnp.concatenate(
                    [
                        (ranks_kept[block, :, index : index + 1] == slot).astype(f32).astype(bf16)
                        for index in range(local + own_count)
                    ],
                    axis=1,
                )

                def rows_of(which, here=here, block=block):
                    kept_rows = (out_kept, dx_kept, t_kept)[which]
                    found = [refs[which][block % 2, index] for index in range(local)]
                    found += [kept_rows[index, here, :] for index in range(own_count)]
                    return jnp.concatenate(found, axis=0)

                for fetch in fetches[block]:
                    fetch.wait()
                if block >= 2:
                    gives[block - 2].wait()
                out = dot_nn(put, rows_of(0)).astype(bf16)
                dx = dot_nn(put, rows_of(1)).astype(bf16)
                for part in range(4):
                    there = slice(part * cut, (part + 1) * cut)
                    returned[block % 2, :, columns(part)] = out[:, there]
                    returned[block % 2, :, columns(part, width)] = dx[:, there]
                returned[block % 2, :, 2 * width :] = dot_nn(put, rows_of(2)).astype(bf16)
                gives[block].start()
                for fetch in fetches[block + 2] if block + 2 < blocks else ():
                    fetch.start()
            for give in gives[-2:]:
                give.wait()
        for copy in row_copies:
            copy.wait()


def run_experts(meta, x_blocks, g_blocks, early, parts, ffe, experts, slots, local, final):
    blocks = len(x_blocks)
    tok, padded = x_blocks[0].shape
    width = padded - LANES
    own, packed, _ = parts[0].shape
    rows = blocks * slots
    anywhere = pl.BlockSpec(memory_space=pl.ANY)
    back = 2 * width + LANES
    kept_shapes = [(own, rows, width), (own, rows, width), (own, rows, LANES)]
    row_shapes = [(own, rows, width), (own, rows, width), (own, rows, ffe), (own, rows, 2 * ffe)]

    def one(*shape):
        return pl.BlockSpec((1,) + shape, lambda e, meta: (e, 0, 0))

    out_specs = [anywhere] * 2 + [one(rows, ffe), one(rows, 2 * ffe)]
    out_shapes = [jax.ShapeDtypeStruct(shape, bf16) for shape in row_shapes]
    scratch = []
    if final:
        out_specs = [anywhere] * blocks + out_specs
        out_shapes = [jax.ShapeDtypeStruct((tok, back), bf16)] * blocks + out_shapes
        scratch += [pltpu.VMEM(shape, bf16) for shape in kept_shapes]
    else:
        out_specs += [one(*shape[1:]) for shape in kept_shapes]
        out_shapes += [jax.ShapeDtypeStruct(shape, bf16) for shape in kept_shapes]
    scratch += [
        pltpu.VMEM((own, rows, width), bf16),
        pltpu.VMEM((own, rows, width), bf16),
        pltpu.VMEM((own, rows, 1), f32),
        pltpu.SemaphoreType.DMA((2,)),
        pltpu.VMEM((2, tok, padded), bf16),
        pltpu.VMEM((2, tok, padded), bf16),
        pltpu.SemaphoreType.DMA((2, 2)),
    ]
    if final:
        scratch += [
            pltpu.VMEM((blocks, tok, LANES), f32),
            pltpu.VMEM((2, tok, back), bf16),
            pltpu.SemaphoreType.DMA((blocks,)),
        ]
    if early:
        scratch += [
            pltpu.VMEM((2, array.shape[0], slots, array.shape[2]), bf16) for array in early
        ] + [pltpu.SemaphoreType.DMA((3, 2))]
    return pl.pallas_call(
        partial(
            experts_kernel,
            experts=experts,
            slots=slots,
            local=local,
            final=final,
            earlier=len(early),
        ),
        grid_spec=pltpu.PrefetchScalarGridSpec(
            num_scalar_prefetch=1,
            grid=(own,),
            in_specs=[anywhere] * (2 * blocks + len(early)) + [one(packed, LANES)] * 4,
            out_specs=out_specs,
            scratch_shapes=scratch,
        ),
        out_shape=out_shapes,
        compiler_params=call_params(60),
        cost_estimate=cost(4),
        name="experts",
    )(meta, *x_blocks, *g_blocks, *early, *parts)


def weight_grad_kernel(*refs, chunks, own_count):
    x_refs, grad_refs, active_refs, g_refs = (
        refs[chunks * index : chunks * (index + 1)] for index in range(4)
    )
    refs = refs[4 * chunks :]
    outs, (made, sent) = refs[: 4 * own_count], refs[4 * own_count :]
    x_rows = jnp.concatenate([ref[0] for ref in x_refs], axis=0)
    grads = jnp.concatenate([ref[0] for ref in grad_refs], axis=0)
    active = jnp.concatenate([ref[0] for ref in active_refs], axis=0)
    g_rows = jnp.concatenate([ref[0] for ref in g_refs], axis=0)
    cut = x_rows.shape[1] // 4
    ffe = grads.shape[1] // 2
    first = 2 * ffe // LANES * cut
    own = pl.program_id(0)
    for part in range(4):
        hidden = dot_tn(x_rows[:, part * cut : (part + 1) * cut], grads).astype(bf16)
        for t in range(2 * ffe // LANES):
            made[own, part, t * cut : (t + 1) * cut, :] = hidden[:, t * LANES : (t + 1) * LANES]
    down = (dot_tn(active, g_rows) * res_scale).astype(bf16)
    for part in range(4):
        for t in range(cut // LANES):
            at = part * cut + t * LANES
            here = slice(first + t * ffe, first + (t + 1) * ffe)
            made[own, part, here, :] = down[:, at : at + LANES]
    copies = [
        [
            pltpu.make_async_copy(
                made.at[expert, part], outs[part * own_count + expert].at[0], sent.at[expert, part]
            )
            for part in range(4)
        ]
        for expert in range(own_count)
    ]
    for expert in range(own_count):

        @pl.when(own == expert)
        def _(expert=expert):
            for copy in copies[expert]:
                copy.start()

    @pl.when(own == own_count - 1)
    def _():
        for group in copies:
            for copy in group:
                copy.wait()


def weight_grads(x_chunks, grad_chunks, active_chunks, g_chunks):
    own, rows, width = x_chunks[0].shape
    ffe = active_chunks[0].shape[2]
    chunks = len(x_chunks)
    packed = 3 * ffe * (width // 4) // LANES

    def one(*shape):
        return pl.BlockSpec((1,) + shape, lambda e: (e, 0, 0))

    outs = pl.pallas_call(
        partial(weight_grad_kernel, chunks=chunks, own_count=own),
        grid=(own,),
        in_specs=[one(rows, width)] * chunks
        + [one(rows, 2 * ffe)] * chunks
        + [one(rows, ffe)] * chunks
        + [one(rows, width)] * chunks,
        out_specs=[pl.BlockSpec(memory_space=pl.ANY)] * (4 * own),
        out_shape=[jax.ShapeDtypeStruct((1, packed, LANES), bf16)] * (4 * own),
        scratch_shapes=[
            pltpu.VMEM((own, 4, packed, LANES), bf16),
            pltpu.SemaphoreType.DMA((own, 4)),
        ],
        compiler_params=call_params(60),
        cost_estimate=cost(13),
        name="weight_grads",
    )(*x_chunks, *grad_chunks, *active_chunks, *g_chunks)
    return [list(outs[part * own : (part + 1) * own]) for part in range(4)]


def two_halves(arrays):
    return arrays if len(arrays) == 2 else list(halves(arrays[0])[1:])


def join_halves(array, own):
    return array.reshape(own, 2 * array.shape[1] // own, array.shape[2])


def pack_weights(gate, up, down):
    return jnp.concatenate(
        [
            lax.slice_in_dim(array, at, at + LANES, axis=2)
            for array in (gate, up, down)
            for at in range(0, array.shape[2], LANES)
        ],
        axis=1,
    )


def unpack_weights(packed, cut, ffe):
    tiles = ffe // LANES

    def beside(first, rows, count):
        return jnp.concatenate(
            [packed[:, first + t * rows : first + (t + 1) * rows, :] for t in range(count)], axis=2
        )

    return (
        beside(0, cut, tiles),
        beside(tiles * cut, cut, tiles),
        beside(2 * tiles * cut, ffe, cut // LANES),
    )


def after(array, *earlier):
    return lax.optimization_barrier((array, earlier))[0]


def per_device(
    tokens,
    segment_ids,
    expert_ids,
    w_query,
    key_matrix,
    value_matrix,
    w_out,
    norm_attn,
    norm_moe,
    w_router,
    w_gate,
    w_up,
    w_down,
    cotangent,
):
    row = lax.axis_index("rows")
    column = lax.axis_index("cols")
    columns = lax.axis_size("cols")
    chips = columns // 2
    chip, core = column // 2, column % 2
    own_tokens = tokens[0]
    tok, width = own_tokens.shape
    own_experts = w_gate.shape[0]
    experts = own_experts * columns
    top_count = expert_ids.shape[2]
    capacity = 5 * tok * top_count // (4 * experts)
    slots = -(-capacity // LANES) * LANES
    q_cols, k_cols = w_query.shape[1], key_matrix.shape[1]

    token_near = gather_near(own_tokens)
    qkv_cols = q_cols + 2 * k_cols
    sixth = w_out.shape[0]
    found = chips_gather(
        jnp.concatenate(
            [w_query, key_matrix, value_matrix, w_out.reshape(4 * sixth, width // 4)], axis=1
        )
    )
    small = jnp.concatenate(
        [
            w_router,
            norm_attn[:, None],
            norm_moe[:, None],
            jnp.zeros((w_router.shape[0], LANES - experts - 2), bf16),
        ],
        axis=1,
    )
    small_full = lax.all_to_all(
        jnp.tile(small, (4 * columns, 1)), ("rows", "cols"), 0, 0, tiled=True
    )
    gain_attn = small_full[:, experts].astype(f32)[None, :]
    gain_moe = small_full[:, experts + 1].astype(f32)[None, :]
    router_full = jnp.where(jnp.arange(LANES) < experts, small_full, 0)
    token_parts = gather_far(own_tokens, *token_near)
    found = after(found, token_parts[3])
    project_found = jnp.stack([rows[:, :qkv_cols] for rows in found])
    project_swapped = core_swap(project_found)

    out_half = jnp.stack([rows[:, qkv_cols:].reshape(sixth, width) for rows in found])
    out_half = chips_in_order(out_half, chip).reshape(chips * sixth, width)
    out_near = gather_near(after(out_half, token_parts[3]))

    expert_rows = expert_ids[0]
    lane_range = jnp.arange(LANES, dtype=jnp.int32)
    member = jnp.any(expert_rows[:, :, None] == lane_range[None, None, :], axis=1).astype(bf16)
    cot_rows = jnp.concatenate([cotangent[0], member], axis=1)
    cot_same = [cot_rows, chip_shift(after(cot_rows, found[1:], token_parts[3]), 1)]

    groups = 2 if own_experts % 2 == 0 else 1
    group_size = own_experts // groups
    packed = []
    for group in range(groups):
        here = slice(group * group_size, (group + 1) * group_size)
        packed.append(pack_weights(after(w_gate[here], own_tokens), w_up[here], w_down[here]))
    weight_near = [gather_near(after(packed[0], token_parts[3], project_swapped, out_half))]

    segments = segment_ids[0]
    length = segments.shape[0]
    starts = jnp.sum((segments[None, :] < segments[:, None]).astype(jnp.int32), axis=1)
    positions = (jnp.arange(length, dtype=jnp.int32) - starts).astype(f32)
    half = HEAD_SIZE // 2
    frequency = rope_base ** (-(2.0 * jnp.arange(half, dtype=f32)) / HEAD_SIZE)
    angles = positions[:, None] * frequency[None, :]
    cos_half, sin_half = jnp.cos(angles), jnp.sin(angles)
    cosine = jnp.concatenate([cos_half] * 4, axis=1)
    sine = jnp.concatenate([-sin_half, sin_half] * 2, axis=1)
    first_blocks = starts[::tok] // tok
    place = jnp.stack([row, chip, core])
    meta = jnp.concatenate([place.astype(jnp.int32), first_blocks.astype(jnp.int32)])

    queries, key_rows, value_rows, normed, project_w = project(
        meta, token_parts, project_found, project_swapped, gain_attn, cosine, sine, q_cols, k_cols
    )
    attended, lse = attend(meta, queries, key_rows, value_rows, starts[:, None], tok)
    cot_same[1], out_near = after((cot_same[1], out_near), attended)
    cot_other = [core_swap(rows) for rows in cot_same]
    for d in range(2, chips):
        cot_same.append(chip_shift(cot_same[-1], 1))
    attended, out_near = after((attended, out_near), weight_near[0], cot_same[2], cot_other)
    own_heads = lax.all_to_all(attended, "rows", 0, 0, tiled=True)
    out_mine = jnp.stack(gather_far(out_half, *out_near)).reshape(4, chips, sixth, width)
    out_parts = cores_in_order(out_mine, core_swap(out_mine), core, 2).reshape(4, tok, width)
    weight_near[0] = after(weight_near[0], own_heads)
    first_far = far_halves(*weight_near[0])
    mixed_rows, moe_rows, gates = mix(
        meta,
        own_heads,
        out_parts,
        own_tokens,
        member,
        gain_moe,
        router_full,
        experts,
    )
    weight_parts = [join_far(packed[0], *weight_near[0], after(first_far, moe_rows))]
    for group in range(1, groups):
        weight_near.append(gather_near(after(packed[group], weight_parts[0][3])))
    moe_same = [moe_rows, chip_shift(after(moe_rows, cot_same[3], weight_parts[0][3]), 1)]
    moe_other = [core_swap(rows) for rows in moe_same]
    moe_same.append(chip_shift(moe_same[1], 1))
    cot_other += [core_swap(rows) for rows in cot_same[2:]]

    moe_meta = jnp.stack([row, column * own_experts]).astype(jnp.int32)
    ffe = w_down.shape[1]
    kept = [[] for _ in range(groups)]
    pieces = [None] * chips
    grads = []

    def piece(d, start, stop):
        return add_low(pieces[d][0][:, start:stop], pieces[d][1][:, start:stop])

    both = 2 * width + LANES
    pairs = [(d, d + 1) for d in range(0, chips, 2)]
    early = [[] for _ in pairs]
    held = ()
    far, late, sums = [], [], []

    def make_grads(group, first_rows):
        chunks = kept[group]
        parts = weight_grads(
            [first_rows] + [k[0] for k in chunks[1:]],
            [k[3] for k in chunks],
            [k[2] for k in chunks],
            [k[1] for k in chunks],
        )
        grads.append([two_halves(part) for part in parts])

    for index, pair in enumerate(pairs):
        for group in range(groups):
            final = group == groups - 1
            if final and index == len(pairs) - 1 and groups > 1:
                make_grads(0, kept[0][0][0])
                far.append(reduce_first(grads[0]))
                held = grads[0]
            result = list(
                run_experts(
                    after(moe_meta, held),
                    [rows for d in pair for rows in (moe_same[d], moe_other[d])],
                    [rows for d in pair for rows in (cot_same[d], cot_other[d])],
                    early[index],
                    weight_parts[group],
                    ffe,
                    experts,
                    slots,
                    group * group_size,
                    final,
                )
            )
            held = result[0]
            if len(moe_other) == 2:
                moe_same[2] = after(moe_same[2], held)
                held = (held, moe_same[2])
                for d in range(3, chips):
                    moe_same.append(chip_shift(moe_same[-1], 1))
                moe_other += [core_swap(rows) for rows in moe_same[2:]]
                for later in range(1, groups):
                    weight_near[later] = after(weight_near[later], held)
                    weight_parts.append(gather_far(packed[later], *weight_near[later]))
            if not final:
                kept[group].append(result[:4])
                early[index] = result[4:]
                continue
            if index == 0:
                result = after(result, moe_same[3])
            if index == len(pairs) - 1:
                result = after(result, dx_hop, far if groups > 1 else ())
            kept[group].append(result[4:8])
            for place, d in enumerate(pair):
                pieces[d] = (result[2 * place], core_swap(result[2 * place + 1]))
            if index == 0:
                dx_ring = piece(1, width, both)
                held = dx_ring
                dx_hop = chip_shift(dx_ring, 1)
                continue
            for d in pair:
                came = dx_hop if d == 2 else chip_shift(dx_ring, 1)
                if d == chips - 1:
                    came = after(came, grads[-1])
                    far.append(reduce_first(after(grads[-1], came)))
                dx_ring = add_low(came, last_pieces[0] if d == chips - 1 else piece(d, width, both))
                if d != chips - 2:
                    continue
                last_pieces = [piece(chips - 1, width, both), piece(0, width, both)]
                if groups > 1:
                    sums.append(reduce_second(grads[0], after(far[0], dx_ring)))
                    late.append([rows_swap(*sent) for sent in zip(sums[0], (1, 2))])
                make_grads(group, after(kept[group][0][0], dx_ring, sums, last_pieces))
    for d in range(chips):
        pieces[d] = after(pieces[d], dx_ring)
    outs = [piece(d, 0, width) for d in range(chips - 1)]
    outs.append(piece(chips - 1, 0, width))
    dx_came = after(chip_shift(dx_ring, 1), outs)
    out_hop = chip_shift(after(outs[1], dx_came), 1)

    grad_mixed, grad_heads, wide_mine, wide_other = unmix(
        after(meta, late[:1]),
        dx_came,
        last_pieces[1],
        mixed_rows,
        cotangent[0],
        gates,
        gain_moe,
        router_full,
        out_parts,
        own_heads,
        experts,
        chips,
    )
    grad_attended = lax.all_to_all(grad_heads, "rows", 0, 0, tiled=True)

    wide_chip = add_low(wide_mine, core_swap(after(wide_other, far[-1])))
    wide_came = lax.all_to_all(wide_chip, "rows", 0, 0, tiled=True)

    grad_lin = attend_back(
        after(meta, wide_chip),
        queries,
        grad_attended,
        lse.T,
        starts[None, :],
        key_rows,
        value_rows,
        cosine,
        sine,
        tok,
    )
    grad_lin = after(grad_lin, late[:1], wide_came)
    normed_parts = [None] * 4
    for j in (3, 1, 2, 0):
        normed_parts[j] = dot_nt(grad_lin[j], project_w).astype(bf16)
    normed_sums = reduce_add(normed_parts, *reduce_far(normed_parts))
    normed_near = reduce_near(*normed_sums)
    sums.append(reduce_second(grads[-1], after(far[-1], *normed_sums)))
    late.append([rows_swap(*sent) for sent in zip(sums[-1], (1, 2))])
    grad_project = dot_tn(
        after(normed, *normed_parts).reshape(length, width), grad_lin.reshape(length, qkv_cols)
    )
    project_pairs = after(grad_project.astype(bf16), *normed_sums)
    project_pairs = project_pairs.reshape(chips, 2, width // columns, qkv_cols)
    project_chip = cores_sum(project_pairs.transpose(1, 0, 2, 3))
    project_came = chips_exchange(project_chip)
    project_sum = jnp.sum(after(project_came, late[-1]).astype(f32), axis=0)
    grad_normed = add_wide([normed_parts[0], *after(normed_near, project_sum)])
    wide_row = add_low_all(after(wide_came, project_came))
    wide_sum = jnp.sum(chips_exchange(wide_row).astype(f32), axis=0)
    grad_out_w = wide_sum[:, :width]
    grad_router_w = wide_sum[:, width : width + experts]
    grad_gain_moe_w = wide_sum[:, width + experts]

    out_ring = add_low(after(out_hop, grad_lin), outs[2])
    for d in range(3, chips):
        out_ring = add_low(after(chip_shift(out_ring, 1), *normed_sums), outs[d])
    moe_out = add_wide([after(chip_shift(out_ring, 1), project_chip), outs[0]])
    block_out = mixed_rows + res_scale * moe_out

    totals = []
    for parts, came in zip(grads, late):
        total = reduce_total([after(parts[0], *normed_sums, project_chip)], came)
        totals.append(unpack_weights(join_halves(total, group_size), width // 4, ffe))
    grad_gate_w, grad_up_w, grad_down_w = (
        jnp.concatenate(arrays, axis=0) for arrays in zip(*totals)
    )

    own_w = jnp.concatenate([w_query, key_matrix, value_matrix], axis=1).astype(f32)
    own_gain = lax.dynamic_slice_in_dim(gain_attn[0], column * own_w.shape[0], own_w.shape[0], 0)
    gain_rows = (jnp.sum(project_sum * own_w, axis=1) / own_gain).reshape(4, -1)
    gain_rows = after(gain_rows, wide_sum)
    gain_sum = jnp.sum(lax.all_to_all(gain_rows, "rows", 0, 0, tiled=True), axis=0)
    grad_gain_attn = lax.ppermute(
        gain_sum,
        ("rows", "cols"),
        [(r * columns + c, 4 * c + r) for r in range(4) for c in range(columns)],
    )

    own_float = own_tokens.astype(f32)
    scale_attn = rms_scale(own_float)
    unit_attn = own_float * scale_attn
    grad_unit = grad_normed * gain_attn
    grad_tokens = grad_mixed + scale_attn * (
        grad_unit - unit_attn * jnp.mean(grad_unit * unit_attn, axis=-1, keepdims=True)
    )
    return (
        block_out[None],
        grad_tokens[None],
        project_sum[:, :q_cols],
        project_sum[:, q_cols : q_cols + k_cols],
        project_sum[:, q_cols + k_cols :],
        grad_out_w,
        grad_gain_attn,
        grad_gain_moe_w,
        grad_router_w,
        grad_gate_w,
        grad_up_w,
        grad_down_w,
    )


def solution(mesh):
    placed = (
        P("cols", "rows", None),
        P("cols", None),
        P("cols", "rows", None),
        P("cols", "rows"),
        P("cols", "rows"),
        P("cols", "rows"),
        P(("rows", "cols"), None),
        P(("rows", "cols")),
        P(("rows", "cols")),
        P(("rows", "cols"), None),
        P("cols", "rows", None),
        P("cols", "rows", None),
        P("cols", None, "rows"),
        P("cols", "rows", None),
    )
    return jax.shard_map(
        per_device,
        mesh=mesh,
        in_specs=placed,
        out_specs=(
            P("cols", "rows", None),
            P("cols", "rows", None),
            P("cols", "rows"),
            P("cols", "rows"),
            P("cols", "rows"),
            P(("rows", "cols"), None),
            P(("rows", "cols")),
            P(("rows", "cols")),
            P(("rows", "cols"), None),
            P("cols", "rows", None),
            P("cols", "rows", None),
            P("cols", None, "rows"),
        ),
        check_vma=False,
    )
```

```python
from functools import partial

import jax
import jax.numpy as jnp
from jax import lax
from jax.experimental import pallas as pl
from jax.experimental.pallas import tpu as pltpu
from jax.sharding import PartitionSpec as P

HEAD_SIZE = 64
LANES = 128
LONGEST_DOC = 768

res_scale = 0.22
att_scale = 0.015625
norm_eps = 1e-06
rope_base = 10000.0
masked_score = -1e30
log2_e = 1.4426950408889634
highest = lax.Precision.HIGHEST
bf16 = jnp.bfloat16
f32 = jnp.float32


def rms_scale(hidden_rows):
    return lax.rsqrt(jnp.mean(hidden_rows * hidden_rows, axis=-1, keepdims=True) + norm_eps)


def dot_nt(left, right):
    return lax.dot_general(left, right, (((1,), (1,)), ((), ())), preferred_element_type=f32)


def dot_tn(left, right):
    return lax.dot_general(left, right, (((0,), (0,)), ((), ())), preferred_element_type=f32)


def dot_nn(left, right):
    return jnp.dot(left, right, preferred_element_type=f32)


def rows_swap(array, distance):
    return lax.ppermute(array, "rows", [(i, i ^ distance) for i in range(4)])


def halves(array):
    axis = 0 if array.shape[0] % 2 == 0 else 1
    cut = array.shape[axis] // 2
    return (
        axis,
        lax.slice_in_dim(array, 0, cut, axis=axis),
        lax.slice_in_dim(array, cut, 2 * cut, axis=axis),
    )


def gather_near(array):
    return rows_swap(array, 1), rows_swap(array, 2)


def far_halves(from_x, from_y):
    _, first_y, _ = halves(from_y)
    _, _, second_x = halves(from_x)
    return rows_swap(first_y, 1), rows_swap(second_x, 2)


def join_far(array, from_x, from_y, far):
    return [array, from_x, from_y, jnp.concatenate(far, axis=halves(array)[0])]


def gather_far(array, from_x, from_y):
    return join_far(array, from_x, from_y, far_halves(from_x, from_y))


def rows_exchange(pieces):
    return [pieces[0]] + [rows_swap(pieces[j], j) for j in (1, 2, 3)]


def reduce_far(pieces):
    _, first, second = halves(pieces[3])
    return rows_swap(first, 1), rows_swap(second, 2)


def reduce_add(pieces, from_x, from_y):
    axis, first_x, second_x = halves(pieces[1])
    _, first_y, second_y = halves(pieces[2])
    return (
        jnp.concatenate([first_x, add_low(second_x, from_y)], axis=axis),
        jnp.concatenate([add_low(first_y, from_x), second_y], axis=axis),
    )


def reduce_near(to_x, to_y):
    return rows_swap(to_x, 1), rows_swap(to_y, 2)


def reduce_first(pieces):
    return rows_swap(pieces[3][0], 1), rows_swap(pieces[3][1], 2)


def reduce_second(pieces, far):
    return (
        jnp.concatenate([pieces[1][0], add_low(pieces[1][1], far[1])], axis=0),
        jnp.concatenate([add_low(pieces[2][0], far[0]), pieces[2][1]], axis=0),
    )


def reduce_total(pieces, late):
    return add_wide([jnp.concatenate(pieces[0], axis=0), *late])


def add_wide(arrays):
    return sum(array.astype(f32) for array in arrays)


def add_low_all(array):
    return jnp.sum(array.astype(f32), axis=0).astype(bf16)


def add_low(left, right):
    return (left.astype(f32) + right.astype(f32)).astype(bf16)


def chip_shift(array, distance):
    count = lax.axis_size("cols")
    return lax.ppermute(
        array, "cols", [(i, (i + 2 * distance) % count) for i in range(count)]
    )


def core_swap(array):
    count = lax.axis_size("cols")
    return lax.ppermute(array, "cols", [(i, i ^ 1) for i in range(count)])


def chips_gather(array):
    chips = lax.axis_size("cols") // 2
    return [array] + [chip_shift(array, d) for d in range(1, chips)]


def chips_in_order(array, chip):
    chips = array.shape[0]
    twice = jnp.concatenate([array[::-1]] * 2, axis=0)
    return lax.dynamic_slice_in_dim(twice, chips - 1 - chip, chips, 0)


def cores_sum(array):
    count = lax.axis_size("cols")
    pairs = [[i, i + 1] for i in range(0, count, 2)]
    came = lax.all_to_all(array, "cols", 0, 0, axis_index_groups=pairs, tiled=True)
    return add_low(came[0], came[1])


def chips_exchange(array):
    count = lax.axis_size("cols")
    alike = [list(range(core, count, 2)) for core in range(2)]
    return lax.all_to_all(array, "cols", 0, 0, axis_index_groups=alike, tiled=True)


def cores_in_order(mine, other, core, axis):
    return jnp.stack(
        [jnp.where(core == 0, mine, other), jnp.where(core == 0, other, mine)], axis=axis
    )


def call_params(mebibytes):
    return pltpu.CompilerParams(vmem_limit_bytes=mebibytes * 1024 * 1024)


def cost(micros):
    return pl.CostEstimate(flops=int(micros * 1.15e9), bytes_accessed=0, transcendentals=0)


def turn(rows, cosine, sine):
    lane = lax.broadcasted_iota(jnp.int32, rows.shape, 1)
    partner = jnp.where(
        (lane & (HEAD_SIZE - 1)) < HEAD_SIZE // 2,
        pltpu.roll(rows, LANES - HEAD_SIZE // 2, 1),
        pltpu.roll(rows, HEAD_SIZE // 2, 1),
    )
    return rows * cosine + partner * sine


def project_kernel(meta, *refs):
    parts, found, swapped, gain, cosine, sine = refs[:4], refs[4], refs[5], *refs[6:9]
    q_out, k_out, v_out, n_out, w_out = refs[9:]
    step = pl.program_id(0)
    chips, rows, _ = found.shape
    chip = meta[1]

    @pl.when(step == 0)
    def _():
        first_core = meta[2] == 0
        for d in range(chips):
            mine, other = found[d], swapped[d]
            here = pl.multiple_of(lax.rem(chip + chips - d, chips) * (2 * rows), 2 * rows)
            w_out[pl.ds(here, 2 * rows), :] = jnp.concatenate(
                [jnp.where(first_core, mine, other), jnp.where(first_core, other, mine)], axis=0
            )

    for index, part in enumerate(parts):

        @pl.when(step == index)
        def _(part=part):
            rows = part[...].astype(f32)
            n_out[0] = (rows * rms_scale(rows) * gain[...]).astype(bf16)

    linear = dot_nn(n_out[0], w_out[...])
    q_cols, k_cols = q_out.shape[1], k_out.shape[1]
    cos_rows, sin_rows = cosine[...], sine[...]
    turned = jnp.concatenate(
        [
            turn(linear[:, at : at + LANES], cos_rows, sin_rows)
            for at in range(0, q_cols + k_cols, LANES)
        ],
        axis=1,
    ).astype(bf16)
    q_out[...] = turned[:, :q_cols]
    k_out[...] = turned[:, q_cols:]
    v_out[...] = linear[:, q_cols + k_cols :].astype(bf16)


def project(meta, parts, found, swapped, gain, cosine, sine, q_cols, k_cols):
    tok, width = parts[0].shape
    length = 4 * tok
    whole = pl.BlockSpec(memory_space=pltpu.VMEM)

    def natural(step, meta):
        return (step ^ meta[0], 0)

    return pl.pallas_call(
        project_kernel,
        grid_spec=pltpu.PrefetchScalarGridSpec(
            num_scalar_prefetch=1,
            grid=(4,),
            in_specs=[whole] * 7
            + [pl.BlockSpec((tok, LANES), natural), pl.BlockSpec((tok, LANES), natural)],
            out_specs=[
                pl.BlockSpec((tok, q_cols), natural),
                pl.BlockSpec((tok, k_cols), natural),
                pl.BlockSpec((tok, k_cols), natural),
                pl.BlockSpec((1, tok, width), lambda step, meta: (step, 0, 0)),
                pl.BlockSpec((width, q_cols + 2 * k_cols), lambda step, meta: (0, 0)),
            ],
        ),
        out_shape=[
            jax.ShapeDtypeStruct((length, q_cols), bf16),
            jax.ShapeDtypeStruct((length, k_cols), bf16),
            jax.ShapeDtypeStruct((length, k_cols), bf16),
            jax.ShapeDtypeStruct((4, tok, width), bf16),
            jax.ShapeDtypeStruct((width, q_cols + 2 * k_cols), bf16),
        ],
        compiler_params=call_params(32),
        cost_estimate=cost(10),
        name="project",
    )(meta, *parts, found, swapped, gain, cosine, sine)


def attend_kernel(meta, queries, keys, values, starts, out, lse, *, bands):
    block = pl.program_id(0)
    rows = queries.shape[0]
    first = meta[3 + block]
    heads = queries.shape[1] // HEAD_SIZE
    group = queries.shape[1] // keys.shape[1]
    for band in range(1, bands + 1):

        @pl.when(block - first + 1 == band)
        def _(band=band):
            width = band * rows
            base = pl.multiple_of(first * rows, rows)
            key_band = keys[pl.ds(base, width), :]
            value_band = values[pl.ds(base, width), :]
            query_pos = block * rows + lax.broadcasted_iota(jnp.int32, (rows, width), 0)
            key_pos = base + lax.broadcasted_iota(jnp.int32, (rows, width), 1)
            allowed = (key_pos >= starts[...]) & (key_pos <= query_pos)
            results = []
            for head in range(heads):
                at = head // group * HEAD_SIZE
                scores = dot_nt(
                    queries[:, head * HEAD_SIZE : (head + 1) * HEAD_SIZE],
                    key_band[:, at : at + HEAD_SIZE],
                )
                scores = jnp.where(allowed, scores, masked_score)
                top = jnp.max(scores, axis=1, keepdims=True)
                weights = jnp.exp2((scores - top) * (att_scale * log2_e))
                total = jnp.sum(weights, axis=1, keepdims=True)
                result = dot_nn(weights.astype(bf16), value_band[:, at : at + HEAD_SIZE])
                results.append(result * (1.0 / total))
                lse[:, head : head + 1] = top * (att_scale * log2_e) + jnp.log2(total)
            out[0] = jnp.concatenate(results, axis=1).astype(bf16)


def attend(meta, queries, keys, values, starts, tok):
    length, q_cols = queries.shape
    k_cols = keys.shape[1]
    blocks = length // tok
    whole = pl.BlockSpec(memory_space=pltpu.VMEM)
    return pl.pallas_call(
        partial(attend_kernel, bands=min(blocks, LONGEST_DOC // tok + 1)),
        grid_spec=pltpu.PrefetchScalarGridSpec(
            num_scalar_prefetch=1,
            grid=(blocks,),
            in_specs=[
                pl.BlockSpec((tok, q_cols), lambda i, meta: (i, 0)),
                whole,
                whole,
                pl.BlockSpec((tok, 1), lambda i, meta: (i, 0)),
            ],
            out_specs=[
                pl.BlockSpec((1, tok, q_cols), lambda i, meta: (i, 0, 0)),
                pl.BlockSpec((tok, 8), lambda i, meta: (i, 0)),
            ],
        ),
        out_shape=[
            jax.ShapeDtypeStruct((blocks, tok, q_cols), bf16),
            jax.ShapeDtypeStruct((length, 8), f32),
        ],
        compiler_params=call_params(32),
        cost_estimate=cost(5),
        name="attend",
    )(meta, queries, keys, values, starts)


def attend_back_kernel(
    meta, queries, grads, lse, starts, keys, values, cosine, sine, out, key_sum, value_sum, *, bands
):
    block = pl.program_id(0)
    rows = queries.shape[0]
    first = meta[3 + block]
    q_cols, k_cols = queries.shape[1], keys.shape[1]
    heads = q_cols // HEAD_SIZE
    group = q_cols // k_cols

    @pl.when(block == 0)
    def _():
        key_sum[...] = jnp.zeros_like(key_sum)
        value_sum[...] = jnp.zeros_like(value_sum)

    for band in range(1, bands + 1):

        @pl.when(block - first + 1 == band)
        def _(band=band):
            width = band * rows
            base = pl.multiple_of(first * rows, rows)
            key_band = keys[pl.ds(base, width), :]
            value_band = values[pl.ds(base, width), :]
            key_pos = base + lax.broadcasted_iota(jnp.int32, (width, rows), 0)
            query_pos = block * rows + lax.broadcasted_iota(jnp.int32, (width, rows), 1)
            allowed = (key_pos >= starts[...]) & (key_pos <= query_pos)
            query_grads, key_parts, value_parts = [], [], []
            for kv_head in range(k_cols // HEAD_SIZE):
                at = kv_head * HEAD_SIZE
                key_rows = key_band[:, at : at + HEAD_SIZE]
                value_rows = value_band[:, at : at + HEAD_SIZE]
                key_part = jnp.zeros((width, HEAD_SIZE), f32)
                value_part = jnp.zeros((width, HEAD_SIZE), f32)
                for head in range(kv_head * group, (kv_head + 1) * group):
                    query_rows = queries[:, head * HEAD_SIZE : (head + 1) * HEAD_SIZE]
                    grad_rows = grads[0, :, head * HEAD_SIZE : (head + 1) * HEAD_SIZE]
                    scores = dot_nt(key_rows, query_rows)
                    probs = jnp.where(
                        allowed,
                        jnp.exp2(scores * (att_scale * log2_e) - lse[head : head + 1, :]),
                        0.0,
                    )
                    grad_probs = dot_nt(value_rows, grad_rows)
                    delta = jnp.sum(probs * grad_probs, axis=0, keepdims=True)
                    grad_scores = (probs * (grad_probs - delta)).astype(bf16)
                    value_part += dot_nn(probs.astype(bf16), grad_rows)
                    key_part += dot_nn(grad_scores, query_rows)
                    query_grads.append(dot_tn(grad_scores, key_rows))
                key_parts.append(key_part)
                value_parts.append(value_part)
            key_sum[pl.ds(base, width), :] += jnp.concatenate(key_parts, axis=1)
            value_sum[pl.ds(base, width), :] += jnp.concatenate(value_parts, axis=1)
            here = pl.ds(pl.multiple_of(block * rows, rows), rows)
            query_grad = jnp.concatenate(query_grads, axis=1) * att_scale
            turned = [
                turn(query_grad[:, c : c + LANES], cosine[here, :], -sine[here, :])
                for c in range(0, q_cols, LANES)
            ]
            out[block ^ meta[0], :, :q_cols] = jnp.concatenate(turned, axis=1).astype(bf16)

    @pl.when(block == pl.num_programs(0) - 1)
    def _():
        for part in range(4):
            here = pl.ds(pl.multiple_of((meta[0] ^ part) * rows, rows), rows)
            key_grad = key_sum[here, :] * att_scale
            turned = [
                turn(key_grad[:, c : c + LANES], cosine[here, :], -sine[here, :])
                for c in range(0, k_cols, LANES)
            ]
            out[part, :, q_cols : q_cols + k_cols] = jnp.concatenate(turned, axis=1).astype(bf16)
            out[part, :, q_cols + k_cols :] = value_sum[here, :].astype(bf16)


def attend_back(meta, queries, grads, lse, starts, keys, values, cosine, sine, tok):
    length, q_cols = queries.shape
    k_cols = keys.shape[1]
    blocks = length // tok
    whole = pl.BlockSpec(memory_space=pltpu.VMEM)
    return pl.pallas_call(
        partial(attend_back_kernel, bands=min(blocks, LONGEST_DOC // tok + 1)),
        grid_spec=pltpu.PrefetchScalarGridSpec(
            num_scalar_prefetch=1,
            grid=(blocks,),
            in_specs=[
                pl.BlockSpec((tok, q_cols), lambda i, meta: (i, 0)),
                pl.BlockSpec((1, tok, q_cols), lambda i, meta: (i, 0, 0)),
                pl.BlockSpec((8, tok), lambda i, meta: (0, i)),
                pl.BlockSpec((1, tok), lambda i, meta: (0, i)),
                whole,
                whole,
                whole,
                whole,
            ],
            out_specs=pl.BlockSpec(
                (blocks, tok, q_cols + 2 * k_cols), lambda i, meta: (0, 0, 0)
            ),
            scratch_shapes=[
                pltpu.VMEM((length, k_cols), f32),
                pltpu.VMEM((length, k_cols), f32),
            ],
        ),
        out_shape=jax.ShapeDtypeStruct((blocks, tok, q_cols + 2 * k_cols), bf16),
        compiler_params=call_params(40),
        cost_estimate=cost(29),
        name="attend_back",
    )(meta, queries, grads, lse, starts, keys, values, cosine, sine)


def low_pair(values):
    high = values.astype(bf16)
    return high, (values - high.astype(f32)).astype(bf16)


def mix_kernel(
    meta, heads, out_parts, tokens, member, gain, router, mixed_out, rows_out, gates_out, *, experts
):
    width = tokens.shape[1]
    branch = sum(dot_nn(heads[meta[0] ^ part], out_parts[part]) for part in range(4))
    mixed = tokens[...].astype(f32) + res_scale * branch
    mixed_out[...] = mixed
    normed = (mixed * rms_scale(mixed) * gain[...]).astype(bf16)
    logits = dot_nn(normed, router[...])
    named = member[...] > 0
    logits = jnp.where(named, logits, masked_score)
    lifted = jnp.exp(logits - jnp.max(logits, axis=1, keepdims=True))
    lifted = jnp.where(named, lifted, 0.0)
    gates = lifted * (1.0 / jnp.sum(lifted, axis=1, keepdims=True))
    gates_out[...] = gates
    high, low = low_pair(gates)
    low = pltpu.roll(low.astype(f32), experts, 1)
    rows_out[:, :width] = normed
    rows_out[:, width:] = (high.astype(f32) + low).astype(bf16)


def mix(meta, heads, out_parts, tokens, member, gain, router, experts):
    tok, width = tokens.shape
    whole = pl.BlockSpec(memory_space=pltpu.VMEM)
    return pl.pallas_call(
        partial(mix_kernel, experts=experts),
        in_specs=[pl.BlockSpec(memory_space=pltpu.SMEM)] + [whole] * 6,
        out_specs=[whole] * 3,
        out_shape=[
            jax.ShapeDtypeStruct((tok, width), f32),
            jax.ShapeDtypeStruct((tok, width + LANES), bf16),
            jax.ShapeDtypeStruct((tok, LANES), f32),
        ],
        compiler_params=call_params(40),
        cost_estimate=cost(6),
        name="mix",
    )(meta, heads, out_parts, tokens, member, gain, router)


def unmix_kernel(
    meta, came, last, mixed_in, cotangent, gates, gain, router, out_parts, heads,
    mixed_grad, heads_out, mine_out, other_out, *, experts
):
    width = cotangent.shape[1]
    summed = came[...].astype(f32) + last[...].astype(f32)
    beside = summed[:, width:]
    lane = lax.broadcasted_iota(jnp.int32, beside.shape, 1)
    weighted = jnp.where(lane < experts, beside + pltpu.roll(beside, LANES - experts, 1), 0.0)
    logit_grads = weighted - gates[...] * jnp.sum(weighted, axis=1, keepdims=True)
    high, low = low_pair(logit_grads)
    normed_grad = summed[:, :width] + dot_nt(high, router[...]) + dot_nt(low, router[...])
    mixed = mixed_in[...]
    scale = rms_scale(mixed)
    unit = mixed * scale
    normed = (unit * gain[...]).astype(bf16)
    one_lane = lax.broadcasted_iota(jnp.int32, (unit.shape[0], LANES), 1) == experts
    one_lane = one_lane.astype(f32).astype(bf16)
    gain_high, gain_low = low_pair(normed_grad * unit)
    shares = dot_tn(normed, high) + dot_tn(normed, low)
    shares = (shares + dot_tn(gain_high, one_lane) + dot_tn(gain_low, one_lane)).astype(bf16)
    unit_grad = normed_grad * gain[...]
    grad = cotangent[...].astype(f32) + scale * (
        unit_grad - unit * jnp.mean(unit_grad * unit, axis=-1, keepdims=True)
    )
    mixed_grad[...] = grad
    branch = (res_scale * grad).astype(bf16)
    for part in range(4):
        heads_out[meta[0] ^ part] = dot_nt(branch, out_parts[part]).astype(bf16)
    first_core = meta[2] == 0
    _, chips, sixth, _ = mine_out.shape
    tok = branch.shape[0]
    for part in range(4):
        wide = dot_tn(heads[part], branch).astype(bf16)
        wide = jnp.concatenate([wide, shares[part * tok : (part + 1) * tok]], axis=1)
        for chip in range(chips):
            at = 2 * chip * sixth
            even, odd = wide[at : at + sixth], wide[at + sixth : at + 2 * sixth]
            mine_out[part, chip] = jnp.where(first_core, even, odd)
            other_out[part, chip] = jnp.where(first_core, odd, even)


def unmix(meta, came, last, mixed, cotangent, gates, gain, router, out_parts, heads, experts, chips):
    tok, width = mixed.shape
    wide = (4, chips, tok // (2 * chips), width + LANES)
    whole = pl.BlockSpec(memory_space=pltpu.VMEM)
    return pl.pallas_call(
        partial(unmix_kernel, experts=experts),
        in_specs=[pl.BlockSpec(memory_space=pltpu.SMEM)] + [whole] * 9,
        out_specs=[whole] * 4,
        out_shape=[
            jax.ShapeDtypeStruct((tok, width), f32),
            jax.ShapeDtypeStruct((4, tok, out_parts.shape[1]), bf16),
            jax.ShapeDtypeStruct(wide, bf16),
            jax.ShapeDtypeStruct(wide, bf16),
        ],
        compiler_params=call_params(32),
        cost_estimate=cost(12),
        name="unmix",
    )(meta, came, last, mixed, cotangent, gates, gain, router, out_parts, heads)


def hidden_weights(parts, cut, ffe):
    tiles = 2 * ffe // LANES
    return jnp.concatenate(
        [
            jnp.concatenate([ref[0, t * cut : (t + 1) * cut, :] for t in range(tiles)], axis=1)
            for ref in parts
        ],
        axis=0,
    )


def down_weights(parts, cut, ffe):
    first = 2 * ffe // LANES * cut
    return jnp.concatenate(
        [
            ref[0, first + t * ffe : first + (t + 1) * ffe, :]
            for ref in parts
            for t in range(cut // LANES)
        ],
        axis=1,
    )


def experts_kernel(meta, *refs, experts, slots, local, final, earlier):
    blocks = 4
    x_refs, g_refs, refs = refs[:blocks], refs[blocks : 2 * blocks], refs[2 * blocks :]
    early, refs = refs[:earlier], refs[earlier:]
    parts, refs = refs[:4], refs[4:]
    returned_out, refs = refs[: blocks * final], refs[blocks * final :]
    x_out, g_out, active_out, grads_out, out_kept, dx_kept, t_kept, refs = *refs[:7], refs[7:]
    x_rows, g_rows, gate_kept, rows_sent, x_here, g_here, arrived, refs = *refs[:7], refs[7:]
    own = pl.program_id(0)
    own_count = x_rows.shape[0]
    tok = x_refs[0].shape[0]
    width = x_rows.shape[2]
    cut = width // 4
    ffe = active_out.shape[2]
    row, first_expert = meta[0], meta[1]
    loads = [
        (
            pltpu.make_async_copy(x_refs[block], x_here.at[block % 2], arrived.at[0, block % 2]),
            pltpu.make_async_copy(g_refs[block], g_here.at[block % 2], arrived.at[1, block % 2]),
        )
        for block in range(blocks)
    ]
    if final:
        ranks_kept, returned, sent, refs = *refs[:3], refs[3:]
    fetches = [
        [
            pltpu.make_async_copy(
                early[which].at[:, pl.ds(block * slots, slots), :],
                refs[which].at[block % 2],
                refs[3].at[which, block % 2],
            )
            for which in range(earlier)
        ]
        for block in range(blocks)
    ]
    row_copies = [
        pltpu.make_async_copy(x_rows, x_out, rows_sent.at[0]),
        pltpu.make_async_copy(g_rows, g_out, rows_sent.at[1]),
    ]

    def columns(part, start=0):
        return pl.ds(pl.multiple_of(start + (row ^ part) * cut, LANES), cut)

    @pl.when(own == 0)
    def _():
        for load in loads[0]:
            load.start()
        slot = lax.broadcasted_iota(jnp.int32, (slots, tok), 0).astype(f32)
        lower = (
            lax.broadcasted_iota(jnp.int32, (tok, tok), 0)
            > lax.broadcasted_iota(jnp.int32, (tok, tok), 1)
        ).astype(f32).astype(bf16)
        source = lax.broadcasted_iota(jnp.int32, (LANES, LANES), 1)
        target = lax.broadcasted_iota(jnp.int32, (LANES, LANES), 0)
        choose = (source == target + first_expert).astype(f32).astype(bf16)
        for block in range(blocks):
            for load in loads[block + 1] if block + 1 < blocks else ():
                load.start()
            for load in loads[block]:
                load.wait()
            x_block, g_block = x_here.at[block % 2], g_here.at[block % 2]
            member = g_block[:, width:]
            rank = jnp.where(member > 0, dot_nn(lower, member), -1.0).astype(bf16)
            if final:
                ranks_kept[block] = dot_nt(rank, choose)
            rank_rows = dot_nt(choose, rank)
            pick = jnp.concatenate(
                [
                    (rank_rows[index : index + 1, :] == slot).astype(f32).astype(bf16)
                    for index in range(local, local + own_count)
                ],
                axis=0,
            )
            beside = dot_nn(pick, x_block[:, width:])
            lane = lax.broadcasted_iota(jnp.int32, beside.shape, 1)
            named = lax.broadcasted_iota(jnp.int32, beside.shape, 0) // slots
            named = named + first_expert + local
            gates = jnp.sum(
                jnp.where((lane == named) | (lane == named + experts), beside, 0.0),
                axis=1,
                keepdims=True,
            )
            here = slice(block * slots, (block + 1) * slots)
            x_part = dot_nn(pick, x_block[:, :width]).astype(bf16)
            g_part = dot_nn(pick, g_block[:, :width]).astype(bf16)
            for index in range(own_count):
                rows = slice(index * slots, (index + 1) * slots)
                gate_kept[index, here, :] = gates[rows]
                for part in range(4):
                    there = slice(part * cut, (part + 1) * cut)
                    x_rows[index, here, columns(part)] = x_part[rows, there]
                    g_rows[index, here, columns(part)] = g_part[rows, there]
        for copy in row_copies:
            copy.start()

    @pl.when(own == own_count - 1)
    def _():
        for fetch in fetches[0] + fetches[1]:
            fetch.start()

    hidden_w = hidden_weights(parts, cut, ffe)
    down_w = down_weights(parts, cut, ffe)
    hidden = dot_nn(x_rows[own], hidden_w)
    hidden_gate, hidden_up = hidden[:, :ffe], hidden[:, ffe:]
    gates = gate_kept[own]
    grad_active = dot_nt(g_rows[own], down_w) * (res_scale * gates)
    sigmoid = jax.nn.sigmoid(hidden_gate)
    silu = hidden_gate * sigmoid
    active = silu * hidden_up
    gated = (active * gates).astype(bf16)
    grad_gate = grad_active * hidden_up * (sigmoid * (1.0 + hidden_gate * (1.0 - sigmoid)))
    grads = jnp.concatenate(
        [grad_gate.astype(bf16), (grad_active * silu).astype(bf16)], axis=1
    )
    weighted = jnp.sum(active * grad_active, axis=1, keepdims=True)
    active_out[0] = gated
    grads_out[0] = grads
    kept = own if final else 0
    out_kept[kept] = dot_nn(gated, down_w).astype(bf16)
    dx_kept[kept] = dot_nt(grads, hidden_w).astype(bf16)
    weighted_high = weighted.astype(bf16).astype(f32)
    lane = lax.broadcasted_iota(jnp.int32, (blocks * slots, LANES), 1)
    named = first_expert + local + own
    t_kept[kept] = jnp.where(
        lane == named,
        weighted_high,
        jnp.where(lane == named + experts, weighted - weighted_high, 0.0),
    ).astype(bf16)

    @pl.when(own == own_count - 1)
    def _():
        if final:
            slot = lax.broadcasted_iota(jnp.int32, (tok, slots), 1).astype(f32)
            gives = [
                pltpu.make_async_copy(
                    returned.at[block % 2], returned_out[block], sent.at[block]
                )
                for block in range(blocks)
            ]
            for block in range(blocks):
                here = slice(block * slots, (block + 1) * slots)
                put = jnp.concatenate(
                    [
                        (ranks_kept[block, :, index : index + 1] == slot).astype(f32).astype(bf16)
                        for index in range(local + own_count)
                    ],
                    axis=1,
                )

                def rows_of(which, here=here, block=block):
                    kept_rows = (out_kept, dx_kept, t_kept)[which]
                    found = [refs[which][block % 2, index] for index in range(local)]
                    found += [kept_rows[index, here, :] for index in range(own_count)]
                    return jnp.concatenate(found, axis=0)

                for fetch in fetches[block]:
                    fetch.wait()
                if block >= 2:
                    gives[block - 2].wait()
                out = dot_nn(put, rows_of(0)).astype(bf16)
                dx = dot_nn(put, rows_of(1)).astype(bf16)
                for part in range(4):
                    there = slice(part * cut, (part + 1) * cut)
                    returned[block % 2, :, columns(part)] = out[:, there]
                    returned[block % 2, :, columns(part, width)] = dx[:, there]
                returned[block % 2, :, 2 * width :] = dot_nn(put, rows_of(2)).astype(bf16)
                gives[block].start()
                for fetch in fetches[block + 2] if block + 2 < blocks else ():
                    fetch.start()
            for give in gives[-2:]:
                give.wait()
        for copy in row_copies:
            copy.wait()


def run_experts(meta, x_blocks, g_blocks, early, parts, ffe, experts, slots, local, final):
    blocks = len(x_blocks)
    tok, padded = x_blocks[0].shape
    width = padded - LANES
    own, packed, _ = parts[0].shape
    rows = blocks * slots
    anywhere = pl.BlockSpec(memory_space=pl.ANY)
    back = 2 * width + LANES
    kept_shapes = [(own, rows, width), (own, rows, width), (own, rows, LANES)]
    row_shapes = [(own, rows, width), (own, rows, width), (own, rows, ffe), (own, rows, 2 * ffe)]

    def one(*shape):
        return pl.BlockSpec((1,) + shape, lambda e, meta: (e, 0, 0))

    out_specs = [anywhere] * 2 + [one(rows, ffe), one(rows, 2 * ffe)]
    out_shapes = [jax.ShapeDtypeStruct(shape, bf16) for shape in row_shapes]
    scratch = []
    if final:
        out_specs = [anywhere] * blocks + out_specs
        out_shapes = [jax.ShapeDtypeStruct((tok, back), bf16)] * blocks + out_shapes
        scratch += [pltpu.VMEM(shape, bf16) for shape in kept_shapes]
    else:
        out_specs += [one(*shape[1:]) for shape in kept_shapes]
        out_shapes += [jax.ShapeDtypeStruct(shape, bf16) for shape in kept_shapes]
    scratch += [
        pltpu.VMEM((own, rows, width), bf16),
        pltpu.VMEM((own, rows, width), bf16),
        pltpu.VMEM((own, rows, 1), f32),
        pltpu.SemaphoreType.DMA((2,)),
        pltpu.VMEM((2, tok, padded), bf16),
        pltpu.VMEM((2, tok, padded), bf16),
        pltpu.SemaphoreType.DMA((2, 2)),
    ]
    if final:
        scratch += [
            pltpu.VMEM((blocks, tok, LANES), f32),
            pltpu.VMEM((2, tok, back), bf16),
            pltpu.SemaphoreType.DMA((blocks,)),
        ]
    if early:
        scratch += [
            pltpu.VMEM((2, array.shape[0], slots, array.shape[2]), bf16) for array in early
        ] + [pltpu.SemaphoreType.DMA((3, 2))]
    return pl.pallas_call(
        partial(
            experts_kernel,
            experts=experts,
            slots=slots,
            local=local,
            final=final,
            earlier=len(early),
        ),
        grid_spec=pltpu.PrefetchScalarGridSpec(
            num_scalar_prefetch=1,
            grid=(own,),
            in_specs=[anywhere] * (2 * blocks + len(early)) + [one(packed, LANES)] * 4,
            out_specs=out_specs,
            scratch_shapes=scratch,
        ),
        out_shape=out_shapes,
        compiler_params=call_params(60),
        cost_estimate=cost(4),
        name="experts",
    )(meta, *x_blocks, *g_blocks, *early, *parts)


def weight_grad_kernel(*refs, chunks, own_count):
    x_refs, grad_refs, active_refs, g_refs = (
        refs[chunks * index : chunks * (index + 1)] for index in range(4)
    )
    refs = refs[4 * chunks :]
    outs, (made, sent) = refs[: 4 * own_count], refs[4 * own_count :]
    x_rows = jnp.concatenate([ref[0] for ref in x_refs], axis=0)
    grads = jnp.concatenate([ref[0] for ref in grad_refs], axis=0)
    active = jnp.concatenate([ref[0] for ref in active_refs], axis=0)
    g_rows = jnp.concatenate([ref[0] for ref in g_refs], axis=0)
    cut = x_rows.shape[1] // 4
    ffe = grads.shape[1] // 2
    first = 2 * ffe // LANES * cut
    own = pl.program_id(0)
    for part in range(4):
        hidden = dot_tn(x_rows[:, part * cut : (part + 1) * cut], grads).astype(bf16)
        for t in range(2 * ffe // LANES):
            made[own, part, t * cut : (t + 1) * cut, :] = hidden[:, t * LANES : (t + 1) * LANES]
    down = (dot_tn(active, g_rows) * res_scale).astype(bf16)
    for part in range(4):
        for t in range(cut // LANES):
            at = part * cut + t * LANES
            here = slice(first + t * ffe, first + (t + 1) * ffe)
            made[own, part, here, :] = down[:, at : at + LANES]
    copies = [
        [
            pltpu.make_async_copy(
                made.at[expert, part], outs[part * own_count + expert].at[0], sent.at[expert, part]
            )
            for part in range(4)
        ]
        for expert in range(own_count)
    ]
    for expert in range(own_count):

        @pl.when(own == expert)
        def _(expert=expert):
            for copy in copies[expert]:
                copy.start()

    @pl.when(own == own_count - 1)
    def _():
        for group in copies:
            for copy in group:
                copy.wait()


def weight_grads(x_chunks, grad_chunks, active_chunks, g_chunks):
    own, rows, width = x_chunks[0].shape
    ffe = active_chunks[0].shape[2]
    chunks = len(x_chunks)
    packed = 3 * ffe * (width // 4) // LANES

    def one(*shape):
        return pl.BlockSpec((1,) + shape, lambda e: (e, 0, 0))

    outs = pl.pallas_call(
        partial(weight_grad_kernel, chunks=chunks, own_count=own),
        grid=(own,),
        in_specs=[one(rows, width)] * chunks
        + [one(rows, 2 * ffe)] * chunks
        + [one(rows, ffe)] * chunks
        + [one(rows, width)] * chunks,
        out_specs=[pl.BlockSpec(memory_space=pl.ANY)] * (4 * own),
        out_shape=[jax.ShapeDtypeStruct((1, packed, LANES), bf16)] * (4 * own),
        scratch_shapes=[
            pltpu.VMEM((own, 4, packed, LANES), bf16),
            pltpu.SemaphoreType.DMA((own, 4)),
        ],
        compiler_params=call_params(60),
        cost_estimate=cost(13),
        name="weight_grads",
    )(*x_chunks, *grad_chunks, *active_chunks, *g_chunks)
    return [list(outs[part * own : (part + 1) * own]) for part in range(4)]


def two_halves(arrays):
    return arrays if len(arrays) == 2 else list(halves(arrays[0])[1:])


def join_halves(array, own):
    return array.reshape(own, 2 * array.shape[1] // own, array.shape[2])


def pack_weights(gate, up, down):
    return jnp.concatenate(
        [
            lax.slice_in_dim(array, at, at + LANES, axis=2)
            for array in (gate, up, down)
            for at in range(0, array.shape[2], LANES)
        ],
        axis=1,
    )


def unpack_weights(packed, cut, ffe):
    tiles = ffe // LANES

    def beside(first, rows, count):
        return jnp.concatenate(
            [packed[:, first + t * rows : first + (t + 1) * rows, :] for t in range(count)], axis=2
        )

    return (
        beside(0, cut, tiles),
        beside(tiles * cut, cut, tiles),
        beside(2 * tiles * cut, ffe, cut // LANES),
    )


def after(array, *earlier):
    return lax.optimization_barrier((array, earlier))[0]


def per_device(
    tokens,
    segment_ids,
    expert_ids,
    w_query,
    key_matrix,
    value_matrix,
    w_out,
    norm_attn,
    norm_moe,
    w_router,
    w_gate,
    w_up,
    w_down,
    cotangent,
):
    row = lax.axis_index("rows")
    column = lax.axis_index("cols")
    columns = lax.axis_size("cols")
    chips = columns // 2
    chip, core = column // 2, column % 2
    own_tokens = tokens[0]
    tok, width = own_tokens.shape
    own_experts = w_gate.shape[0]
    experts = own_experts * columns
    top_count = expert_ids.shape[2]
    capacity = 5 * tok * top_count // (4 * experts)
    slots = -(-capacity // LANES) * LANES
    q_cols, k_cols = w_query.shape[1], key_matrix.shape[1]

    token_near = gather_near(own_tokens)
    qkv_cols = q_cols + 2 * k_cols
    sixth = w_out.shape[0]
    found = chips_gather(
        jnp.concatenate(
            [w_query, key_matrix, value_matrix, w_out.reshape(4 * sixth, width // 4)], axis=1
        )
    )
    small = jnp.concatenate(
        [
            w_router,
            norm_attn[:, None],
            norm_moe[:, None],
            jnp.zeros((w_router.shape[0], LANES - experts - 2), bf16),
        ],
        axis=1,
    )
    small_full = lax.all_to_all(
        jnp.tile(small, (4 * columns, 1)), ("rows", "cols"), 0, 0, tiled=True
    )
    gain_attn = small_full[:, experts].astype(f32)[None, :]
    gain_moe = small_full[:, experts + 1].astype(f32)[None, :]
    router_full = jnp.where(jnp.arange(LANES) < experts, small_full, 0)
    token_parts = gather_far(own_tokens, *token_near)
    found = after(found, token_parts[3])
    project_found = jnp.stack([rows[:, :qkv_cols] for rows in found])
    project_swapped = core_swap(project_found)

    expert_rows = expert_ids[0]
    lane_range = jnp.arange(LANES, dtype=jnp.int32)
    member = jnp.any(expert_rows[:, :, None] == lane_range[None, None, :], axis=1).astype(bf16)
    cot_rows = jnp.concatenate([cotangent[0], member], axis=1)
    cot_same = [cot_rows, chip_shift(after(cot_rows, found[1:], token_parts[3]), 1)]

    groups = 2 if own_experts % 2 == 0 else 1
    group_size = own_experts // groups
    packed = []
    for group in range(groups):
        here = slice(group * group_size, (group + 1) * group_size)
        packed.append(pack_weights(after(w_gate[here], own_tokens), w_up[here], w_down[here]))
    weight_near = [gather_near(after(packed[0], token_parts[3], project_swapped))]

    segments = segment_ids[0]
    length = segments.shape[0]
    starts = jnp.sum((segments[None, :] < segments[:, None]).astype(jnp.int32), axis=1)
    positions = (jnp.arange(length, dtype=jnp.int32) - starts).astype(f32)
    half = HEAD_SIZE // 2
    frequency = rope_base ** (-(2.0 * jnp.arange(half, dtype=f32)) / HEAD_SIZE)
    angles = positions[:, None] * frequency[None, :]
    cos_half, sin_half = jnp.cos(angles), jnp.sin(angles)
    cosine = jnp.concatenate([cos_half] * 4, axis=1)
    sine = jnp.concatenate([-sin_half, sin_half] * 2, axis=1)
    first_blocks = starts[::tok] // tok
    place = jnp.stack([row, chip, core])
    meta = jnp.concatenate([place.astype(jnp.int32), first_blocks.astype(jnp.int32)])

    queries, key_rows, value_rows, normed, project_w = project(
        meta, token_parts, project_found, project_swapped, gain_attn, cosine, sine, q_cols, k_cols
    )
    found = after(found, queries)
    out_half = jnp.stack([rows[:, qkv_cols:].reshape(sixth, width) for rows in found])
    out_half = chips_in_order(out_half, chip).reshape(chips * sixth, width)
    out_near = gather_near(out_half)
    attended, lse = attend(meta, queries, key_rows, value_rows, starts[:, None], tok)
    cot_same[1] = after(cot_same[1], attended)
    cot_same.append(chip_shift(cot_same[1], 1))
    out_near = after(out_near, weight_near[0], attended)
    attended = after(attended, weight_near[0], cot_same[1])
    own_heads = lax.all_to_all(attended, "rows", 0, 0, tiled=True)
    out_mine = jnp.stack(gather_far(out_half, *out_near)).reshape(4, chips, sixth, width)
    out_mine = after(out_mine, cot_same[2])
    out_parts = cores_in_order(out_mine, core_swap(out_mine), core, 2).reshape(4, tok, width)
    weight_near[0] = after(weight_near[0], own_heads)
    first_far = far_halves(*weight_near[0])
    mixed_rows, moe_rows, gates = mix(
        meta,
        own_heads,
        out_parts,
        own_tokens,
        member,
        gain_moe,
        router_full,
        experts,
    )
    weight_parts = [join_far(packed[0], *weight_near[0], after(first_far, moe_rows))]
    for group in range(1, groups):
        weight_near.append(gather_near(after(packed[group], weight_parts[0][3])))
    cot_other = [core_swap(after(rows, own_heads)) for rows in cot_same[:2]]
    moe_same = [
        moe_rows, chip_shift(after(moe_rows, cot_same[2], cot_other, weight_parts[0][3]), 1)
    ]
    for d in range(3, chips):
        cot_same.append(chip_shift(after(cot_same[-1], moe_same[1]), 1))
    moe_other = [core_swap(rows) for rows in moe_same]
    moe_same.append(chip_shift(moe_same[1], 1))
    cot_other += [core_swap(after(rows, moe_rows)) for rows in cot_same[2:]]

    moe_meta = jnp.stack([row, column * own_experts]).astype(jnp.int32)
    ffe = w_down.shape[1]
    kept = [[] for _ in range(groups)]
    pieces = [None] * chips
    grads = []

    def piece(d, start, stop):
        return add_low(pieces[d][0][:, start:stop], pieces[d][1][:, start:stop])

    both = 2 * width + LANES
    pairs = [(d, d + 1) for d in range(0, chips, 2)]
    early = [[] for _ in pairs]
    held = ()
    far, late, sums = [], [], []

    def make_grads(group, first_rows):
        chunks = kept[group]
        parts = weight_grads(
            [first_rows] + [k[0] for k in chunks[1:]],
            [k[3] for k in chunks],
            [k[2] for k in chunks],
            [k[1] for k in chunks],
        )
        grads.append([two_halves(part) for part in parts])

    for index, pair in enumerate(pairs):
        for group in range(groups):
            final = group == groups - 1
            if final and index == len(pairs) - 1 and groups > 1:
                make_grads(0, kept[0][0][0])
                far.append(reduce_first(grads[0]))
                held = grads[0]
            result = list(
                run_experts(
                    after(moe_meta, held),
                    [rows for d in pair for rows in (moe_same[d], moe_other[d])],
                    [rows for d in pair for rows in (cot_same[d], cot_other[d])],
                    early[index],
                    weight_parts[group],
                    ffe,
                    experts,
                    slots,
                    group * group_size,
                    final,
                )
            )
            held = result[0]
            if len(moe_other) == 2:
                moe_same[2] = after(moe_same[2], held)
                held = (held, moe_same[2])
                for d in range(3, chips):
                    moe_same.append(chip_shift(moe_same[-1], 1))
                moe_other += [core_swap(rows) for rows in moe_same[2:]]
                for later in range(1, groups):
                    weight_near[later] = after(weight_near[later], held)
                    weight_parts.append(gather_far(packed[later], *weight_near[later]))
            if not final:
                kept[group].append(result[:4])
                early[index] = result[4:]
                continue
            if index == 0:
                result = after(result, moe_same[3], cot_same[3])
            if index == len(pairs) - 1:
                result = after(result, dx_hop, far if groups > 1 else ())
            kept[group].append(result[4:8])
            for place, d in enumerate(pair):
                pieces[d] = (result[2 * place], core_swap(result[2 * place + 1]))
            if index == 0:
                dx_ring = piece(1, width, both)
                held = dx_ring
                dx_hop = chip_shift(dx_ring, 1)
                continue
            for d in pair:
                came = dx_hop if d == 2 else chip_shift(dx_ring, 1)
                if d == chips - 1:
                    came = after(came, grads[-1])
                    far.append(reduce_first(after(grads[-1], came)))
                dx_ring = add_low(came, last_pieces[0] if d == chips - 1 else piece(d, width, both))
                if d != chips - 2:
                    continue
                last_pieces = [piece(chips - 1, width, both), piece(0, width, both)]
                if groups > 1:
                    sums.append(reduce_second(grads[0], after(far[0], dx_ring)))
                    late.append([rows_swap(*sent) for sent in zip(sums[0], (1, 2))])
                make_grads(group, after(kept[group][0][0], dx_ring, sums, last_pieces))
    for d in range(chips):
        pieces[d] = after(pieces[d], dx_ring)
    outs = [piece(d, 0, width) for d in range(chips - 1)]
    outs.append(piece(chips - 1, 0, width))
    dx_came = after(chip_shift(dx_ring, 1), outs)
    out_hop = chip_shift(after(outs[1], dx_came), 1)

    grad_mixed, grad_heads, wide_mine, wide_other = unmix(
        after(meta, late[:1]),
        dx_came,
        last_pieces[1],
        mixed_rows,
        cotangent[0],
        gates,
        gain_moe,
        router_full,
        out_parts,
        own_heads,
        experts,
        chips,
    )
    grad_attended = lax.all_to_all(grad_heads, "rows", 0, 0, tiled=True)

    wide_chip = add_low(wide_mine, core_swap(after(wide_other, far[-1])))
    wide_came = lax.all_to_all(wide_chip, "rows", 0, 0, tiled=True)

    grad_lin = attend_back(
        after(meta, wide_chip),
        queries,
        grad_attended,
        lse.T,
        starts[None, :],
        key_rows,
        value_rows,
        cosine,
        sine,
        tok,
    )
    grad_lin = after(grad_lin, late[:1], wide_came)
    normed_parts = [None] * 4
    for j in (3, 1, 2, 0):
        normed_parts[j] = dot_nt(grad_lin[j], project_w).astype(bf16)
    normed_sums = reduce_add(normed_parts, *reduce_far(normed_parts))
    normed_near = reduce_near(*normed_sums)
    sums.append(reduce_second(grads[-1], after(far[-1], *normed_sums)))
    late.append([rows_swap(*sent) for sent in zip(sums[-1], (1, 2))])
    grad_project = dot_tn(
        after(normed, *normed_parts).reshape(length, width), grad_lin.reshape(length, qkv_cols)
    )
    project_pairs = after(grad_project.astype(bf16), *normed_sums)
    project_pairs = project_pairs.reshape(chips, 2, width // columns, qkv_cols)
    project_chip = cores_sum(project_pairs.transpose(1, 0, 2, 3))
    project_came = chips_exchange(project_chip)
    project_sum = jnp.sum(project_came.astype(f32), axis=0)
    grad_normed = add_wide([normed_parts[0], *after(normed_near, project_sum)])
    wide_row = add_low_all(after(wide_came, project_came, late[-1]))
    wide_sum = jnp.sum(chips_exchange(wide_row).astype(f32), axis=0)
    grad_out_w = wide_sum[:, :width]
    grad_router_w = wide_sum[:, width : width + experts]
    grad_gain_moe_w = wide_sum[:, width + experts]

    out_ring = add_low(after(out_hop, grad_lin), outs[2])
    for d in range(3, chips):
        out_ring = add_low(after(chip_shift(out_ring, 1), *normed_sums), outs[d])
    moe_out = add_wide([chip_shift(after(out_ring, project_came), 1), outs[0]])
    block_out = mixed_rows + res_scale * moe_out

    totals = []
    for parts, came in zip(grads, late):
        total = reduce_total([after(parts[0], *normed_sums, project_chip)], came)
        totals.append(unpack_weights(join_halves(total, group_size), width // 4, ffe))
    grad_gate_w, grad_up_w, grad_down_w = (
        jnp.concatenate(arrays, axis=0) for arrays in zip(*totals)
    )

    own_w = jnp.concatenate([w_query, key_matrix, value_matrix], axis=1).astype(f32)
    own_gain = lax.dynamic_slice_in_dim(gain_attn[0], column * own_w.shape[0], own_w.shape[0], 0)
    gain_rows = (jnp.sum(project_sum * own_w, axis=1) / own_gain).reshape(4, -1)
    gain_sum = jnp.sum(lax.all_to_all(gain_rows, "rows", 0, 0, tiled=True), axis=0)
    grad_gain_attn = lax.ppermute(
        gain_sum,
        ("rows", "cols"),
        [(r * columns + c, 4 * c + r) for r in range(4) for c in range(columns)],
    )

    own_float = own_tokens.astype(f32)
    scale_attn = rms_scale(own_float)
    unit_attn = own_float * scale_attn
    grad_unit = grad_normed * gain_attn
    grad_tokens = grad_mixed + scale_attn * (
        grad_unit - unit_attn * jnp.mean(grad_unit * unit_attn, axis=-1, keepdims=True)
    )
    return (
        block_out[None],
        grad_tokens[None],
        project_sum[:, :q_cols],
        project_sum[:, q_cols : q_cols + k_cols],
        project_sum[:, q_cols + k_cols :],
        grad_out_w,
        grad_gain_attn,
        grad_gain_moe_w,
        grad_router_w,
        grad_gate_w,
        grad_up_w,
        grad_down_w,
    )


def solution(mesh):
    placed = (
        P("cols", "rows", None),
        P("cols", None),
        P("cols", "rows", None),
        P("cols", "rows"),
        P("cols", "rows"),
        P("cols", "rows"),
        P(("rows", "cols"), None),
        P(("rows", "cols")),
        P(("rows", "cols")),
        P(("rows", "cols"), None),
        P("cols", "rows", None),
        P("cols", "rows", None),
        P("cols", None, "rows"),
        P("cols", "rows", None),
    )
    return jax.shard_map(
        per_device,
        mesh=mesh,
        in_specs=placed,
        out_specs=(
            P("cols", "rows", None),
            P("cols", "rows", None),
            P("cols", "rows"),
            P("cols", "rows"),
            P("cols", "rows"),
            P(("rows", "cols"), None),
            P(("rows", "cols")),
            P(("rows", "cols")),
            P(("rows", "cols"), None),
            P("cols", "rows", None),
            P("cols", "rows", None),
            P("cols", None, "rows"),
        ),
        check_vma=False,
    )
```

```python
from functools import partial

import jax
import jax.numpy as jnp
from jax import lax
from jax.experimental import pallas as pl
from jax.experimental.pallas import tpu as pltpu
from jax.sharding import PartitionSpec as P

HEAD_SIZE = 64
LANES = 128
LONGEST_DOC = 768

res_scale = 0.22
att_scale = 0.015625
norm_eps = 1e-06
rope_base = 10000.0
masked_score = -1e30
log2_e = 1.4426950408889634
highest = lax.Precision.HIGHEST
bf16 = jnp.bfloat16
f32 = jnp.float32


def rms_scale(hidden_rows):
    return lax.rsqrt(jnp.mean(hidden_rows * hidden_rows, axis=-1, keepdims=True) + norm_eps)


def dot_nt(left, right):
    return lax.dot_general(left, right, (((1,), (1,)), ((), ())), preferred_element_type=f32)


def dot_tn(left, right):
    return lax.dot_general(left, right, (((0,), (0,)), ((), ())), preferred_element_type=f32)


def dot_nn(left, right):
    return jnp.dot(left, right, preferred_element_type=f32)


def rows_swap(array, distance):
    return lax.ppermute(array, "rows", [(i, i ^ distance) for i in range(4)])


def halves(array):
    axis = 0 if array.shape[0] % 2 == 0 else 1
    cut = array.shape[axis] // 2
    return (
        axis,
        lax.slice_in_dim(array, 0, cut, axis=axis),
        lax.slice_in_dim(array, cut, 2 * cut, axis=axis),
    )


def gather_near(array):
    return rows_swap(array, 1), rows_swap(array, 2)


def far_halves(from_x, from_y):
    _, first_y, _ = halves(from_y)
    _, _, second_x = halves(from_x)
    return rows_swap(first_y, 1), rows_swap(second_x, 2)


def join_far(array, from_x, from_y, far):
    return [array, from_x, from_y, jnp.concatenate(far, axis=halves(array)[0])]


def gather_far(array, from_x, from_y):
    return join_far(array, from_x, from_y, far_halves(from_x, from_y))


def rows_exchange(pieces):
    return [pieces[0]] + [rows_swap(pieces[j], j) for j in (1, 2, 3)]


def reduce_far(pieces):
    _, first, second = halves(pieces[3])
    return rows_swap(first, 1), rows_swap(second, 2)


def reduce_add(pieces, from_x, from_y):
    axis, first_x, second_x = halves(pieces[1])
    _, first_y, second_y = halves(pieces[2])
    return (
        jnp.concatenate([first_x, add_low(second_x, from_y)], axis=axis),
        jnp.concatenate([add_low(first_y, from_x), second_y], axis=axis),
    )


def reduce_near(to_x, to_y):
    return rows_swap(to_x, 1), rows_swap(to_y, 2)


def reduce_first(pieces):
    return rows_swap(pieces[3][0], 1), rows_swap(pieces[3][1], 2)


def reduce_second(pieces, far):
    return (
        jnp.concatenate([pieces[1][0], add_low(pieces[1][1], far[1])], axis=0),
        jnp.concatenate([add_low(pieces[2][0], far[0]), pieces[2][1]], axis=0),
    )


def reduce_total(pieces, late):
    return add_wide([jnp.concatenate(pieces[0], axis=0), *late])


def add_wide(arrays):
    return sum(array.astype(f32) for array in arrays)


def add_low_all(array):
    return jnp.sum(array.astype(f32), axis=0).astype(bf16)


def add_low(left, right):
    return (left.astype(f32) + right.astype(f32)).astype(bf16)


def chip_shift(array, distance):
    count = lax.axis_size("cols")
    return lax.ppermute(
        array, "cols", [(i, (i + 2 * distance) % count) for i in range(count)]
    )


def core_swap(array):
    count = lax.axis_size("cols")
    return lax.ppermute(array, "cols", [(i, i ^ 1) for i in range(count)])


def chips_gather(array):
    chips = lax.axis_size("cols") // 2
    return [array] + [chip_shift(array, d) for d in range(1, chips)]


def chips_in_order(array, chip):
    chips = array.shape[0]
    twice = jnp.concatenate([array[::-1]] * 2, axis=0)
    return lax.dynamic_slice_in_dim(twice, chips - 1 - chip, chips, 0)


def cores_sum(array):
    count = lax.axis_size("cols")
    pairs = [[i, i + 1] for i in range(0, count, 2)]
    came = lax.all_to_all(array, "cols", 0, 0, axis_index_groups=pairs, tiled=True)
    return add_low(came[0], came[1])


def chips_exchange(array):
    count = lax.axis_size("cols")
    alike = [list(range(core, count, 2)) for core in range(2)]
    return lax.all_to_all(array, "cols", 0, 0, axis_index_groups=alike, tiled=True)


def cores_in_order(mine, other, core, axis):
    return jnp.stack(
        [jnp.where(core == 0, mine, other), jnp.where(core == 0, other, mine)], axis=axis
    )


def call_params(mebibytes):
    return pltpu.CompilerParams(vmem_limit_bytes=mebibytes * 1024 * 1024)


def cost(micros):
    return pl.CostEstimate(flops=int(micros * 1.15e9), bytes_accessed=0, transcendentals=0)


def turn(rows, cosine, sine):
    lane = lax.broadcasted_iota(jnp.int32, rows.shape, 1)
    partner = jnp.where(
        (lane & (HEAD_SIZE - 1)) < HEAD_SIZE // 2,
        pltpu.roll(rows, LANES - HEAD_SIZE // 2, 1),
        pltpu.roll(rows, HEAD_SIZE // 2, 1),
    )
    return rows * cosine + partner * sine


def project_kernel(meta, *refs):
    parts, found, swapped, gain, cosine, sine = refs[:4], refs[4], refs[5], *refs[6:9]
    q_out, k_out, v_out, n_out, w_out = refs[9:]
    step = pl.program_id(0)
    chips, rows, _ = found.shape
    chip = meta[1]

    @pl.when(step == 0)
    def _():
        first_core = meta[2] == 0
        for d in range(chips):
            mine, other = found[d], swapped[d]
            here = pl.multiple_of(lax.rem(chip + chips - d, chips) * (2 * rows), 2 * rows)
            w_out[pl.ds(here, 2 * rows), :] = jnp.concatenate(
                [jnp.where(first_core, mine, other), jnp.where(first_core, other, mine)], axis=0
            )

    for index, part in enumerate(parts):

        @pl.when(step == index)
        def _(part=part):
            rows = part[...].astype(f32)
            n_out[0] = (rows * rms_scale(rows) * gain[...]).astype(bf16)

    linear = dot_nn(n_out[0], w_out[...])
    q_cols, k_cols = q_out.shape[1], k_out.shape[1]
    cos_rows, sin_rows = cosine[...], sine[...]
    turned = jnp.concatenate(
        [
            turn(linear[:, at : at + LANES], cos_rows, sin_rows)
            for at in range(0, q_cols + k_cols, LANES)
        ],
        axis=1,
    ).astype(bf16)
    q_out[...] = turned[:, :q_cols]
    k_out[...] = turned[:, q_cols:]
    v_out[...] = linear[:, q_cols + k_cols :].astype(bf16)


def project(meta, parts, found, swapped, gain, cosine, sine, q_cols, k_cols):
    tok, width = parts[0].shape
    length = 4 * tok
    whole = pl.BlockSpec(memory_space=pltpu.VMEM)

    def natural(step, meta):
        return (step ^ meta[0], 0)

    return pl.pallas_call(
        project_kernel,
        grid_spec=pltpu.PrefetchScalarGridSpec(
            num_scalar_prefetch=1,
            grid=(4,),
            in_specs=[whole] * 7
            + [pl.BlockSpec((tok, LANES), natural), pl.BlockSpec((tok, LANES), natural)],
            out_specs=[
                pl.BlockSpec((tok, q_cols), natural),
                pl.BlockSpec((tok, k_cols), natural),
                pl.BlockSpec((tok, k_cols), natural),
                pl.BlockSpec((1, tok, width), lambda step, meta: (step, 0, 0)),
                pl.BlockSpec((width, q_cols + 2 * k_cols), lambda step, meta: (0, 0)),
            ],
        ),
        out_shape=[
            jax.ShapeDtypeStruct((length, q_cols), bf16),
            jax.ShapeDtypeStruct((length, k_cols), bf16),
            jax.ShapeDtypeStruct((length, k_cols), bf16),
            jax.ShapeDtypeStruct((4, tok, width), bf16),
            jax.ShapeDtypeStruct((width, q_cols + 2 * k_cols), bf16),
        ],
        compiler_params=call_params(32),
        cost_estimate=cost(10),
        name="project",
    )(meta, *parts, found, swapped, gain, cosine, sine)


def attend_kernel(meta, queries, keys, values, starts, out, lse, *, bands):
    block = pl.program_id(0)
    rows = queries.shape[0]
    first = meta[3 + block]
    heads = queries.shape[1] // HEAD_SIZE
    group = queries.shape[1] // keys.shape[1]
    for band in range(1, bands + 1):

        @pl.when(block - first + 1 == band)
        def _(band=band):
            width = band * rows
            base = pl.multiple_of(first * rows, rows)
            key_band = keys[pl.ds(base, width), :]
            value_band = values[pl.ds(base, width), :]
            query_pos = block * rows + lax.broadcasted_iota(jnp.int32, (rows, width), 0)
            key_pos = base + lax.broadcasted_iota(jnp.int32, (rows, width), 1)
            allowed = (key_pos >= starts[...]) & (key_pos <= query_pos)
            results = []
            for head in range(heads):
                at = head // group * HEAD_SIZE
                scores = dot_nt(
                    queries[:, head * HEAD_SIZE : (head + 1) * HEAD_SIZE],
                    key_band[:, at : at + HEAD_SIZE],
                )
                scores = jnp.where(allowed, scores, masked_score)
                top = jnp.max(scores, axis=1, keepdims=True)
                weights = jnp.exp2((scores - top) * (att_scale * log2_e))
                total = jnp.sum(weights, axis=1, keepdims=True)
                result = dot_nn(weights.astype(bf16), value_band[:, at : at + HEAD_SIZE])
                results.append(result * (1.0 / total))
                lse[:, head : head + 1] = top * (att_scale * log2_e) + jnp.log2(total)
            out[0] = jnp.concatenate(results, axis=1).astype(bf16)


def attend(meta, queries, keys, values, starts, tok):
    length, q_cols = queries.shape
    k_cols = keys.shape[1]
    blocks = length // tok
    whole = pl.BlockSpec(memory_space=pltpu.VMEM)
    return pl.pallas_call(
        partial(attend_kernel, bands=min(blocks, LONGEST_DOC // tok + 1)),
        grid_spec=pltpu.PrefetchScalarGridSpec(
            num_scalar_prefetch=1,
            grid=(blocks,),
            in_specs=[
                pl.BlockSpec((tok, q_cols), lambda i, meta: (i, 0)),
                whole,
                whole,
                pl.BlockSpec((tok, 1), lambda i, meta: (i, 0)),
            ],
            out_specs=[
                pl.BlockSpec((1, tok, q_cols), lambda i, meta: (i, 0, 0)),
                pl.BlockSpec((tok, 8), lambda i, meta: (i, 0)),
            ],
        ),
        out_shape=[
            jax.ShapeDtypeStruct((blocks, tok, q_cols), bf16),
            jax.ShapeDtypeStruct((length, 8), f32),
        ],
        compiler_params=call_params(32),
        cost_estimate=cost(5),
        name="attend",
    )(meta, queries, keys, values, starts)


def attend_back_kernel(
    meta, queries, grads, lse, starts, keys, values, cosine, sine, out, key_sum, value_sum, *, bands
):
    block = pl.program_id(0)
    rows = queries.shape[0]
    first = meta[3 + block]
    q_cols, k_cols = queries.shape[1], keys.shape[1]
    heads = q_cols // HEAD_SIZE
    group = q_cols // k_cols

    @pl.when(block == 0)
    def _():
        key_sum[...] = jnp.zeros_like(key_sum)
        value_sum[...] = jnp.zeros_like(value_sum)

    for band in range(1, bands + 1):

        @pl.when(block - first + 1 == band)
        def _(band=band):
            width = band * rows
            base = pl.multiple_of(first * rows, rows)
            key_band = keys[pl.ds(base, width), :]
            value_band = values[pl.ds(base, width), :]
            key_pos = base + lax.broadcasted_iota(jnp.int32, (width, rows), 0)
            query_pos = block * rows + lax.broadcasted_iota(jnp.int32, (width, rows), 1)
            allowed = (key_pos >= starts[...]) & (key_pos <= query_pos)
            query_grads, key_parts, value_parts = [], [], []
            for kv_head in range(k_cols // HEAD_SIZE):
                at = kv_head * HEAD_SIZE
                key_rows = key_band[:, at : at + HEAD_SIZE]
                value_rows = value_band[:, at : at + HEAD_SIZE]
                key_part = jnp.zeros((width, HEAD_SIZE), f32)
                value_part = jnp.zeros((width, HEAD_SIZE), f32)
                for head in range(kv_head * group, (kv_head + 1) * group):
                    query_rows = queries[:, head * HEAD_SIZE : (head + 1) * HEAD_SIZE]
                    grad_rows = grads[0, :, head * HEAD_SIZE : (head + 1) * HEAD_SIZE]
                    scores = dot_nt(key_rows, query_rows)
                    probs = jnp.where(
                        allowed,
                        jnp.exp2(scores * (att_scale * log2_e) - lse[head : head + 1, :]),
                        0.0,
                    )
                    grad_probs = dot_nt(value_rows, grad_rows)
                    delta = jnp.sum(probs * grad_probs, axis=0, keepdims=True)
                    grad_scores = (probs * (grad_probs - delta)).astype(bf16)
                    value_part += dot_nn(probs.astype(bf16), grad_rows)
                    key_part += dot_nn(grad_scores, query_rows)
                    query_grads.append(dot_tn(grad_scores, key_rows))
                key_parts.append(key_part)
                value_parts.append(value_part)
            key_sum[pl.ds(base, width), :] += jnp.concatenate(key_parts, axis=1)
            value_sum[pl.ds(base, width), :] += jnp.concatenate(value_parts, axis=1)
            here = pl.ds(pl.multiple_of(block * rows, rows), rows)
            query_grad = jnp.concatenate(query_grads, axis=1) * att_scale
            turned = [
                turn(query_grad[:, c : c + LANES], cosine[here, :], -sine[here, :])
                for c in range(0, q_cols, LANES)
            ]
            out[block ^ meta[0], :, :q_cols] = jnp.concatenate(turned, axis=1).astype(bf16)

    @pl.when(block == pl.num_programs(0) - 1)
    def _():
        for part in range(4):
            here = pl.ds(pl.multiple_of((meta[0] ^ part) * rows, rows), rows)
            key_grad = key_sum[here, :] * att_scale
            turned = [
                turn(key_grad[:, c : c + LANES], cosine[here, :], -sine[here, :])
                for c in range(0, k_cols, LANES)
            ]
            out[part, :, q_cols : q_cols + k_cols] = jnp.concatenate(turned, axis=1).astype(bf16)
            out[part, :, q_cols + k_cols :] = value_sum[here, :].astype(bf16)


def attend_back(meta, queries, grads, lse, starts, keys, values, cosine, sine, tok):
    length, q_cols = queries.shape
    k_cols = keys.shape[1]
    blocks = length // tok
    whole = pl.BlockSpec(memory_space=pltpu.VMEM)
    return pl.pallas_call(
        partial(attend_back_kernel, bands=min(blocks, LONGEST_DOC // tok + 1)),
        grid_spec=pltpu.PrefetchScalarGridSpec(
            num_scalar_prefetch=1,
            grid=(blocks,),
            in_specs=[
                pl.BlockSpec((tok, q_cols), lambda i, meta: (i, 0)),
                pl.BlockSpec((1, tok, q_cols), lambda i, meta: (i, 0, 0)),
                pl.BlockSpec((8, tok), lambda i, meta: (0, i)),
                pl.BlockSpec((1, tok), lambda i, meta: (0, i)),
                whole,
                whole,
                whole,
                whole,
            ],
            out_specs=pl.BlockSpec(
                (blocks, tok, q_cols + 2 * k_cols), lambda i, meta: (0, 0, 0)
            ),
            scratch_shapes=[
                pltpu.VMEM((length, k_cols), f32),
                pltpu.VMEM((length, k_cols), f32),
            ],
        ),
        out_shape=jax.ShapeDtypeStruct((blocks, tok, q_cols + 2 * k_cols), bf16),
        compiler_params=call_params(40),
        cost_estimate=cost(29),
        name="attend_back",
    )(meta, queries, grads, lse, starts, keys, values, cosine, sine)


def low_pair(values):
    high = values.astype(bf16)
    return high, (values - high.astype(f32)).astype(bf16)


def mix_kernel(
    meta, heads, out_parts, tokens, member, gain, router, mixed_out, rows_out, gates_out, *, experts
):
    width = tokens.shape[1]
    branch = sum(dot_nn(heads[meta[0] ^ part], out_parts[part]) for part in range(4))
    mixed = tokens[...].astype(f32) + res_scale * branch
    mixed_out[...] = mixed
    normed = (mixed * rms_scale(mixed) * gain[...]).astype(bf16)
    logits = dot_nn(normed, router[...])
    named = member[...] > 0
    logits = jnp.where(named, logits, masked_score)
    lifted = jnp.exp(logits - jnp.max(logits, axis=1, keepdims=True))
    lifted = jnp.where(named, lifted, 0.0)
    gates = lifted * (1.0 / jnp.sum(lifted, axis=1, keepdims=True))
    gates_out[...] = gates
    high, low = low_pair(gates)
    low = pltpu.roll(low.astype(f32), experts, 1)
    rows_out[:, :width] = normed
    rows_out[:, width:] = (high.astype(f32) + low).astype(bf16)


def mix(meta, heads, out_parts, tokens, member, gain, router, experts):
    tok, width = tokens.shape
    whole = pl.BlockSpec(memory_space=pltpu.VMEM)
    return pl.pallas_call(
        partial(mix_kernel, experts=experts),
        in_specs=[pl.BlockSpec(memory_space=pltpu.SMEM)] + [whole] * 6,
        out_specs=[whole] * 3,
        out_shape=[
            jax.ShapeDtypeStruct((tok, width), f32),
            jax.ShapeDtypeStruct((tok, width + LANES), bf16),
            jax.ShapeDtypeStruct((tok, LANES), f32),
        ],
        compiler_params=call_params(40),
        cost_estimate=cost(6),
        name="mix",
    )(meta, heads, out_parts, tokens, member, gain, router)


def unmix_kernel(
    meta, came, last, mixed_in, cotangent, gates, gain, router, out_parts, heads,
    mixed_grad, heads_out, mine_out, other_out, *, experts
):
    width = cotangent.shape[1]
    summed = came[...].astype(f32) + last[...].astype(f32)
    beside = summed[:, width:]
    lane = lax.broadcasted_iota(jnp.int32, beside.shape, 1)
    weighted = jnp.where(lane < experts, beside + pltpu.roll(beside, LANES - experts, 1), 0.0)
    logit_grads = weighted - gates[...] * jnp.sum(weighted, axis=1, keepdims=True)
    high, low = low_pair(logit_grads)
    normed_grad = summed[:, :width] + dot_nt(high, router[...]) + dot_nt(low, router[...])
    mixed = mixed_in[...]
    scale = rms_scale(mixed)
    unit = mixed * scale
    normed = (unit * gain[...]).astype(bf16)
    one_lane = lax.broadcasted_iota(jnp.int32, (unit.shape[0], LANES), 1) == experts
    one_lane = one_lane.astype(f32).astype(bf16)
    gain_high, gain_low = low_pair(normed_grad * unit)
    shares = dot_tn(normed, high) + dot_tn(normed, low)
    shares = (shares + dot_tn(gain_high, one_lane) + dot_tn(gain_low, one_lane)).astype(bf16)
    unit_grad = normed_grad * gain[...]
    grad = cotangent[...].astype(f32) + scale * (
        unit_grad - unit * jnp.mean(unit_grad * unit, axis=-1, keepdims=True)
    )
    mixed_grad[...] = grad
    branch = (res_scale * grad).astype(bf16)
    for part in range(4):
        heads_out[meta[0] ^ part] = dot_nt(branch, out_parts[part]).astype(bf16)
    first_core = meta[2] == 0
    _, chips, sixth, _ = mine_out.shape
    tok = branch.shape[0]
    for part in range(4):
        wide = dot_tn(heads[part], branch).astype(bf16)
        wide = jnp.concatenate([wide, shares[part * tok : (part + 1) * tok]], axis=1)
        for chip in range(chips):
            at = 2 * chip * sixth
            even, odd = wide[at : at + sixth], wide[at + sixth : at + 2 * sixth]
            mine_out[part, chip] = jnp.where(first_core, even, odd)
            other_out[part, chip] = jnp.where(first_core, odd, even)


def unmix(meta, came, last, mixed, cotangent, gates, gain, router, out_parts, heads, experts, chips):
    tok, width = mixed.shape
    wide = (4, chips, tok // (2 * chips), width + LANES)
    whole = pl.BlockSpec(memory_space=pltpu.VMEM)
    return pl.pallas_call(
        partial(unmix_kernel, experts=experts),
        in_specs=[pl.BlockSpec(memory_space=pltpu.SMEM)] + [whole] * 9,
        out_specs=[whole] * 4,
        out_shape=[
            jax.ShapeDtypeStruct((tok, width), f32),
            jax.ShapeDtypeStruct((4, tok, out_parts.shape[1]), bf16),
            jax.ShapeDtypeStruct(wide, bf16),
            jax.ShapeDtypeStruct(wide, bf16),
        ],
        compiler_params=call_params(32),
        cost_estimate=cost(12),
        name="unmix",
    )(meta, came, last, mixed, cotangent, gates, gain, router, out_parts, heads)


def hidden_weights(parts, cut, ffe):
    tiles = 2 * ffe // LANES
    return jnp.concatenate(
        [
            jnp.concatenate([ref[0, t * cut : (t + 1) * cut, :] for t in range(tiles)], axis=1)
            for ref in parts
        ],
        axis=0,
    )


def down_weights(parts, cut, ffe):
    first = 2 * ffe // LANES * cut
    return jnp.concatenate(
        [
            ref[0, first + t * ffe : first + (t + 1) * ffe, :]
            for ref in parts
            for t in range(cut // LANES)
        ],
        axis=1,
    )


def experts_kernel(meta, *refs, experts, slots, local, final, earlier):
    blocks = 4
    x_refs, g_refs, refs = refs[:blocks], refs[blocks : 2 * blocks], refs[2 * blocks :]
    early, refs = refs[:earlier], refs[earlier:]
    parts, refs = refs[:4], refs[4:]
    returned_out, refs = refs[: blocks * final], refs[blocks * final :]
    x_out, g_out, active_out, grads_out, out_kept, dx_kept, t_kept, refs = *refs[:7], refs[7:]
    x_rows, g_rows, gate_kept, rows_sent, x_here, g_here, arrived, refs = *refs[:7], refs[7:]
    own = pl.program_id(0)
    own_count = x_rows.shape[0]
    tok = x_refs[0].shape[0]
    width = x_rows.shape[2]
    cut = width // 4
    ffe = active_out.shape[2]
    row, first_expert = meta[0], meta[1]
    loads = [
        (
            pltpu.make_async_copy(x_refs[block], x_here.at[block % 2], arrived.at[0, block % 2]),
            pltpu.make_async_copy(g_refs[block], g_here.at[block % 2], arrived.at[1, block % 2]),
        )
        for block in range(blocks)
    ]
    if final:
        ranks_kept, returned, sent, refs = *refs[:3], refs[3:]
    fetches = [
        [
            pltpu.make_async_copy(
                early[which].at[:, pl.ds(block * slots, slots), :],
                refs[which].at[block % 2],
                refs[3].at[which, block % 2],
            )
            for which in range(earlier)
        ]
        for block in range(blocks)
    ]
    row_copies = [
        pltpu.make_async_copy(x_rows, x_out, rows_sent.at[0]),
        pltpu.make_async_copy(g_rows, g_out, rows_sent.at[1]),
    ]

    def columns(part, start=0):
        return pl.ds(pl.multiple_of(start + (row ^ part) * cut, LANES), cut)

    @pl.when(own == 0)
    def _():
        for load in loads[0]:
            load.start()
        slot = lax.broadcasted_iota(jnp.int32, (slots, tok), 0).astype(f32)
        lower = (
            lax.broadcasted_iota(jnp.int32, (tok, tok), 0)
            > lax.broadcasted_iota(jnp.int32, (tok, tok), 1)
        ).astype(f32).astype(bf16)
        source = lax.broadcasted_iota(jnp.int32, (LANES, LANES), 1)
        target = lax.broadcasted_iota(jnp.int32, (LANES, LANES), 0)
        choose = (source == target + first_expert).astype(f32).astype(bf16)
        for block in range(blocks):
            for load in loads[block + 1] if block + 1 < blocks else ():
                load.start()
            for load in loads[block]:
                load.wait()
            x_block, g_block = x_here.at[block % 2], g_here.at[block % 2]
            member = g_block[:, width:]
            rank = jnp.where(member > 0, dot_nn(lower, member), -1.0).astype(bf16)
            if final:
                ranks_kept[block] = dot_nt(rank, choose)
            rank_rows = dot_nt(choose, rank)
            pick = jnp.concatenate(
                [
                    (rank_rows[index : index + 1, :] == slot).astype(f32).astype(bf16)
                    for index in range(local, local + own_count)
                ],
                axis=0,
            )
            beside = dot_nn(pick, x_block[:, width:])
            lane = lax.broadcasted_iota(jnp.int32, beside.shape, 1)
            named = lax.broadcasted_iota(jnp.int32, beside.shape, 0) // slots
            named = named + first_expert + local
            gates = jnp.sum(
                jnp.where((lane == named) | (lane == named + experts), beside, 0.0),
                axis=1,
                keepdims=True,
            )
            here = slice(block * slots, (block + 1) * slots)
            x_part = dot_nn(pick, x_block[:, :width]).astype(bf16)
            g_part = dot_nn(pick, g_block[:, :width]).astype(bf16)
            for index in range(own_count):
                rows = slice(index * slots, (index + 1) * slots)
                gate_kept[index, here, :] = gates[rows]
                for part in range(4):
                    there = slice(part * cut, (part + 1) * cut)
                    x_rows[index, here, columns(part)] = x_part[rows, there]
                    g_rows[index, here, columns(part)] = g_part[rows, there]
        for copy in row_copies:
            copy.start()

    @pl.when(own == own_count - 1)
    def _():
        for fetch in fetches[0] + fetches[1]:
            fetch.start()

    hidden_w = hidden_weights(parts, cut, ffe)
    down_w = down_weights(parts, cut, ffe)
    hidden = dot_nn(x_rows[own], hidden_w)
    hidden_gate, hidden_up = hidden[:, :ffe], hidden[:, ffe:]
    gates = gate_kept[own]
    grad_active = dot_nt(g_rows[own], down_w) * (res_scale * gates)
    sigmoid = jax.nn.sigmoid(hidden_gate)
    silu = hidden_gate * sigmoid
    active = silu * hidden_up
    gated = (active * gates).astype(bf16)
    grad_gate = grad_active * hidden_up * (sigmoid * (1.0 + hidden_gate * (1.0 - sigmoid)))
    grads = jnp.concatenate(
        [grad_gate.astype(bf16), (grad_active * silu).astype(bf16)], axis=1
    )
    weighted = jnp.sum(active * grad_active, axis=1, keepdims=True)
    active_out[0] = gated
    grads_out[0] = grads
    kept = own if final else 0
    out_kept[kept] = dot_nn(gated, down_w).astype(bf16)
    dx_kept[kept] = dot_nt(grads, hidden_w).astype(bf16)
    weighted_high = weighted.astype(bf16).astype(f32)
    lane = lax.broadcasted_iota(jnp.int32, (blocks * slots, LANES), 1)
    named = first_expert + local + own
    t_kept[kept] = jnp.where(
        lane == named,
        weighted_high,
        jnp.where(lane == named + experts, weighted - weighted_high, 0.0),
    ).astype(bf16)

    @pl.when(own == own_count - 1)
    def _():
        if final:
            slot = lax.broadcasted_iota(jnp.int32, (tok, slots), 1).astype(f32)
            gives = [
                pltpu.make_async_copy(
                    returned.at[block % 2], returned_out[block], sent.at[block]
                )
                for block in range(blocks)
            ]
            for block in range(blocks):
                here = slice(block * slots, (block + 1) * slots)
                put = jnp.concatenate(
                    [
                        (ranks_kept[block, :, index : index + 1] == slot).astype(f32).astype(bf16)
                        for index in range(local + own_count)
                    ],
                    axis=1,
                )

                def rows_of(which, here=here, block=block):
                    kept_rows = (out_kept, dx_kept, t_kept)[which]
                    found = [refs[which][block % 2, index] for index in range(local)]
                    found += [kept_rows[index, here, :] for index in range(own_count)]
                    return jnp.concatenate(found, axis=0)

                for fetch in fetches[block]:
                    fetch.wait()
                if block >= 2:
                    gives[block - 2].wait()
                out = dot_nn(put, rows_of(0)).astype(bf16)
                dx = dot_nn(put, rows_of(1)).astype(bf16)
                for part in range(4):
                    there = slice(part * cut, (part + 1) * cut)
                    returned[block % 2, :, columns(part)] = out[:, there]
                    returned[block % 2, :, columns(part, width)] = dx[:, there]
                returned[block % 2, :, 2 * width :] = dot_nn(put, rows_of(2)).astype(bf16)
                gives[block].start()
                for fetch in fetches[block + 2] if block + 2 < blocks else ():
                    fetch.start()
            for give in gives[-2:]:
                give.wait()
        for copy in row_copies:
            copy.wait()


def run_experts(meta, x_blocks, g_blocks, early, parts, ffe, experts, slots, local, final):
    blocks = len(x_blocks)
    tok, padded = x_blocks[0].shape
    width = padded - LANES
    own, packed, _ = parts[0].shape
    rows = blocks * slots
    anywhere = pl.BlockSpec(memory_space=pl.ANY)
    back = 2 * width + LANES
    kept_shapes = [(own, rows, width), (own, rows, width), (own, rows, LANES)]
    row_shapes = [(own, rows, width), (own, rows, width), (own, rows, ffe), (own, rows, 2 * ffe)]

    def one(*shape):
        return pl.BlockSpec((1,) + shape, lambda e, meta: (e, 0, 0))

    out_specs = [anywhere] * 2 + [one(rows, ffe), one(rows, 2 * ffe)]
    out_shapes = [jax.ShapeDtypeStruct(shape, bf16) for shape in row_shapes]
    scratch = []
    if final:
        out_specs = [anywhere] * blocks + out_specs
        out_shapes = [jax.ShapeDtypeStruct((tok, back), bf16)] * blocks + out_shapes
        scratch += [pltpu.VMEM(shape, bf16) for shape in kept_shapes]
    else:
        out_specs += [one(*shape[1:]) for shape in kept_shapes]
        out_shapes += [jax.ShapeDtypeStruct(shape, bf16) for shape in kept_shapes]
    scratch += [
        pltpu.VMEM((own, rows, width), bf16),
        pltpu.VMEM((own, rows, width), bf16),
        pltpu.VMEM((own, rows, 1), f32),
        pltpu.SemaphoreType.DMA((2,)),
        pltpu.VMEM((2, tok, padded), bf16),
        pltpu.VMEM((2, tok, padded), bf16),
        pltpu.SemaphoreType.DMA((2, 2)),
    ]
    if final:
        scratch += [
            pltpu.VMEM((blocks, tok, LANES), f32),
            pltpu.VMEM((2, tok, back), bf16),
            pltpu.SemaphoreType.DMA((blocks,)),
        ]
    if early:
        scratch += [
            pltpu.VMEM((2, array.shape[0], slots, array.shape[2]), bf16) for array in early
        ] + [pltpu.SemaphoreType.DMA((3, 2))]
    return pl.pallas_call(
        partial(
            experts_kernel,
            experts=experts,
            slots=slots,
            local=local,
            final=final,
            earlier=len(early),
        ),
        grid_spec=pltpu.PrefetchScalarGridSpec(
            num_scalar_prefetch=1,
            grid=(own,),
            in_specs=[anywhere] * (2 * blocks + len(early)) + [one(packed, LANES)] * 4,
            out_specs=out_specs,
            scratch_shapes=scratch,
        ),
        out_shape=out_shapes,
        compiler_params=call_params(60),
        cost_estimate=cost(4),
        name="experts",
    )(meta, *x_blocks, *g_blocks, *early, *parts)


def weight_grad_kernel(*refs, chunks, own_count):
    x_refs, grad_refs, active_refs, g_refs = (
        refs[chunks * index : chunks * (index + 1)] for index in range(4)
    )
    refs = refs[4 * chunks :]
    outs, (made, sent) = refs[: 4 * own_count], refs[4 * own_count :]
    x_rows = jnp.concatenate([ref[0] for ref in x_refs], axis=0)
    grads = jnp.concatenate([ref[0] for ref in grad_refs], axis=0)
    active = jnp.concatenate([ref[0] for ref in active_refs], axis=0)
    g_rows = jnp.concatenate([ref[0] for ref in g_refs], axis=0)
    cut = x_rows.shape[1] // 4
    ffe = grads.shape[1] // 2
    first = 2 * ffe // LANES * cut
    own = pl.program_id(0)
    for part in range(4):
        hidden = dot_tn(x_rows[:, part * cut : (part + 1) * cut], grads).astype(bf16)
        for t in range(2 * ffe // LANES):
            made[own, part, t * cut : (t + 1) * cut, :] = hidden[:, t * LANES : (t + 1) * LANES]
    down = (dot_tn(active, g_rows) * res_scale).astype(bf16)
    for part in range(4):
        for t in range(cut // LANES):
            at = part * cut + t * LANES
            here = slice(first + t * ffe, first + (t + 1) * ffe)
            made[own, part, here, :] = down[:, at : at + LANES]
    copies = [
        [
            pltpu.make_async_copy(
                made.at[expert, part], outs[part * own_count + expert].at[0], sent.at[expert, part]
            )
            for part in range(4)
        ]
        for expert in range(own_count)
    ]
    for expert in range(own_count):

        @pl.when(own == expert)
        def _(expert=expert):
            for copy in copies[expert]:
                copy.start()

    @pl.when(own == own_count - 1)
    def _():
        for group in copies:
            for copy in group:
                copy.wait()


def weight_grads(x_chunks, grad_chunks, active_chunks, g_chunks):
    own, rows, width = x_chunks[0].shape
    ffe = active_chunks[0].shape[2]
    chunks = len(x_chunks)
    packed = 3 * ffe * (width // 4) // LANES

    def one(*shape):
        return pl.BlockSpec((1,) + shape, lambda e: (e, 0, 0))

    outs = pl.pallas_call(
        partial(weight_grad_kernel, chunks=chunks, own_count=own),
        grid=(own,),
        in_specs=[one(rows, width)] * chunks
        + [one(rows, 2 * ffe)] * chunks
        + [one(rows, ffe)] * chunks
        + [one(rows, width)] * chunks,
        out_specs=[pl.BlockSpec(memory_space=pl.ANY)] * (4 * own),
        out_shape=[jax.ShapeDtypeStruct((1, packed, LANES), bf16)] * (4 * own),
        scratch_shapes=[
            pltpu.VMEM((own, 4, packed, LANES), bf16),
            pltpu.SemaphoreType.DMA((own, 4)),
        ],
        compiler_params=call_params(60),
        cost_estimate=cost(13),
        name="weight_grads",
    )(*x_chunks, *grad_chunks, *active_chunks, *g_chunks)
    return [list(outs[part * own : (part + 1) * own]) for part in range(4)]


def two_halves(arrays):
    return arrays if len(arrays) == 2 else list(halves(arrays[0])[1:])


def join_halves(array, own):
    return array.reshape(own, 2 * array.shape[1] // own, array.shape[2])


def pack_weights(gate, up, down):
    return jnp.concatenate(
        [
            lax.slice_in_dim(array, at, at + LANES, axis=2)
            for array in (gate, up, down)
            for at in range(0, array.shape[2], LANES)
        ],
        axis=1,
    )


def unpack_weights(packed, cut, ffe):
    tiles = ffe // LANES

    def beside(first, rows, count):
        return jnp.concatenate(
            [packed[:, first + t * rows : first + (t + 1) * rows, :] for t in range(count)], axis=2
        )

    return (
        beside(0, cut, tiles),
        beside(tiles * cut, cut, tiles),
        beside(2 * tiles * cut, ffe, cut // LANES),
    )


def after(array, *earlier):
    return lax.optimization_barrier((array, earlier))[0]


def per_device(
    tokens,
    segment_ids,
    expert_ids,
    w_query,
    key_matrix,
    value_matrix,
    w_out,
    norm_attn,
    norm_moe,
    w_router,
    w_gate,
    w_up,
    w_down,
    cotangent,
):
    row = lax.axis_index("rows")
    column = lax.axis_index("cols")
    columns = lax.axis_size("cols")
    chips = columns // 2
    chip, core = column // 2, column % 2
    own_tokens = tokens[0]
    tok, width = own_tokens.shape
    own_experts = w_gate.shape[0]
    experts = own_experts * columns
    top_count = expert_ids.shape[2]
    capacity = 5 * tok * top_count // (4 * experts)
    slots = -(-capacity // LANES) * LANES
    q_cols, k_cols = w_query.shape[1], key_matrix.shape[1]

    token_near = gather_near(own_tokens)
    qkv_cols = q_cols + 2 * k_cols
    sixth = w_out.shape[0]
    found = chips_gather(
        jnp.concatenate(
            [w_query, key_matrix, value_matrix, w_out.reshape(4 * sixth, width // 4)], axis=1
        )
    )
    small = jnp.concatenate(
        [
            w_router,
            norm_attn[:, None],
            norm_moe[:, None],
            jnp.zeros((w_router.shape[0], LANES - experts - 2), bf16),
        ],
        axis=1,
    )
    small_full = lax.all_to_all(
        jnp.tile(small, (4 * columns, 1)), ("rows", "cols"), 0, 0, tiled=True
    )
    gain_attn = small_full[:, experts].astype(f32)[None, :]
    gain_moe = small_full[:, experts + 1].astype(f32)[None, :]
    router_full = jnp.where(jnp.arange(LANES) < experts, small_full, 0)
    token_parts = gather_far(own_tokens, *token_near)
    found = after(found, token_parts[3])
    project_found = jnp.stack([rows[:, :qkv_cols] for rows in found])
    project_swapped = core_swap(project_found)

    expert_rows = expert_ids[0]
    lane_range = jnp.arange(LANES, dtype=jnp.int32)
    member = jnp.any(expert_rows[:, :, None] == lane_range[None, None, :], axis=1).astype(bf16)
    cot_rows = jnp.concatenate([cotangent[0], member], axis=1)
    cot_same = [cot_rows, chip_shift(after(cot_rows, found[1:], token_parts[3]), 1)]

    groups = 2 if own_experts % 2 == 0 else 1
    group_size = own_experts // groups
    packed = []
    for group in range(groups):
        here = slice(group * group_size, (group + 1) * group_size)
        packed.append(pack_weights(after(w_gate[here], own_tokens), w_up[here], w_down[here]))
    weight_near = [gather_near(after(packed[0], token_parts[3], project_swapped))]

    segments = segment_ids[0]
    length = segments.shape[0]
    starts = jnp.sum((segments[None, :] < segments[:, None]).astype(jnp.int32), axis=1)
    positions = (jnp.arange(length, dtype=jnp.int32) - starts).astype(f32)
    half = HEAD_SIZE // 2
    frequency = rope_base ** (-(2.0 * jnp.arange(half, dtype=f32)) / HEAD_SIZE)
    angles = positions[:, None] * frequency[None, :]
    cos_half, sin_half = jnp.cos(angles), jnp.sin(angles)
    cosine = jnp.concatenate([cos_half] * 4, axis=1)
    sine = jnp.concatenate([-sin_half, sin_half] * 2, axis=1)
    first_blocks = starts[::tok] // tok
    place = jnp.stack([row, chip, core])
    meta = jnp.concatenate([place.astype(jnp.int32), first_blocks.astype(jnp.int32)])

    queries, key_rows, value_rows, normed, project_w = project(
        meta, token_parts, project_found, project_swapped, gain_attn, cosine, sine, q_cols, k_cols
    )
    found = after(found, queries)
    out_half = jnp.stack([rows[:, qkv_cols:].reshape(sixth, width) for rows in found])
    out_half = chips_in_order(out_half, chip).reshape(chips * sixth, width)
    out_near = gather_near(out_half)
    attended, lse = attend(meta, queries, key_rows, value_rows, starts[:, None], tok)
    cot_same[1] = after(cot_same[1], attended)
    cot_same.append(chip_shift(cot_same[1], 1))
    out_near = after(out_near, weight_near[0], attended)
    attended = after(attended, weight_near[0], cot_same[1])
    own_heads = lax.all_to_all(attended, "rows", 0, 0, tiled=True)
    out_mine = jnp.stack(gather_far(out_half, *out_near)).reshape(4, chips, sixth, width)
    out_mine = after(out_mine, cot_same[2])
    out_parts = cores_in_order(out_mine, core_swap(out_mine), core, 2).reshape(4, tok, width)
    weight_near[0] = after(weight_near[0], own_heads)
    first_far = far_halves(*weight_near[0])
    mixed_rows, moe_rows, gates = mix(
        meta,
        own_heads,
        out_parts,
        own_tokens,
        member,
        gain_moe,
        router_full,
        experts,
    )
    weight_parts = [join_far(packed[0], *weight_near[0], after(first_far, moe_rows))]
    for group in range(1, groups):
        weight_near.append(gather_near(after(packed[group], weight_parts[0][3])))
    cot_other = [core_swap(after(rows, own_heads)) for rows in cot_same[:2]]
    moe_same = [
        moe_rows, chip_shift(after(moe_rows, cot_same[2], cot_other, weight_parts[0][3]), 1)
    ]
    for d in range(3, chips):
        cot_same.append(chip_shift(after(cot_same[-1], moe_same[1]), 1))
    moe_other = [core_swap(rows) for rows in moe_same]
    moe_same.append(chip_shift(moe_same[1], 1))
    cot_other += [core_swap(after(rows, moe_rows)) for rows in cot_same[2:]]

    moe_meta = jnp.stack([row, column * own_experts]).astype(jnp.int32)
    ffe = w_down.shape[1]
    kept = [[] for _ in range(groups)]
    pieces = [None] * chips
    grads = []

    def piece(d, start, stop):
        return add_low(pieces[d][0][:, start:stop], pieces[d][1][:, start:stop])

    both = 2 * width + LANES
    pairs = [(d, d + 1) for d in range(0, chips, 2)]
    early = [[] for _ in pairs]
    held = ()
    far, late, sums = [], [], []

    def make_grads(group, first_rows):
        chunks = kept[group]
        parts = weight_grads(
            [first_rows] + [k[0] for k in chunks[1:]],
            [k[3] for k in chunks],
            [k[2] for k in chunks],
            [k[1] for k in chunks],
        )
        grads.append([two_halves(part) for part in parts])

    for index, pair in enumerate(pairs):
        for group in range(groups):
            final = group == groups - 1
            if final and index == len(pairs) - 1 and groups > 1:
                make_grads(0, kept[0][0][0])
                far.append(reduce_first(grads[0]))
                held = grads[0]
            result = list(
                run_experts(
                    after(moe_meta, held),
                    [rows for d in pair for rows in (moe_same[d], moe_other[d])],
                    [rows for d in pair for rows in (cot_same[d], cot_other[d])],
                    early[index],
                    weight_parts[group],
                    ffe,
                    experts,
                    slots,
                    group * group_size,
                    final,
                )
            )
            held = result[0]
            if len(moe_other) == 2:
                moe_same[2] = after(moe_same[2], held)
                held = (held, moe_same[2])
                for d in range(3, chips):
                    moe_same.append(chip_shift(moe_same[-1], 1))
                moe_other += [core_swap(rows) for rows in moe_same[2:]]
                for later in range(1, groups):
                    weight_near[later] = after(weight_near[later], held)
                    weight_parts.append(gather_far(packed[later], *weight_near[later]))
            if not final:
                kept[group].append(result[:4])
                early[index] = result[4:]
                continue
            if index == 0:
                result = after(result, moe_same[3], cot_same[3])
            if index == len(pairs) - 1:
                result = after(result, dx_hop, far if groups > 1 else ())
            kept[group].append(result[4:8])
            for place, d in enumerate(pair):
                pieces[d] = (result[2 * place], core_swap(result[2 * place + 1]))
            if index == 0:
                dx_ring = piece(1, width, both)
                held = dx_ring
                dx_hop = chip_shift(dx_ring, 1)
                continue
            for d in pair:
                came = dx_hop if d == 2 else chip_shift(dx_ring, 1)
                if d == chips - 1:
                    came = after(came, grads[-1])
                    far.append(reduce_first(after(grads[-1], came)))
                dx_ring = add_low(came, last_pieces[0] if d == chips - 1 else piece(d, width, both))
                if d != chips - 2:
                    continue
                last_pieces = [piece(chips - 1, width, both), piece(0, width, both)]
                if groups > 1:
                    sums.append(reduce_second(grads[0], after(far[0], dx_ring)))
                    late.append([rows_swap(*sent) for sent in zip(sums[0], (1, 2))])
                make_grads(group, after(kept[group][0][0], dx_ring, sums, last_pieces))
    for d in range(chips):
        pieces[d] = after(pieces[d], dx_ring)
    outs = [piece(d, 0, width) for d in range(chips - 1)]
    outs.append(piece(chips - 1, 0, width))
    dx_came = after(chip_shift(dx_ring, 1), outs)
    out_hop = chip_shift(after(outs[1], dx_came), 1)

    grad_mixed, grad_heads, wide_mine, wide_other = unmix(
        after(meta, late[:1]),
        dx_came,
        last_pieces[1],
        mixed_rows,
        cotangent[0],
        gates,
        gain_moe,
        router_full,
        out_parts,
        own_heads,
        experts,
        chips,
    )
    grad_attended = lax.all_to_all(grad_heads, "rows", 0, 0, tiled=True)

    wide_chip = add_low(wide_mine, core_swap(after(wide_other, far[-1])))
    wide_came = lax.all_to_all(wide_chip, "rows", 0, 0, tiled=True)

    grad_lin = attend_back(
        after(meta, wide_chip),
        queries,
        grad_attended,
        lse.T,
        starts[None, :],
        key_rows,
        value_rows,
        cosine,
        sine,
        tok,
    )
    grad_lin = after(grad_lin, late[:1], wide_came)
    normed_parts = [None] * 4
    for j in (3, 1, 2, 0):
        normed_parts[j] = dot_nt(grad_lin[j], project_w).astype(bf16)
    normed_sums = reduce_add(normed_parts, *reduce_far(normed_parts))
    normed_near = reduce_near(*normed_sums)
    sums.append(reduce_second(grads[-1], after(far[-1], *normed_sums)))
    late.append([rows_swap(*sent) for sent in zip(sums[-1], (1, 2))])
    grad_project = dot_tn(
        after(normed, *normed_parts).reshape(length, width), grad_lin.reshape(length, qkv_cols)
    )
    project_pairs = after(grad_project.astype(bf16), *normed_sums)
    project_pairs = project_pairs.reshape(chips, 2, width // columns, qkv_cols)
    project_chip = cores_sum(project_pairs.transpose(1, 0, 2, 3))
    project_came = chips_exchange(project_chip)
    project_sum = jnp.sum(after(project_came, late[-1]).astype(f32), axis=0)
    grad_normed = add_wide([normed_parts[0], *after(normed_near, project_sum)])
    wide_row = add_low_all(after(wide_came, project_came))
    wide_sum = jnp.sum(chips_exchange(wide_row).astype(f32), axis=0)
    grad_out_w = wide_sum[:, :width]
    grad_router_w = wide_sum[:, width : width + experts]
    grad_gain_moe_w = wide_sum[:, width + experts]

    out_ring = add_low(after(out_hop, grad_lin), outs[2])
    for d in range(3, chips):
        out_ring = add_low(after(chip_shift(out_ring, 1), *normed_sums), outs[d])
    moe_out = add_wide([chip_shift(after(out_ring, project_came), 1), outs[0]])
    block_out = mixed_rows + res_scale * moe_out

    totals = []
    for parts, came in zip(grads, late):
        total = reduce_total([after(parts[0], *normed_sums, project_chip)], came)
        totals.append(unpack_weights(join_halves(total, group_size), width // 4, ffe))
    grad_gate_w, grad_up_w, grad_down_w = (
        jnp.concatenate(arrays, axis=0) for arrays in zip(*totals)
    )

    own_w = jnp.concatenate([w_query, key_matrix, value_matrix], axis=1).astype(f32)
    own_gain = lax.dynamic_slice_in_dim(gain_attn[0], column * own_w.shape[0], own_w.shape[0], 0)
    gain_rows = (jnp.sum(project_sum * own_w, axis=1) / own_gain).reshape(4, -1)
    gain_rows = after(gain_rows, wide_sum)
    gain_sum = jnp.sum(lax.all_to_all(gain_rows, "rows", 0, 0, tiled=True), axis=0)
    grad_gain_attn = lax.ppermute(
        gain_sum,
        ("rows", "cols"),
        [(r * columns + c, 4 * c + r) for r in range(4) for c in range(columns)],
    )

    own_float = own_tokens.astype(f32)
    scale_attn = rms_scale(own_float)
    unit_attn = own_float * scale_attn
    grad_unit = grad_normed * gain_attn
    grad_tokens = grad_mixed + scale_attn * (
        grad_unit - unit_attn * jnp.mean(grad_unit * unit_attn, axis=-1, keepdims=True)
    )
    return (
        block_out[None],
        grad_tokens[None],
        project_sum[:, :q_cols],
        project_sum[:, q_cols : q_cols + k_cols],
        project_sum[:, q_cols + k_cols :],
        grad_out_w,
        grad_gain_attn,
        grad_gain_moe_w,
        grad_router_w,
        grad_gate_w,
        grad_up_w,
        grad_down_w,
    )


def solution(mesh):
    placed = (
        P("cols", "rows", None),
        P("cols", None),
        P("cols", "rows", None),
        P("cols", "rows"),
        P("cols", "rows"),
        P("cols", "rows"),
        P(("rows", "cols"), None),
        P(("rows", "cols")),
        P(("rows", "cols")),
        P(("rows", "cols"), None),
        P("cols", "rows", None),
        P("cols", "rows", None),
        P("cols", None, "rows"),
        P("cols", "rows", None),
    )
    return jax.shard_map(
        per_device,
        mesh=mesh,
        in_specs=placed,
        out_specs=(
            P("cols", "rows", None),
            P("cols", "rows", None),
            P("cols", "rows"),
            P("cols", "rows"),
            P("cols", "rows"),
            P(("rows", "cols"), None),
            P(("rows", "cols")),
            P(("rows", "cols")),
            P(("rows", "cols"), None),
            P("cols", "rows", None),
            P("cols", "rows", None),
            P("cols", None, "rows"),
        ),
        check_vma=False,
    )
```
